32 devices in a mesh: dp: 8 (over y, x, core), seq: 4 (over z).
Axes of the slice: x: 2, y: 2, z: 4, core: 2. Of those that a mesh axis runs over, the one named last changes fastest.
Arguments:
- tokens: bfloat16 [16, 512, 1024], P('dp', 'seq'), may hold values from -32 to 32
- group_count: int32 [8], P('dp'), may hold values from 1 to 2, as said below
- pad_mask: int32 [16, 512], P('dp'), may hold values from 0 to 1, as said below
- w_qkv: bfloat16 [1024, 3072], P('dp'), may hold values from -0.1875 to 0.1875
- w_proj: bfloat16 [1024, 1024], P('dp'), may hold values from -1.5 to 1.5
- w_fc1: bfloat16 [1024, 4096], P('dp'), may hold values from -0.1875 to 0.1875
- w_fc2: bfloat16 [4096, 1024], P('dp'), may hold values from -0.09375 to 0.09375
- fc1_bias: bfloat16 [4096], P('dp'), may hold values from -3 to 3
- scales: bfloat16 [4, 1024], P(None, 'dp'), may hold values from 0.099609375 to 1.8984375
- shifts: bfloat16 [6, 1024], P(None, 'dp'), may hold values from -3 to 3
- cotangent: bfloat16 [16, 512, 1024], P('dp', 'seq'), may hold values from -6 to 6
Outputs:
- output: bfloat16 [16, 512, 1024], P('dp', 'seq')
- grad_tokens: bfloat16 [16, 512, 1024], P('dp', 'seq')
- grad_qkv: float32 [1024, 3072], P('dp')
- grad_proj: float32 [1024, 1024], P('dp')
- grad_fc1: float32 [1024, 4096], P('dp')
- grad_fc2: float32 [4096, 1024], P('dp')
- grad_fc1_bias: float32 [4096], P('dp')
- grad_scales: float32 [4, 1024], P(None, 'dp')
- grad_shifts: float32 [6, 1024], P(None, 'dp')
The draws below stay inside these ranges and needn't reach their ends.
Inputs may be any that keep to these rules, and one draw needn't show every extreme that they name: `group_count`: every group holds 1 or 2 images; in every draw some group holds 2 and some group holds 1. `pad_mask`: each slot's mask is 1 on its first tokens and 0 on its last tokens, with at most 32 zeros.
All inputs are finite; a program needn't handle non-finite values.
Results may differ from the reference program's by a relative error of at most 0.035.
Values may be sent and summed in bfloat16 or wider, within the bound.
No kernel may reach another device: no remote copies, remote signals or barrier semaphores. Data moves between devices by JAX's collectives and lax.ppermute only.
A program may use at most 192 MiB of HBM per device.

```python
import math
import jax
import jax.numpy as jnp
from jax import lax

D = 1024
HD = 64
FF = 4096
SEQ_LEN = 512
SLOTS = 2
GROUPS = 8
IMAGES_CAP = 16


def draw_tokens(key, part):
    key = jax.random.fold_in(key, 11)
    key_base, key_rows, key_cols = jax.random.split(key, 3)
    base = jax.random.normal(key_base, (IMAGES_CAP, SEQ_LEN, D), jnp.float32)
    rows = jnp.exp(jax.random.uniform(key_rows, (IMAGES_CAP, SEQ_LEN, 1), jnp.float32, math.log(0.3), math.log(3.0)))
    cols = jnp.exp(jax.random.uniform(key_cols, (1, 1, D), jnp.float32, math.log(0.7), math.log(1.4)))
    return (base * rows * cols).astype(jnp.bfloat16)


def draw_group_count(key, part):
    key = jax.random.fold_in(key, 12)
    key_counts, key_full, key_single = jax.random.split(key, 3)
    counts = jax.random.randint(key_counts, (GROUPS,), 1, 3, dtype=jnp.int32)
    full_at = jax.random.randint(key_full, (), 0, GROUPS, dtype=jnp.int32)
    single_at = (full_at + jax.random.randint(key_single, (), 1, GROUPS, dtype=jnp.int32)) % GROUPS
    counts = counts.at[full_at].set(2).at[single_at].set(1)
    return counts.astype(jnp.int32)


def draw_pad_mask(key, part):
    key = jax.random.fold_in(key, 13)
    padding = jax.random.randint(key, (IMAGES_CAP, 1), 0, SEQ_LEN // 16 + 1, dtype=jnp.int32)
    position = jnp.arange(SEQ_LEN, dtype=jnp.int32)[None, :]
    return (position < SEQ_LEN - padding).astype(jnp.int32)


def steps_of(stream_key, extent, cuts, low, top_value):
    def one(dim, parts):
        heights = jax.random.uniform(jax.random.fold_in(jax.random.fold_in(stream_key, 6), dim), (parts,), jnp.float32, low / len(cuts), top_value / len(cuts))
        return jnp.repeat(jnp.exp(heights), extent[dim] // parts).reshape((-1,) + (1,) * (len(extent) - dim - 1))

    loudness = one(*cuts[0])
    for cut in cuts[1:]:
        loudness = loudness * one(*cut)
    return loudness


def noise(key, extent, deviation, limit, shards=(), held_as=jnp.bfloat16):
    drawn = jax.random.normal(key, extent, jnp.float32) * deviation
    if len(shards) > 0:
        drawn = steps_of(key, extent, shards, -0.22, 0.18) * drawn
    return jnp.clip(drawn, min=-limit, max=limit).astype(held_as)


def setup_inputs(seed: int = 0) -> dict:
    seeds = jax.random.split(jax.random.key(seed), 12)
    tokens = draw_tokens(jax.random.fold_in(seeds[11], 71), 0)
    group_count = draw_group_count(jax.random.fold_in(seeds[11], 71), 0)
    pad_mask = draw_pad_mask(jax.random.fold_in(seeds[11], 71), 0)
    w_qkv = noise(seeds[3], (D, 3 * D), D ** -0.5, 0.1875, ((0, 8),))
    w_proj = noise(seeds[4], (D, D), (D * 8 // SEQ_LEN) ** -0.5, 1.5, ((0, 8),))
    w_fc1 = noise(seeds[5], (D, FF), D ** -0.5, 0.1875, ((0, 8),))
    w_fc2 = noise(seeds[6], (FF, D), FF ** -0.5, 0.09375, ((0, 8),))
    fc1_bias = noise(seeds[7], (FF,), 0.5, 3.0, ((0, 8),))
    scales = jnp.clip(1.0 + 0.18 * jax.random.normal(seeds[8], (4, D), jnp.float32), 0.099609375, 1.8984375).astype(jnp.bfloat16)
    shifts = noise(seeds[9], (6, D), 0.5, 3.0, ((1, 8),))
    cotangent = noise(seeds[10], (IMAGES_CAP, SEQ_LEN, D), 1.0, 6.0, ((0, 8), (1, 4)))
    return {"tokens": tokens, "group_count": group_count, "pad_mask": pad_mask, "w_qkv": w_qkv, "w_proj": w_proj, "w_fc1": w_fc1, "w_fc2": w_fc2, "fc1_bias": fc1_bias, "scales": scales, "shifts": shifts, "cotangent": cotangent}


EPSILON = 1e-06
ROOT_HALF = 0.7071067811865476
HIGHEST = lax.Precision.HIGHEST

@jax.custom_vjp
def low(v):
    return lax.optimization_barrier(v.astype(jnp.bfloat16)).astype(jnp.float32)

@jax.custom_vjp
def low_back(v):
    return v

def low_keep(v):
    return (low(v), None)

def low_pass(kept, grad):
    return (grad,)

def back_keep(v):
    return (v, None)

def back_low(kept, grad):
    return (low(grad),)
low.defvjp(low_keep, low_pass)
low_back.defvjp(back_keep, back_low)

def both_ways(values):
    return low(low_back(values))

def layer_norm(values, gain, shift):
    mean_row = lax.optimization_barrier(jnp.mean(values, axis=-1, keepdims=True))
    centred = values - mean_row
    inverse = lax.rsqrt(lax.optimization_barrier(jnp.mean(centred * centred, axis=-1, keepdims=True)) + EPSILON)
    return centred * inverse * gain + shift

def gelu_exact(values):
    return 0.5 * values * (1.0 + lax.erf(values * ROOT_HALF))

def matmul_hi(left, right):
    return jnp.dot(left, right, precision=HIGHEST)

def layer_forward(params, inputs, mask):
    w_qkv, w_proj, w_fc1, w_fc2, fc1_bias, scales, shifts = params
    count, length, width = inputs.shape
    head_count = width // HD
    normed_one = low(layer_norm(inputs, scales[0], shifts[0]))
    projected = matmul_hi(normed_one, w_qkv)
    queries = both_ways(projected[:, :, :width] + shifts[1]).reshape(count, length, head_count, HD)
    key_rows = both_ways(projected[:, :, width:2 * width]).reshape(count, length, head_count, HD)
    value_rows = both_ways(projected[:, :, 2 * width:] + shifts[2]).reshape(count, length, head_count, HD)
    scores = jnp.einsum('bqhe,bkhe->bhqk', queries, key_rows, precision=HIGHEST) * HD ** (-0.5)
    scores = low_back(jnp.where(mask[:, None, None, :] > 0, scores, -1e+30))
    top = lax.optimization_barrier(jnp.max(scores, axis=-1, keepdims=True))
    expo = jnp.exp(scores - top)
    probs = low(expo / lax.optimization_barrier(jnp.sum(expo, axis=-1, keepdims=True)))
    attended = jnp.einsum('bhqk,bkhe->bqhe', probs, value_rows, precision=HIGHEST)
    attended = both_ways(attended.reshape(count, length, width))
    branch_one = low_back(matmul_hi(attended, w_proj) + shifts[3])
    gate = mask[:, :, None]
    hidden_state = inputs + branch_one * scales[1] * gate
    normed_two = low(layer_norm(hidden_state, scales[2], shifts[4]))
    pre_act = low_back(matmul_hi(normed_two, w_fc1) + fc1_bias)
    activated = low(gelu_exact(pre_act))
    branch_two = low_back(matmul_hi(activated, w_fc2) + shifts[5])
    return hidden_state + branch_two * scales[3] * gate

def reference(tokens, group_count, pad_mask, w_qkv, w_proj, w_fc1, w_fc2, fc1_bias, scales, shifts, cotangent):
    alive = (jnp.arange(SLOTS, dtype=jnp.int32)[None, :] < group_count[:, None]).reshape(-1)
    mask = jnp.where(alive[:, None], pad_mask, 0).astype(jnp.float32)
    params = tuple((item.astype(jnp.float32) for item in (w_qkv, w_proj, w_fc1, w_fc2, fc1_bias, scales, shifts)))
    per_step = math.gcd(IMAGES_CAP, max(1, 4096 // SEQ_LEN))
    steps_count = IMAGES_CAP // per_step
    inputs = tokens.astype(jnp.float32).reshape(steps_count, per_step, SEQ_LEN, D)
    masks = mask.reshape(steps_count, per_step, SEQ_LEN)
    grads_in = cotangent.astype(jnp.float32).reshape(steps_count, per_step, SEQ_LEN, D)

    def one_step(total, block):
        block_in, block_mask, block_grad = block
        result, pull = jax.vjp(lambda weights, values: layer_forward(weights, values, block_mask), params, block_in)
        grad_params, grad_in = pull(block_grad)
        total = jax.tree.map(lambda left, right: left + right, total, grad_params)
        return (total, (result.astype(jnp.bfloat16), grad_in.astype(jnp.bfloat16)))
    zero_grads = jax.tree.map(jnp.zeros_like, params)
    totals, (results, grad_inputs) = lax.scan(one_step, zero_grads, (inputs, masks, grads_in))
    output = results.reshape(IMAGES_CAP, SEQ_LEN, D)
    grad_tokens = grad_inputs.reshape(IMAGES_CAP, SEQ_LEN, D)
    return (output, grad_tokens, totals[0], totals[1], totals[2], totals[3], totals[4], totals[5], totals[6])
```

```python
import jax
import jax.numpy as jnp
from jax import lax
from jax.sharding import PartitionSpec as P

HD = 64


EPSILON = 1e-06
ROOT_HALF = 0.7071067811865476
INV_ROOT_TWO_PI = 0.3989422804014327


def layer_norm(values, gain, shift):
    mean_row = jnp.mean(values, axis=-1, keepdims=True)
    centred = values - mean_row
    inverse = lax.rsqrt(jnp.mean(centred * centred, axis=-1, keepdims=True) + EPSILON)
    unit_rows = centred * inverse
    return (unit_rows * gain + shift, unit_rows, inverse)


def norm_back(grad_normed, unit_rows, inverse, gain):
    scaled = grad_normed * gain
    centre = jnp.mean(scaled, axis=-1, keepdims=True)
    along = jnp.mean(scaled * unit_rows, axis=-1, keepdims=True)
    return inverse * (scaled - centre - unit_rows * along)


def gelu_exact(values):
    return 0.5 * values * (1.0 + lax.erf(values * ROOT_HALF))


def gelu_slope(values):
    return (
        0.5 * (1.0 + lax.erf(values * ROOT_HALF))
        + values * jnp.exp(-0.5 * values * values) * INV_ROOT_TWO_PI
    )


def token_sum(values):
    return jnp.sum(values, axis=(0, 1))


def general_plan(
    tokens, group_count, pad_mask, w_qkv, w_proj, w_fc1, w_fc2, fc1_bias, scales, shifts, cotangent
):
    slot_count, piece, width = tokens.shape
    seq_total = pad_mask.shape[1]
    part_width = width // lax.axis_size("seq")
    head_count = part_width // HD
    factor = HD ** (-0.5)
    alive = jnp.arange(slot_count, dtype=jnp.int32) < group_count[0]
    key_mask = jnp.where(alive[:, None], pad_mask, 0).astype(jnp.float32)
    query_mask = lax.dynamic_slice_in_dim(key_mask, lax.axis_index("seq") * piece, piece, 1)[
        :, :, None
    ]
    full_qkv, full_proj, full_fc1, full_fc2, full_bias, full_scales, full_shifts = (
        lax.all_gather(w_qkv, "dp", axis=0, tiled=True),
        lax.all_gather(w_proj, "dp", axis=0, tiled=True),
        lax.all_gather(w_fc1, "dp", axis=0, tiled=True),
        lax.all_gather(w_fc2, "dp", axis=0, tiled=True),
        lax.all_gather(fc1_bias, "dp", axis=0, tiled=True),
        lax.all_gather(scales, "dp", axis=1, tiled=True),
        lax.all_gather(shifts, "dp", axis=1, tiled=True),
    )
    gains = full_scales.astype(jnp.float32)
    offsets = full_shifts.astype(jnp.float32)
    hidden_bias = full_bias.astype(jnp.float32)
    inputs = tokens.astype(jnp.float32)
    normed_one, unit_one, inverse_one = layer_norm(inputs, gains[0], offsets[0])
    normed_one = normed_one.astype(jnp.bfloat16)
    projected = jnp.dot(normed_one, full_qkv, preferred_element_type=jnp.float32)
    queries = (projected[:, :, :width] + offsets[1]).astype(jnp.bfloat16)
    key_rows = projected[:, :, width : 2 * width].astype(jnp.bfloat16)
    value_rows = (projected[:, :, 2 * width :] + offsets[2]).astype(jnp.bfloat16)
    head_query, head_key, head_value = (
        lax.all_to_all(queries, "seq", split_axis=2, concat_axis=1, tiled=True),
        lax.all_to_all(key_rows, "seq", split_axis=2, concat_axis=1, tiled=True),
        lax.all_to_all(value_rows, "seq", split_axis=2, concat_axis=1, tiled=True),
    )
    head_shape = (slot_count, seq_total, head_count, HD)
    query_heads = head_query.reshape(head_shape)
    key_heads = head_key.reshape(head_shape)
    value_heads = head_value.reshape(head_shape)

    def scores_of():
        raw = (
            jnp.einsum(
                "bqhe,bkhe->bhqk", query_heads, key_heads, preferred_element_type=jnp.float32
            )
            * factor
        )
        return jnp.where(key_mask[:, None, None, :] > 0, raw, -1e30)

    scores = scores_of()
    top = jnp.max(scores, axis=-1, keepdims=True)
    log_total = top + jnp.log(jnp.sum(jnp.exp(scores - top), axis=-1, keepdims=True))
    probs_low = jnp.exp(scores - log_total).astype(jnp.bfloat16)
    attended = jnp.einsum(
        "bhqk,bkhe->bqhe", probs_low, value_heads, preferred_element_type=jnp.float32
    )
    attended = attended.astype(jnp.bfloat16).reshape(slot_count, seq_total, part_width)
    mixed = lax.all_to_all(attended, "seq", split_axis=1, concat_axis=2, tiled=True)
    branch_one = jnp.dot(mixed, full_proj, preferred_element_type=jnp.float32) + offsets[3]
    hidden_state = inputs + branch_one * gains[1] * query_mask
    normed_two, unit_two, inverse_two = layer_norm(hidden_state, gains[2], offsets[4])
    normed_two = normed_two.astype(jnp.bfloat16)
    pre_act = jnp.dot(normed_two, full_fc1, preferred_element_type=jnp.float32) + hidden_bias
    activated = gelu_exact(pre_act).astype(jnp.bfloat16)
    branch_two = jnp.dot(activated, full_fc2, preferred_element_type=jnp.float32) + offsets[5]
    output = (hidden_state + branch_two * gains[3] * query_mask).astype(jnp.bfloat16)
    back_qkv, back_proj, back_fc1, back_fc2, back_gains = (
        full_qkv,
        full_proj,
        full_fc1,
        full_fc2,
        gains,
    )
    grad_out = cotangent.astype(jnp.float32)
    layer_gain_two = token_sum(grad_out * query_mask * branch_two)
    grad_branch_two = (grad_out * back_gains[3] * query_mask).astype(jnp.bfloat16)
    shift_five = token_sum(grad_branch_two.astype(jnp.float32))
    grad_fc2 = jnp.einsum(
        "spf,spd->fd", activated, grad_branch_two, preferred_element_type=jnp.float32
    )
    grad_act = jnp.einsum(
        "spd,fd->spf", grad_branch_two, back_fc2, preferred_element_type=jnp.float32
    )
    grad_pre = (grad_act * gelu_slope(pre_act)).astype(jnp.bfloat16)
    grad_hidden_bias = token_sum(grad_pre.astype(jnp.float32))
    grad_fc1 = jnp.einsum("spd,spf->df", normed_two, grad_pre, preferred_element_type=jnp.float32)
    grad_normed_two = jnp.einsum(
        "spf,df->spd", grad_pre, back_fc1, preferred_element_type=jnp.float32
    )
    norm_gain_two = token_sum(grad_normed_two * unit_two)
    norm_shift_two = token_sum(grad_normed_two)
    grad_hidden = grad_out + norm_back(grad_normed_two, unit_two, inverse_two, back_gains[2])
    layer_gain_one = token_sum(grad_hidden * query_mask * branch_one)
    grad_branch_one = (grad_hidden * back_gains[1] * query_mask).astype(jnp.bfloat16)
    shift_proj = token_sum(grad_branch_one.astype(jnp.float32))
    grad_proj = jnp.einsum(
        "spd,spe->de", mixed, grad_branch_one, preferred_element_type=jnp.float32
    )
    grad_mixed = jnp.einsum(
        "spe,de->spd", grad_branch_one, back_proj, preferred_element_type=jnp.float32
    )
    grad_mixed = grad_mixed.astype(jnp.bfloat16)
    grad_attended = lax.all_to_all(
        grad_mixed, "seq", split_axis=2, concat_axis=1, tiled=True
    ).reshape(head_shape)
    probs = jnp.exp(scores_of() - log_total)
    probs_again = probs.astype(jnp.bfloat16)
    grad_probs = jnp.einsum(
        "bqhe,bkhe->bhqk", grad_attended, value_heads, preferred_element_type=jnp.float32
    )
    row_dot = jnp.sum(grad_probs * probs, axis=-1, keepdims=True)
    grad_scores = (probs * (grad_probs - row_dot)).astype(jnp.bfloat16)
    flat_shape = (slot_count, seq_total, part_width)
    grad_query = (
        jnp.einsum("bhqk,bkhe->bqhe", grad_scores, key_heads, preferred_element_type=jnp.float32)
        * factor
    )
    grad_key = (
        jnp.einsum("bhqk,bqhe->bkhe", grad_scores, query_heads, preferred_element_type=jnp.float32)
        * factor
    )
    grad_value = jnp.einsum(
        "bhqk,bqhe->bkhe", probs_again, grad_attended, preferred_element_type=jnp.float32
    )
    grad_query = grad_query.astype(jnp.bfloat16).reshape(flat_shape)
    grad_key = grad_key.astype(jnp.bfloat16).reshape(flat_shape)
    grad_value = grad_value.astype(jnp.bfloat16).reshape(flat_shape)
    token_query, token_key, token_value = (
        lax.all_to_all(grad_query, "seq", split_axis=1, concat_axis=2, tiled=True),
        lax.all_to_all(grad_key, "seq", split_axis=1, concat_axis=2, tiled=True),
        lax.all_to_all(grad_value, "seq", split_axis=1, concat_axis=2, tiled=True),
    )
    grad_joined = jnp.concatenate([token_query, token_key, token_value], axis=2)
    grad_qkv = jnp.einsum(
        "spd,spe->de", normed_one, grad_joined, preferred_element_type=jnp.float32
    )
    grad_normed_one = jnp.einsum(
        "spe,de->spd", grad_joined, back_qkv, preferred_element_type=jnp.float32
    )
    norm_gain_one = token_sum(grad_normed_one * unit_one)
    norm_shift_one = token_sum(grad_normed_one)
    grad_input = (
        grad_hidden + norm_back(grad_normed_one, unit_one, inverse_one, back_gains[0])
    ).astype(jnp.bfloat16)
    gain_terms = jnp.stack([norm_gain_one, layer_gain_one, norm_gain_two, layer_gain_two])
    shift_terms = jnp.stack(
        [
            norm_shift_one,
            token_sum(token_query.astype(jnp.float32)),
            token_sum(token_value.astype(jnp.float32)),
            shift_proj,
            norm_shift_two,
            shift_five,
        ]
    )
    shares = (
        lax.psum_scatter(
            grad_qkv.astype(jnp.bfloat16), "dp", scatter_dimension=0, tiled=True
        ).astype(jnp.float32),
        lax.psum_scatter(
            grad_proj.astype(jnp.bfloat16), "dp", scatter_dimension=0, tiled=True
        ).astype(jnp.float32),
        lax.psum_scatter(
            grad_fc1.astype(jnp.bfloat16), "dp", scatter_dimension=0, tiled=True
        ).astype(jnp.float32),
        lax.psum_scatter(
            grad_fc2.astype(jnp.bfloat16), "dp", scatter_dimension=0, tiled=True
        ).astype(jnp.float32),
        lax.psum_scatter(
            grad_hidden_bias.astype(jnp.bfloat16), "dp", scatter_dimension=0, tiled=True
        ).astype(jnp.float32),
        lax.psum_scatter(
            gain_terms.astype(jnp.bfloat16), "dp", scatter_dimension=1, tiled=True
        ).astype(jnp.float32),
        lax.psum_scatter(
            shift_terms.astype(jnp.bfloat16), "dp", scatter_dimension=1, tiled=True
        ).astype(jnp.float32),
    )
    totals = (
        lax.psum(shares[0].astype(jnp.bfloat16), "seq").astype(jnp.float32),
        lax.psum(shares[1].astype(jnp.bfloat16), "seq").astype(jnp.float32),
        lax.psum(shares[2].astype(jnp.bfloat16), "seq").astype(jnp.float32),
        lax.psum(shares[3].astype(jnp.bfloat16), "seq").astype(jnp.float32),
        lax.psum(shares[4].astype(jnp.bfloat16), "seq").astype(jnp.float32),
        lax.psum(shares[5].astype(jnp.bfloat16), "seq").astype(jnp.float32),
        lax.psum(shares[6].astype(jnp.bfloat16), "seq").astype(jnp.float32),
    )
    return (
        output,
        grad_input,
        totals[0],
        totals[1],
        totals[2],
        totals[3],
        totals[4],
        totals[5],
        totals[6],
    )


CORE, ALONG_X, ALONG_Y = 1, 2, 4


def swap(values, bit):
    size = lax.axis_size("dp")
    return lax.ppermute(values, "dp", [(i, i ^ bit) for i in range(size)])


def after(values, earlier):
    return lax.optimization_barrier((values, earlier))[0]


def place():
    index = lax.axis_index("dp")
    return index % 2, (index // 2) % 2, index // 4


def ordered(mine, theirs, bit, axis):
    low = jnp.where(bit == 0, mine, theirs)
    high = jnp.where(bit == 0, theirs, mine)
    return jnp.stack([low, high], axis=axis)


def joined(mine, theirs, bit, axis):
    low = jnp.where(bit == 0, mine, theirs)
    high = jnp.where(bit == 0, theirs, mine)
    return jnp.concatenate([low, high], axis=axis)


class Wire:
    def __init__(self, bit):
        self.bit = bit
        self.done = []

    def __call__(self, values):
        if len(self.done) >= 2:
            values = after(values, self.done[-2])
        result = swap(values, self.bit)
        self.done.append(result)
        return result


def gather_pair(block_a, block_b, wire_x, wire_y):
    _, at_x, at_y = place()
    far_a, far_b = wire_x(block_a), wire_y(block_b)
    pair_a = ordered(block_a, far_a, at_x, 0)
    pair_b = ordered(block_b, far_b, at_y, 0)
    far_a, far_b = wire_y(pair_a), wire_x(pair_b)
    quad_a = ordered(pair_a, far_a, at_y, 0)
    quad_b = ordered(pair_b, far_b, at_x, 1)
    return (
        quad_a.reshape((4,) + block_a.shape),
        quad_b.reshape((4,) + block_b.shape),
    )


def columns(values, start, count):
    return lax.dynamic_slice_in_dim(values, start, count, 1)


def product_of(left, right):
    return jnp.einsum("td,te->de", left, right, preferred_element_type=jnp.float32)


def reduce_part(left, right, first_x):
    _, at_x, at_y = place()
    rows = left.shape[1] // 4
    if first_x:
        near = jnp.concatenate(
            [columns(left, at_x * rows, rows), columns(left, (2 + at_x) * rows, rows)], axis=1
        )
        far = jnp.concatenate(
            [columns(left, (1 - at_x) * rows, rows), columns(left, (3 - at_x) * rows, rows)], axis=1
        )
        first, second, at_second = ALONG_X, ALONG_Y, at_y
    else:
        near = columns(left, at_y * 2 * rows, 2 * rows)
        far = columns(left, (1 - at_y) * 2 * rows, 2 * rows)
        first, second, at_second = ALONG_Y, ALONG_X, at_x
    got = swap(product_of(far, right).astype(jnp.bfloat16), first)
    partial = product_of(near, right) + got.astype(jnp.float32)
    partial = partial.astype(jnp.bfloat16).reshape(2, rows, right.shape[1])
    keep = lax.dynamic_index_in_dim(partial, at_second, 0, False)
    give = lax.dynamic_index_in_dim(partial, 1 - at_second, 0, False)
    got = swap(give, second)
    return (keep.astype(jnp.float32) + got.astype(jnp.float32)).astype(jnp.bfloat16)


def sum_along_line(values):
    at_z = lax.axis_index("seq")
    wide = values.dtype
    got = lax.ppermute(values, "seq", [(0, 1), (3, 2)])
    half = (values.astype(jnp.float32) + got.astype(jnp.float32)).astype(wide)
    got = lax.ppermute(half, "seq", [(1, 2), (2, 1)])
    total = (half.astype(jnp.float32) + got.astype(jnp.float32)).astype(wide)
    got = lax.ppermute(total, "seq", [(1, 0), (2, 3)])
    return jnp.where((at_z == 1) | (at_z == 2), total, got)


def image_moves(back):
    seq = lax.axis_size("seq")
    rounds = []
    for turn in range(2):
        moves = []
        for chip in range(lax.axis_size("dp") // 2):
            for core in range(2):
                for quarter in range(seq):
                    slot = (quarter + turn) % 2
                    source = (2 * chip + core) * seq + quarter
                    target = (2 * chip + quarter // 2) * seq + 2 * core + slot
                    moves.append((target, source) if back else (source, target))
        rounds.append(moves)
    return rounds


def to_images(values):
    at_z = lax.axis_index("seq")
    got = []
    for turn, moves in enumerate(image_moves(False)):
        sent = lax.dynamic_index_in_dim(values, (at_z + turn) % 2, 0, False)
        got.append(lax.ppermute(sent, ("dp", "seq"), moves))
    return joined(got[0], got[1], at_z % 2, 0)


def from_images(values):
    at_z = lax.axis_index("seq")
    pieces = values.reshape(2, values.shape[0] // 2, values.shape[1])
    got = []
    for turn, moves in enumerate(image_moves(True)):
        sent = lax.dynamic_index_in_dim(pieces, (at_z + turn) % 2, 0, False)
        got.append(lax.ppermute(sent, ("dp", "seq"), moves))
    return ordered(got[0], got[1], at_z % 2, 0)


def image_plan(
    tokens, group_count, pad_mask, w_qkv, w_proj, w_fc1, w_fc2, fc1_bias, scales, shifts, cotangent
):
    slot_count, _, width = tokens.shape
    length = pad_mask.shape[1]
    half_length = length // 2
    factor = HD ** (-0.5)
    f32, bf16 = jnp.float32, jnp.bfloat16
    core, at_x, at_y = place()
    at_z = lax.axis_index("seq")

    def own_half(values):
        return lax.dynamic_slice_in_dim(values, core * half_length, half_length, 0)

    small = jnp.concatenate([scales, shifts, fc1_bias.reshape(4, 128)], axis=0)
    alive = jnp.arange(slot_count, dtype=jnp.int32) < group_count[0]
    mask_own = jnp.where(alive[:, None], pad_mask, 0).astype(bf16)
    small_pair = ordered(small, swap(small, CORE), core, 0)
    mask_both = ordered(mask_own, swap(mask_own, CORE), core, 0)
    mask_row = mask_both.reshape(2 * slot_count, length)
    mask_row = lax.dynamic_index_in_dim(mask_row, at_z, 0, False).astype(f32)
    token_gate = mask_row[:, None]

    x_half = to_images(tokens)

    qkv_cut = w_qkv.reshape(128, 3, 2, 2, 2, 128)
    fc1_cut = w_fc1.reshape(128, 4, 2, 2, 256)
    qkv_mine = lax.dynamic_index_in_dim(qkv_cut, core, 4, False)
    qkv_give = lax.dynamic_index_in_dim(qkv_cut, 1 - core, 4, False)
    qkv_rows = joined(qkv_mine, swap(qkv_give, CORE), core, 0)
    fc1_mine = lax.dynamic_index_in_dim(fc1_cut, core, 2, False)
    fc1_give = lax.dynamic_index_in_dim(fc1_cut, 1 - core, 2, False)
    fc1_rows = joined(fc1_mine, swap(fc1_give, CORE), core, 0)

    small_quad = ordered(small_pair, swap(small_pair, ALONG_X), at_x, 0)
    small_all = ordered(small_quad, swap(small_quad, ALONG_Y), at_y, 0)
    small_all = small_all.reshape(8, 14, 128).astype(f32)
    vectors = small_all[:, :10].transpose(1, 0, 2).reshape(10, width)
    gains, offsets = vectors[:4], vectors[4:]
    core_small = lax.dynamic_index_in_dim(small_all.reshape(4, 2, 14, 128), core, 1, False)
    bias = core_small[:, 10:].reshape(4, 2, 256).transpose(1, 0, 2).reshape(2, 1024)
    query_shift = core_small[:, 5].reshape(512)
    value_shift = core_small[:, 6].reshape(512)

    wire_x, wire_y = Wire(ALONG_X), Wire(ALONG_Y)
    qkv_a, qkv_b = gather_pair(
        qkv_rows[:, :, 0].reshape(256, 768), qkv_rows[:, :, 1].reshape(256, 768), wire_x, wire_y
    )
    qkv_w = (qkv_a.reshape(width, 768), qkv_b.reshape(width, 768))
    proj_a, proj_b = gather_pair(w_proj[:, :512], w_proj[:, 512:], wire_x, wire_y)
    proj_w = jnp.concatenate([proj_a.reshape(512, 512), proj_b.reshape(512, 512)], axis=1)
    fc1_a, fc1_b = gather_pair(
        fc1_rows[:, :, 0].reshape(256, 1024), fc1_rows[:, :, 1].reshape(256, 1024), wire_x, wire_y
    )
    fc1_w = (fc1_a.reshape(width, 1024), fc1_b.reshape(width, 1024))
    fc2_a, fc2_b = gather_pair(w_fc2[:256], w_fc2[256:], wire_x, wire_y)
    fc2_w = (fc2_a.reshape(1024, width), fc2_b.reshape(1024, width))

    inputs = joined(x_half, swap(x_half, CORE), core, 0).astype(f32)
    normed_one, unit_one, inverse_one = layer_norm(inputs, gains[0], offsets[0])
    normed_one = normed_one.astype(bf16)
    query, key, value = [], [], []
    for part in range(2):
        made = jnp.dot(normed_one, qkv_w[part], preferred_element_type=f32)
        span = slice(256 * part, 256 * part + 256)
        query.append((made[:, :256] + query_shift[span]).astype(bf16))
        key.append(made[:, 256:512].astype(bf16))
        value.append((made[:, 512:] + value_shift[span]).astype(bf16))
    head_shape = (length, 8, HD)
    query = jnp.concatenate(query, axis=1).reshape(head_shape)
    key = jnp.concatenate(key, axis=1).reshape(head_shape)
    value = jnp.concatenate(value, axis=1).reshape(head_shape)

    def scores_of():
        raw = jnp.einsum("qhe,khe->hqk", query, key, preferred_element_type=f32) * factor
        return jnp.where(mask_row[None, None, :] > 0, raw, -1e30)

    scores = scores_of()
    top = jnp.max(scores, axis=-1, keepdims=True)
    log_total = top + jnp.log(jnp.sum(jnp.exp(scores - top), axis=-1, keepdims=True))
    probs_low = jnp.exp(scores - log_total).astype(bf16)
    attended = jnp.einsum("hqk,khe->qhe", probs_low, value, preferred_element_type=f32)
    attended = attended.astype(bf16).reshape(length, 512)
    partial = jnp.dot(attended, proj_w, preferred_element_type=f32)
    other = swap(partial.astype(bf16), CORE)
    branch_one = partial + other.astype(f32) + offsets[3]
    hidden_state = inputs + branch_one * gains[1] * token_gate
    normed_two, unit_two, inverse_two = layer_norm(hidden_state, gains[2], offsets[4])
    normed_two = normed_two.astype(bf16)
    pre_act = [
        jnp.dot(normed_two, fc1_w[part], preferred_element_type=f32) + bias[part]
        for part in range(2)
    ]
    activated = [gelu_exact(item).astype(bf16) for item in pre_act]

    grad_half = to_images(after(cotangent, x_half))
    grad_out = joined(grad_half, swap(grad_half, CORE), core, 0).astype(f32)
    grad_branch_two = (grad_out * gains[3] * token_gate).astype(bf16)
    fc2_grads = [reduce_part(activated[part], grad_branch_two, part == 0) for part in range(2)]
    grad_pre = []
    for part in range(2):
        grad_act = jnp.einsum("td,fd->tf", grad_branch_two, fc2_w[part], preferred_element_type=f32)
        grad_pre.append((grad_act * gelu_slope(pre_act[part])).astype(bf16))
    partial = sum(
        jnp.einsum("tf,df->td", grad_pre[part], fc1_w[part], preferred_element_type=f32)
        for part in range(2)
    )
    other = swap(partial.astype(bf16), CORE)
    fc1_grads = [reduce_part(normed_two, grad_pre[part], part == 0) for part in range(2)]
    grad_normed_two = partial + other.astype(f32)
    grad_hidden = grad_out + norm_back(grad_normed_two, unit_two, inverse_two, gains[2])
    grad_branch_one = (grad_hidden * gains[1] * token_gate).astype(bf16)
    proj_grads = [
        reduce_part(attended, grad_branch_one[:, 512 * part : 512 * part + 512], part == 0)
        for part in range(2)
    ]
    grad_attended = jnp.einsum("te,de->td", grad_branch_one, proj_w, preferred_element_type=f32)
    grad_attended = grad_attended.astype(bf16).reshape(head_shape)
    probs = jnp.exp(scores_of() - log_total)
    probs_again = probs.astype(bf16)
    grad_probs = jnp.einsum("qhe,khe->hqk", grad_attended, value, preferred_element_type=f32)
    row_dot = jnp.sum(grad_probs * probs, axis=-1, keepdims=True)
    grad_scores = (probs * (grad_probs - row_dot)).astype(bf16)
    grad_query = jnp.einsum("hqk,khe->qhe", grad_scores, key, preferred_element_type=f32) * factor
    grad_key = jnp.einsum("hqk,qhe->khe", grad_scores, query, preferred_element_type=f32) * factor
    grad_value = jnp.einsum("hqk,qhe->khe", probs_again, grad_attended, preferred_element_type=f32)
    grad_query = grad_query.astype(bf16).reshape(length, 512)
    grad_key = grad_key.astype(bf16).reshape(length, 512)
    grad_value = grad_value.astype(bf16).reshape(length, 512)
    grad_joined = [
        jnp.concatenate(
            [item[:, 256 * part : 256 * part + 256] for item in (grad_query, grad_key, grad_value)],
            axis=1,
        )
        for part in range(2)
    ]
    qkv_grads = [reduce_part(normed_one, grad_joined[part], part == 0) for part in range(2)]
    partial = sum(
        jnp.einsum("te,de->td", grad_joined[part], qkv_w[part], preferred_element_type=f32)
        for part in range(2)
    )
    give = lax.dynamic_slice_in_dim(partial, (1 - core) * half_length, half_length, 0)
    other = swap(give.astype(bf16), CORE)
    grad_normed_one = own_half(partial) + other.astype(f32)
    unit_half = own_half(unit_one)
    grad_input = own_half(grad_hidden) + norm_back(
        grad_normed_one, unit_half, own_half(inverse_one), gains[0]
    )
    grad_tokens = from_images(grad_input.astype(bf16))

    partial = sum(
        jnp.dot(activated[part], fc2_w[part], preferred_element_type=f32) for part in range(2)
    )
    give = lax.dynamic_slice_in_dim(partial, (1 - core) * half_length, half_length, 0)
    other = swap(give.astype(bf16), CORE)
    branch_two = own_half(partial) + other.astype(f32) + offsets[5]
    gate_half = own_half(token_gate)
    grad_out_half = grad_half.astype(f32)
    output = own_half(hidden_state) + branch_two * gains[3] * gate_half
    output = from_images(output.astype(bf16))

    def rows_sum(values):
        return jnp.sum(values.astype(f32), axis=0)

    grad_normed_half = own_half(grad_normed_two)
    main = jnp.stack(
        [
            rows_sum(grad_normed_one * unit_half),
            rows_sum(own_half(grad_hidden) * gate_half * own_half(branch_one)),
            rows_sum(grad_normed_half * own_half(unit_two)),
            rows_sum(grad_out_half * gate_half * branch_two),
            rows_sum(grad_normed_one),
            rows_sum(own_half(grad_branch_one)),
            rows_sum(grad_normed_half),
            rows_sum(own_half(grad_branch_two)),
        ]
    )
    main = main.reshape(8, 4, 2, 128)
    bias_rows = jnp.stack([rows_sum(item).reshape(4, 256) for item in grad_pre], axis=1)
    local = jnp.concatenate(
        [
            rows_sum(grad_query).reshape(4, 1, 128),
            rows_sum(grad_value).reshape(4, 1, 128),
            bias_rows.reshape(4, 4, 128),
        ],
        axis=1,
    )
    keep = lax.dynamic_index_in_dim(main, core, 2, False)
    give = lax.dynamic_index_in_dim(main, 1 - core, 2, False)
    keep = (keep + swap(give, CORE)).transpose(1, 0, 2)
    small = jnp.concatenate([keep, local], axis=1).reshape(2, 2, 14, 128)
    keep = lax.dynamic_index_in_dim(small, at_x, 1, False)
    give = lax.dynamic_index_in_dim(small, 1 - at_x, 1, False)
    small = keep + swap(give, ALONG_X)
    keep = lax.dynamic_index_in_dim(small, at_y, 0, False)
    give = lax.dynamic_index_in_dim(small, 1 - at_y, 0, False)
    small = sum_along_line(keep + swap(give, ALONG_Y))
    grad_scales = small[:4]
    grad_shifts = jnp.stack([small[4], small[8], small[9], small[5], small[6], small[7]])
    grad_bias = small[10:].reshape(512)

    fc2_total = [sum_along_line(item) for item in fc2_grads]
    fc1_total = [sum_along_line(item) for item in fc1_grads]
    proj_total = [sum_along_line(item) for item in proj_grads]
    qkv_total = [sum_along_line(item) for item in qkv_grads]

    def rows_of_core(values):
        mine = lax.dynamic_slice_in_dim(values, core * 128, 128, 0)
        give = lax.dynamic_slice_in_dim(values, (1 - core) * 128, 128, 0)
        return mine, swap(give, CORE)

    fc1_out = []
    for item in fc1_total:
        mine, theirs = rows_of_core(item)
        fc1_out.append(ordered(mine.reshape(128, 4, 256), theirs.reshape(128, 4, 256), core, 2))
    grad_fc1 = jnp.stack(fc1_out, axis=3).reshape(128, 4096).astype(f32)
    qkv_out = []
    for item in qkv_total:
        mine, theirs = rows_of_core(item)
        shape = (128, 3, 2, 128)
        qkv_out.append(ordered(mine.reshape(shape), theirs.reshape(shape), core, 3))
    grad_qkv = jnp.stack(qkv_out, axis=2).reshape(128, 3072).astype(f32)
    grad_fc2 = jnp.concatenate(fc2_total, axis=0).astype(f32)
    grad_proj = jnp.concatenate(proj_total, axis=1).astype(f32)
    return (
        output,
        grad_tokens,
        grad_qkv,
        grad_proj,
        grad_fc1,
        grad_fc2,
        grad_bias,
        grad_scales,
        grad_shifts,
    )


def on_device(*arrays):
    tokens = arrays[0]
    whole_images = 2 * tokens.shape[0] == lax.axis_size("seq")
    if lax.axis_size("dp") == 8 and lax.axis_size("seq") == 4 and whole_images:
        return image_plan(*arrays)
    return general_plan(*arrays)


def solution(mesh):
    return jax.shard_map(
        on_device,
        mesh=mesh,
        in_specs=(
            P("dp", "seq", None),
            P("dp"),
            P("dp", None),
            P("dp", None),
            P("dp", None),
            P("dp", None),
            P("dp", None),
            P("dp"),
            P(None, "dp"),
            P(None, "dp"),
            P("dp", "seq", None),
        ),
        out_specs=(
            P("dp", "seq", None),
            P("dp", "seq", None),
            P("dp", None),
            P("dp", None),
            P("dp", None),
            P("dp", None),
            P("dp"),
            P(None, "dp"),
            P(None, "dp"),
        ),
        check_vma=False,
    )
```

```python
import jax
import jax.numpy as jnp
from jax import lax
from jax.experimental import pallas as pl
from jax.experimental.pallas import tpu as pltpu
from jax.sharding import PartitionSpec as P

HD = 64


EPSILON = 1e-06
ROOT_HALF = 0.7071067811865476
INV_ROOT_TWO_PI = 0.3989422804014327


def layer_norm(values, gain, shift):
    mean_row = jnp.mean(values, axis=-1, keepdims=True)
    centred = values - mean_row
    inverse = lax.rsqrt(jnp.mean(centred * centred, axis=-1, keepdims=True) + EPSILON)
    unit_rows = centred * inverse
    return (unit_rows * gain + shift, unit_rows, inverse)


def norm_back(grad_normed, unit_rows, inverse, gain):
    scaled = grad_normed * gain
    centre = jnp.mean(scaled, axis=-1, keepdims=True)
    along = jnp.mean(scaled * unit_rows, axis=-1, keepdims=True)
    return inverse * (scaled - centre - unit_rows * along)


def gelu_exact(values):
    return 0.5 * values * (1.0 + lax.erf(values * ROOT_HALF))


def gelu_slope(values):
    return (
        0.5 * (1.0 + lax.erf(values * ROOT_HALF))
        + values * jnp.exp(-0.5 * values * values) * INV_ROOT_TWO_PI
    )


def token_sum(values):
    return jnp.sum(values, axis=(0, 1))


def general_plan(
    tokens, group_count, pad_mask, w_qkv, w_proj, w_fc1, w_fc2, fc1_bias, scales, shifts, cotangent
):
    slot_count, piece, width = tokens.shape
    seq_total = pad_mask.shape[1]
    part_width = width // lax.axis_size("seq")
    head_count = part_width // HD
    factor = HD ** (-0.5)
    alive = jnp.arange(slot_count, dtype=jnp.int32) < group_count[0]
    key_mask = jnp.where(alive[:, None], pad_mask, 0).astype(jnp.float32)
    query_mask = lax.dynamic_slice_in_dim(key_mask, lax.axis_index("seq") * piece, piece, 1)[
        :, :, None
    ]
    full_qkv, full_proj, full_fc1, full_fc2, full_bias, full_scales, full_shifts = (
        lax.all_gather(w_qkv, "dp", axis=0, tiled=True),
        lax.all_gather(w_proj, "dp", axis=0, tiled=True),
        lax.all_gather(w_fc1, "dp", axis=0, tiled=True),
        lax.all_gather(w_fc2, "dp", axis=0, tiled=True),
        lax.all_gather(fc1_bias, "dp", axis=0, tiled=True),
        lax.all_gather(scales, "dp", axis=1, tiled=True),
        lax.all_gather(shifts, "dp", axis=1, tiled=True),
    )
    gains = full_scales.astype(jnp.float32)
    offsets = full_shifts.astype(jnp.float32)
    hidden_bias = full_bias.astype(jnp.float32)
    inputs = tokens.astype(jnp.float32)
    normed_one, unit_one, inverse_one = layer_norm(inputs, gains[0], offsets[0])
    normed_one = normed_one.astype(jnp.bfloat16)
    projected = jnp.dot(normed_one, full_qkv, preferred_element_type=jnp.float32)
    queries = (projected[:, :, :width] + offsets[1]).astype(jnp.bfloat16)
    key_rows = projected[:, :, width : 2 * width].astype(jnp.bfloat16)
    value_rows = (projected[:, :, 2 * width :] + offsets[2]).astype(jnp.bfloat16)
    head_query, head_key, head_value = (
        lax.all_to_all(queries, "seq", split_axis=2, concat_axis=1, tiled=True),
        lax.all_to_all(key_rows, "seq", split_axis=2, concat_axis=1, tiled=True),
        lax.all_to_all(value_rows, "seq", split_axis=2, concat_axis=1, tiled=True),
    )
    head_shape = (slot_count, seq_total, head_count, HD)
    query_heads = head_query.reshape(head_shape)
    key_heads = head_key.reshape(head_shape)
    value_heads = head_value.reshape(head_shape)

    def scores_of():
        raw = (
            jnp.einsum(
                "bqhe,bkhe->bhqk", query_heads, key_heads, preferred_element_type=jnp.float32
            )
            * factor
        )
        return jnp.where(key_mask[:, None, None, :] > 0, raw, -1e30)

    scores = scores_of()
    top = jnp.max(scores, axis=-1, keepdims=True)
    log_total = top + jnp.log(jnp.sum(jnp.exp(scores - top), axis=-1, keepdims=True))
    probs_low = jnp.exp(scores - log_total).astype(jnp.bfloat16)
    attended = jnp.einsum(
        "bhqk,bkhe->bqhe", probs_low, value_heads, preferred_element_type=jnp.float32
    )
    attended = attended.astype(jnp.bfloat16).reshape(slot_count, seq_total, part_width)
    mixed = lax.all_to_all(attended, "seq", split_axis=1, concat_axis=2, tiled=True)
    branch_one = jnp.dot(mixed, full_proj, preferred_element_type=jnp.float32) + offsets[3]
    hidden_state = inputs + branch_one * gains[1] * query_mask
    normed_two, unit_two, inverse_two = layer_norm(hidden_state, gains[2], offsets[4])
    normed_two = normed_two.astype(jnp.bfloat16)
    pre_act = jnp.dot(normed_two, full_fc1, preferred_element_type=jnp.float32) + hidden_bias
    activated = gelu_exact(pre_act).astype(jnp.bfloat16)
    branch_two = jnp.dot(activated, full_fc2, preferred_element_type=jnp.float32) + offsets[5]
    output = (hidden_state + branch_two * gains[3] * query_mask).astype(jnp.bfloat16)
    back_qkv, back_proj, back_fc1, back_fc2, back_gains = (
        full_qkv,
        full_proj,
        full_fc1,
        full_fc2,
        gains,
    )
    grad_out = cotangent.astype(jnp.float32)
    layer_gain_two = token_sum(grad_out * query_mask * branch_two)
    grad_branch_two = (grad_out * back_gains[3] * query_mask).astype(jnp.bfloat16)
    shift_five = token_sum(grad_branch_two.astype(jnp.float32))
    grad_fc2 = jnp.einsum(
        "spf,spd->fd", activated, grad_branch_two, preferred_element_type=jnp.float32
    )
    grad_act = jnp.einsum(
        "spd,fd->spf", grad_branch_two, back_fc2, preferred_element_type=jnp.float32
    )
    grad_pre = (grad_act * gelu_slope(pre_act)).astype(jnp.bfloat16)
    grad_hidden_bias = token_sum(grad_pre.astype(jnp.float32))
    grad_fc1 = jnp.einsum("spd,spf->df", normed_two, grad_pre, preferred_element_type=jnp.float32)
    grad_normed_two = jnp.einsum(
        "spf,df->spd", grad_pre, back_fc1, preferred_element_type=jnp.float32
    )
    norm_gain_two = token_sum(grad_normed_two * unit_two)
    norm_shift_two = token_sum(grad_normed_two)
    grad_hidden = grad_out + norm_back(grad_normed_two, unit_two, inverse_two, back_gains[2])
    layer_gain_one = token_sum(grad_hidden * query_mask * branch_one)
    grad_branch_one = (grad_hidden * back_gains[1] * query_mask).astype(jnp.bfloat16)
    shift_proj = token_sum(grad_branch_one.astype(jnp.float32))
    grad_proj = jnp.einsum(
        "spd,spe->de", mixed, grad_branch_one, preferred_element_type=jnp.float32
    )
    grad_mixed = jnp.einsum(
        "spe,de->spd", grad_branch_one, back_proj, preferred_element_type=jnp.float32
    )
    grad_mixed = grad_mixed.astype(jnp.bfloat16)
    grad_attended = lax.all_to_all(
        grad_mixed, "seq", split_axis=2, concat_axis=1, tiled=True
    ).reshape(head_shape)
    probs = jnp.exp(scores_of() - log_total)
    probs_again = probs.astype(jnp.bfloat16)
    grad_probs = jnp.einsum(
        "bqhe,bkhe->bhqk", grad_attended, value_heads, preferred_element_type=jnp.float32
    )
    row_dot = jnp.sum(grad_probs * probs, axis=-1, keepdims=True)
    grad_scores = (probs * (grad_probs - row_dot)).astype(jnp.bfloat16)
    flat_shape = (slot_count, seq_total, part_width)
    grad_query = (
        jnp.einsum("bhqk,bkhe->bqhe", grad_scores, key_heads, preferred_element_type=jnp.float32)
        * factor
    )
    grad_key = (
        jnp.einsum("bhqk,bqhe->bkhe", grad_scores, query_heads, preferred_element_type=jnp.float32)
        * factor
    )
    grad_value = jnp.einsum(
        "bhqk,bqhe->bkhe", probs_again, grad_attended, preferred_element_type=jnp.float32
    )
    grad_query = grad_query.astype(jnp.bfloat16).reshape(flat_shape)
    grad_key = grad_key.astype(jnp.bfloat16).reshape(flat_shape)
    grad_value = grad_value.astype(jnp.bfloat16).reshape(flat_shape)
    token_query, token_key, token_value = (
        lax.all_to_all(grad_query, "seq", split_axis=1, concat_axis=2, tiled=True),
        lax.all_to_all(grad_key, "seq", split_axis=1, concat_axis=2, tiled=True),
        lax.all_to_all(grad_value, "seq", split_axis=1, concat_axis=2, tiled=True),
    )
    grad_joined = jnp.concatenate([token_query, token_key, token_value], axis=2)
    grad_qkv = jnp.einsum(
        "spd,spe->de", normed_one, grad_joined, preferred_element_type=jnp.float32
    )
    grad_normed_one = jnp.einsum(
        "spe,de->spd", grad_joined, back_qkv, preferred_element_type=jnp.float32
    )
    norm_gain_one = token_sum(grad_normed_one * unit_one)
    norm_shift_one = token_sum(grad_normed_one)
    grad_input = (
        grad_hidden + norm_back(grad_normed_one, unit_one, inverse_one, back_gains[0])
    ).astype(jnp.bfloat16)
    gain_terms = jnp.stack([norm_gain_one, layer_gain_one, norm_gain_two, layer_gain_two])
    shift_terms = jnp.stack(
        [
            norm_shift_one,
            token_sum(token_query.astype(jnp.float32)),
            token_sum(token_value.astype(jnp.float32)),
            shift_proj,
            norm_shift_two,
            shift_five,
        ]
    )
    shares = (
        lax.psum_scatter(
            grad_qkv.astype(jnp.bfloat16), "dp", scatter_dimension=0, tiled=True
        ).astype(jnp.float32),
        lax.psum_scatter(
            grad_proj.astype(jnp.bfloat16), "dp", scatter_dimension=0, tiled=True
        ).astype(jnp.float32),
        lax.psum_scatter(
            grad_fc1.astype(jnp.bfloat16), "dp", scatter_dimension=0, tiled=True
        ).astype(jnp.float32),
        lax.psum_scatter(
            grad_fc2.astype(jnp.bfloat16), "dp", scatter_dimension=0, tiled=True
        ).astype(jnp.float32),
        lax.psum_scatter(
            grad_hidden_bias.astype(jnp.bfloat16), "dp", scatter_dimension=0, tiled=True
        ).astype(jnp.float32),
        lax.psum_scatter(
            gain_terms.astype(jnp.bfloat16), "dp", scatter_dimension=1, tiled=True
        ).astype(jnp.float32),
        lax.psum_scatter(
            shift_terms.astype(jnp.bfloat16), "dp", scatter_dimension=1, tiled=True
        ).astype(jnp.float32),
    )
    totals = (
        lax.psum(shares[0].astype(jnp.bfloat16), "seq").astype(jnp.float32),
        lax.psum(shares[1].astype(jnp.bfloat16), "seq").astype(jnp.float32),
        lax.psum(shares[2].astype(jnp.bfloat16), "seq").astype(jnp.float32),
        lax.psum(shares[3].astype(jnp.bfloat16), "seq").astype(jnp.float32),
        lax.psum(shares[4].astype(jnp.bfloat16), "seq").astype(jnp.float32),
        lax.psum(shares[5].astype(jnp.bfloat16), "seq").astype(jnp.float32),
        lax.psum(shares[6].astype(jnp.bfloat16), "seq").astype(jnp.float32),
    )
    return (
        output,
        grad_input,
        totals[0],
        totals[1],
        totals[2],
        totals[3],
        totals[4],
        totals[5],
        totals[6],
    )


CORE, ALONG_X, ALONG_Y = 1, 2, 4
NEGATIVE = -1e30


def swap(values, bit):
    size = lax.axis_size("dp")
    return lax.ppermute(values, "dp", [(i, i ^ bit) for i in range(size)])


def after(values, *earlier):
    return lax.optimization_barrier((values, earlier))[0]


def place():
    index = lax.axis_index("dp")
    return index % 2, (index // 2) % 2, index // 4


def joined(mine, theirs, bit, axis):
    low = jnp.where(bit == 0, mine, theirs)
    high = jnp.where(bit == 0, theirs, mine)
    return jnp.concatenate([low, high], axis=axis)


def local_call(kernel, outs, position, *arrays, scratch=(), room=40):
    return pl.pallas_call(
        kernel,
        out_shape=[jax.ShapeDtypeStruct(shape, kind) for shape, kind in outs],
        in_specs=[pl.BlockSpec(memory_space=pltpu.SMEM)]
        + [pl.BlockSpec(memory_space=pltpu.VMEM)] * len(arrays),
        out_specs=[pl.BlockSpec(memory_space=pltpu.VMEM)] * len(outs),
        scratch_shapes=[pltpu.VMEM(shape, kind) for shape, kind in scratch],
        compiler_params=pltpu.CompilerParams(vmem_limit_bytes=room * 1024 * 1024),
        cost_estimate=pl.CostEstimate(flops=1 << 20, bytes_accessed=1 << 16, transcendentals=0),
    )(position, *arrays)


def cut_kernel(
    pos, qkv, fc1, proj, fc2, scales, shifts, bias, mask, mine_qkv, mine_rest, give
):
    core = pos[0]
    top = pl.ds(0, 128)
    for j in range(12):
        here = pl.ds(j * 128, 128)
        mine_qkv[top, here] = qkv[:, pl.ds(pl.multiple_of((2 * j + core) * 128, 128), 128)]
        give[top, here] = qkv[:, pl.ds(pl.multiple_of((2 * j + 1 - core) * 128, 128), 128)]
    for j in range(4):
        mine_rest[:, pl.ds(j * 512, 512)] = fc1[
            :, pl.ds(pl.multiple_of((2 * j + core) * 512, 512), 512)
        ]
        give[top, pl.ds(1536 + j * 512, 512)] = fc1[
            :, pl.ds(pl.multiple_of((2 * j + 1 - core) * 512, 512), 512)
        ]
    mine_rest[:, pl.ds(2048, 512)] = proj[:, pl.ds(0, 512)]
    mine_rest[:, pl.ds(2560, 1024)] = fc2[pl.ds(0, 128), :]
    mine_rest[:, pl.ds(3584, 1024)] = fc2[pl.ds(128, 128), :]
    wide = [item[...].astype(jnp.float32) for item in (scales, shifts, bias)]
    small = jnp.concatenate(wide + [jnp.zeros((2, 128), jnp.float32)], axis=0)
    masks = [mask[:, j * 128 : j * 128 + 128] for j in range(mask.shape[1] // 128)]
    masks = jnp.concatenate(masks + [jnp.zeros((8, 128), jnp.float32)], axis=0)
    low = pl.ds(128, 16)
    mine_qkv[low, pl.ds(0, 128)] = small.astype(jnp.bfloat16)
    mine_qkv[low, pl.ds(128, 1408)] = jnp.zeros((16, 1408), jnp.bfloat16)
    give[low, pl.ds(0, 128)] = small.astype(jnp.bfloat16)
    give[low, pl.ds(128, 128)] = masks.astype(jnp.bfloat16)
    give[low, pl.ds(256, 3328)] = jnp.zeros((16, 3328), jnp.bfloat16)


def chips_of(pos):
    chip = 2 * pos[2] + pos[1]
    along_x = 2 * pos[2] + 1 - pos[1]
    along_y = 2 * (1 - pos[2]) + pos[1]
    across = 2 * (1 - pos[2]) + 1 - pos[1]
    return (chip, along_x, along_y, across), (chip, along_y, along_x, across)


def dot_of(left, right, left_dim, right_dim):
    return lax.dot_general(
        left, right, (((left_dim,), (right_dim,)), ((), ())), preferred_element_type=jnp.float32
    )


def low(values):
    return values.astype(jnp.bfloat16)


def wide(values):
    return values.astype(jnp.float32)


def down(values):
    return jnp.sum(values, axis=0, keepdims=True)


def unit_of(values):
    centred = values - jnp.mean(values, axis=1, keepdims=True)
    inverse = lax.rsqrt(jnp.mean(centred * centred, axis=1, keepdims=True) + EPSILON)
    return centred * inverse, inverse


def row_blocks(count, size=128):
    return [pl.ds(n * size, size) for n in range(count // size)]


def join_parts(pos, owners, near_a, far_a, near_b, far_b):
    for part, chips, near, far in zip((0, 1), chips_of(pos), (near_a, near_b), (far_a, far_b)):
        for n in range(4):
            yield part, chips[n], owners[part], (near, far)[n // 2], n % 2


def front_kernel(
    pos, mine, theirs, near_a, far_a, near_b, far_b, mask,
    weight, vectors, bias, inputs, grad_out, normed, qkv, attended,
):
    core = pos[0]
    for part, chip, owner, block, n in join_parts(
        pos, (core, 1 - core), near_a, far_a, near_b, far_b
    ):
        row = pl.multiple_of((2 * chip + owner) * 128, 128)
        weight[pl.ds(row, 128), :] = block[pl.ds(n * 144, 128), :]
        small = wide(block[pl.ds(n * 144 + 128, 16), pl.ds(0, 128)])
        vectors[:, pl.ds(row, 128)] = small
        if part == 0:
            for j in range(4):
                column = pl.multiple_of(chip * 512 + j * 128, 128)
                bias[:, pl.ds(column, 128)] = small[10 + j : 11 + j]
    half = mine.shape[0] // 2
    piece = half // 2
    for there, block in ((core, mine), (1 - core, theirs)):
        for turn in range(2):
            first = there * half + lax.rem(pos[3] + turn, 2) * piece
            rows = pl.ds(pl.multiple_of(first, piece), piece)
            inputs[rows, :] = block[pl.ds(turn * half, piece), :]
            grad_out[rows, :] = block[pl.ds(turn * half + piece, piece), :]
    for rows in row_blocks(2 * half):
        unit, _ = unit_of(wide(inputs[rows, :]))
        normed[rows, :] = low(unit * vectors[0:1, :] + vectors[4:5, :])
    for kind, shift in enumerate((5, None, 6)):
        made = dot_of(normed[...], weight[:, pl.ds(kind * 512, 512)], 1, 0)
        for chip in range(4):
            piece = made[:, chip * 128 : chip * 128 + 128]
            if shift is not None:
                column = pl.multiple_of((2 * chip + core) * 128, 128)
                piece = piece + vectors[shift : shift + 1, pl.ds(column, 128)]
            qkv[:, pl.ds(kind * 512 + chip * 128, 128)] = low(piece)
    lane = lax.broadcasted_iota(jnp.int32, (2 * half, 128), 1)
    live = mask[...] > 0
    for pair in range(4):
        query = qkv[:, pl.ds(pair * 128, 128)] * jnp.bfloat16(HD ** (-0.5))
        key = qkv[:, pl.ds(512 + pair * 128, 128)]
        value = qkv[:, pl.ds(1024 + pair * 128, 128)]
        got = []
        for head in range(2):
            chosen = (lane // HD) == head
            scores = dot_of(jnp.where(chosen, query, jnp.zeros_like(query)), key, 1, 1)
            scores = jnp.where(live, scores, NEGATIVE)
            expo = jnp.exp(scores - jnp.max(scores, axis=1, keepdims=True))
            probs = expo * (1.0 / jnp.sum(expo, axis=1, keepdims=True))
            got.append(dot_of(low(probs), value, 1, 0))
        attended[:, pl.ds(pair * 128, 128)] = low(jnp.where(lane < HD, got[0], got[1]))


def put_halves(values, tile, upper, lower):
    half = values.shape[0] // 2
    upper[:, tile] = low(values[:half])
    lower[:, tile] = low(values[half:])


def of_halves(upper, lower, n, size=128):
    count = upper.shape[0] // size
    return wide((upper, lower)[n // count][pl.ds((n % count) * size, size), :])


def proj_kernel(pos, attended, near_a, far_a, near_b, far_b, fc1, proj, partial, upper, lower):
    core = pos[0]
    for part, chip, owner, block, n in join_parts(
        pos, (core, 1 - core), near_a, far_a, near_b, far_b
    ):
        here = pl.ds(n * 128, 128)
        row = pl.multiple_of((2 * chip + owner) * 128, 128)
        fc1[pl.ds(row, 128), :] = block[here, pl.ds(0, 2048)]
        row = pl.multiple_of(chip * 128, 128)
        proj[pl.ds(row, 128), pl.ds(part * 512, 512)] = block[here, pl.ds(2048, 512)]
    for tile in row_blocks(1024, 256):
        made = dot_of(attended[...], proj[:, tile], 1, 0)
        partial[:, tile] = made
        put_halves(made, tile, upper, lower)


def far_chips(pos):
    return (1 - pos[1], 3 - pos[1]), (2 * (1 - pos[2]), 2 * (1 - pos[2]) + 1)


def second_chips(pos):
    own = 2 * pos[2] + pos[1]
    over_y = 2 * (1 - pos[2]) + pos[1]
    over_x = 2 * pos[2] + 1 - pos[1]
    return ((own, pos[2]), (over_y, 1 - pos[2])), ((own, pos[1]), (over_x, 1 - pos[1]))


def chip_columns(ref, chip, count):
    return ref[:, pl.ds(pl.multiple_of(chip * count, count), count)]


def far_products(pos, left, right, outs):
    rows = left.shape[1] // 4
    cut = right.shape[1] // 2
    for part, chips in enumerate(far_chips(pos)):
        for n in range(2):
            made = dot_of(
                chip_columns(left, chips[n], rows), right[:, pl.ds(part * cut, cut)], 0, 0
            )
            outs[part][pl.ds(n * rows, rows), :] = low(made)


def middle_kernel(
    pos, inputs, partial, upper, lower, vectors, bias, gate, fc1, grad_out,
    hidden, branch, normed, slope, activated, grad_two, far_a, far_b,
):
    for n, rows in enumerate(row_blocks(inputs.shape[0])):
        made = partial[rows, :] + of_halves(upper, lower, n) + vectors[7:8, :]
        branch[rows, :] = made
        state = wide(inputs[rows, :]) + made * vectors[1:2, :] * gate[rows, :]
        hidden[rows, :] = state
        unit, _ = unit_of(state)
        normed[rows, :] = low(unit * vectors[2:3, :] + vectors[8:9, :])
        grad_two[rows, :] = low(wide(grad_out[rows, :]) * vectors[3:4, :] * gate[rows, :])

    def units(n, _):
        tile = pl.ds(pl.multiple_of(n * 256, 256), 256)
        pre = dot_of(normed[...], fc1[:, tile], 1, 0) + bias[:, tile]
        bell = 0.5 * (1.0 + lax.erf(pre * ROOT_HALF))
        activated[:, tile] = low(pre * bell)
        slope[:, tile] = bell + pre * jnp.exp(-0.5 * pre * pre) * INV_ROOT_TWO_PI
        return 0

    lax.fori_loop(0, 8, units, 0)
    far_products(pos, activated, grad_two, (far_a, far_b))


def units_back_kernel(
    pos, near_a, far_a, near_b, far_b, grad_two, slope, activated, normed, fc1,
    grad_pre, sums, partial, upper, lower, out_a, out_b, branch, branch_low, fc2,
):
    for part, chip, _, block, n in join_parts(pos, (0, 0), near_a, far_a, near_b, far_b):
        for j in range(2):
            row = pl.multiple_of(chip * 512 + part * 256 + j * 128, 128)
            fc2[pl.ds(row, 128), :] = block[pl.ds(n * 128, 128), pl.ds(j * 1024, 1024)]

    def units(n, _):
        tile = pl.ds(pl.multiple_of(n * 256, 256), 256)
        made = low(dot_of(grad_two[...], fc2[tile, :], 1, 1) * slope[:, tile])
        grad_pre[:, tile] = made
        sums[:, tile] = down(wide(made))
        return 0

    lax.fori_loop(0, 8, units, 0)
    for tile in row_blocks(1024, 256):
        made = dot_of(grad_pre[...], fc1[tile, :], 1, 1)
        partial[:, tile] = made
        put_halves(made, tile, upper, lower)
    far_products(pos, normed, grad_pre, (out_a, out_b))
    for tile in row_blocks(1024, 256):
        made = dot_of(activated[...], fc2[:, tile], 1, 0)
        branch[:, tile] = made
        branch_low[:, tile] = low(made)


def norm_back_kernel(
    pos, grad_out, partial, upper, lower, hidden, branch, vectors, gate, proj,
    grad_hidden, grad_one, grad_attended, sums,
):
    total = [0.0] * 4
    for n, rows in enumerate(row_blocks(hidden.shape[0])):
        grad = partial[rows, :] + of_halves(upper, lower, n)
        unit, inverse = unit_of(hidden[rows, :])
        state = wide(grad_out[rows, :]) + norm_back(grad, unit, inverse, vectors[2:3, :])
        grad_hidden[rows, :] = state
        gated = state * gate[rows, :]
        made = low(gated * vectors[1:2, :])
        grad_one[rows, :] = made
        terms = (gated * branch[rows, :], grad * unit, wide(made), grad)
        total = [one + down(term) for one, term in zip(total, terms)]
    for n in range(4):
        sums[n : n + 1, :] = total[n]
    grad_attended[...] = low(dot_of(grad_one[...], proj[...], 1, 1))


def fold_kernel(pos, left, right, got_a, got_b, keep_a, give_a, keep_b, give_b):
    rows = left.shape[1] // 4
    cut = right.shape[1] // 2
    outs = ((keep_a, give_a), (keep_b, give_b))
    for part, chips in enumerate(second_chips(pos)):
        for n in range(2):
            chip, arrived = chips[n]
            made = dot_of(chip_columns(left, chip, rows), right[:, pl.ds(part * cut, cut)], 0, 0)
            there = pl.ds(pl.multiple_of(arrived * rows, rows), rows)
            outs[part][n][...] = low(made + wide((got_a, got_b)[part][there, :]))


def pair_products(normed, attended, grad_qkv, grad_one, chip, part):
    first = dot_of(chip_columns(normed, chip, 256), grad_qkv[:, pl.ds(part * 768, 768)], 0, 0)
    second = dot_of(chip_columns(attended, chip, 128), grad_one[:, pl.ds(part * 512, 512)], 0, 0)
    return first, second[:, :256], second[:, 256:]


def attend_back_kernel(
    pos, qkv, mask, grad, normed, attended, grad_one, out, sums, far_a, far_b
):
    length = qkv.shape[0]
    lane = lax.broadcasted_iota(jnp.int32, (length, 128), 1)
    live = mask[...] > 0
    factor = HD ** (-0.5)
    for pair in range(4):
        spans = [pl.ds(offset + pair * 128, 128) for offset in (0, 512, 1024)]
        query, key, value = (qkv[:, span] for span in spans)
        grad_pair = grad[:, pl.ds(pair * 128, 128)]
        grad_query, grad_key, grad_value = [], 0.0, 0.0
        for head in range(2):
            chosen = (lane // HD) == head
            query_one = jnp.where(chosen, query, jnp.zeros_like(query))
            grad_head = jnp.where(chosen, grad_pair, jnp.zeros_like(grad_pair))
            scores = dot_of(key, query_one, 1, 1) * factor
            scores = jnp.where(live, scores, NEGATIVE)
            expo = jnp.exp(scores - jnp.max(scores, axis=0, keepdims=True))
            probs = expo * (1.0 / jnp.sum(expo, axis=0, keepdims=True))
            grad_probs = dot_of(value, grad_head, 1, 1)
            along = jnp.sum(grad_probs * probs, axis=0, keepdims=True)
            grad_scores = low(probs * (grad_probs - along))
            grad_value += dot_of(low(probs), grad_head, 1, 0)
            grad_key += dot_of(grad_scores, query_one, 1, 0)
            grad_query.append(dot_of(grad_scores, key, 0, 0))
        made = jnp.where(lane < HD, grad_query[0], grad_query[1]) * factor
        for span, item in zip(spans, (made, grad_key * factor, grad_value)):
            item = low(item)
            out[:, span] = item
            sums[:, span] = down(wide(item))
    for part, chips in enumerate(far_chips(pos)):
        for n in range(2):
            first, left, right = pair_products(normed, attended, out, grad_one, chips[n], part)
            target = (far_a, far_b)[part]
            target[pl.ds(n * 256, 256), pl.ds(0, 768)] = low(first)
            target[pl.ds(n * 256, 128), pl.ds(768, 256)] = low(left)
            target[pl.ds(n * 256 + 128, 128), pl.ds(768, 256)] = low(right)


def last_fold_kernel(
    pos, normed, attended, grad_qkv, grad_one, got_a, got_b, small, small_got,
    keep_a, give_a, keep_b, give_b,
):
    outs = ((keep_a, give_a), (keep_b, give_b))
    for part, chips in enumerate(second_chips(pos)):
        got = (got_a, got_b)[part]
        for n in range(2):
            chip, arrived = chips[n]
            first, left, right = pair_products(normed, attended, grad_qkv, grad_one, chip, part)
            top = pl.ds(pl.multiple_of(arrived * 256, 256), 256)
            upper = pl.ds(pl.multiple_of(arrived * 256, 256), 128)
            lower = pl.ds(pl.multiple_of(arrived * 256 + 128, 128), 128)
            side = pl.ds(768, 256)
            out = outs[part][n]
            out[pl.ds(0, 256), pl.ds(0, 768)] = low(first + wide(got[top, pl.ds(0, 768)]))
            out[pl.ds(0, 128), side] = low(left + wide(got[upper, side]))
            out[pl.ds(128, 128), side] = low(right + wide(got[lower, side]))
    for out, at_y in ((keep_a, pos[2]), (give_a, 1 - pos[2])):
        column = pl.multiple_of(at_y * 128, 128)
        sums = small[at_y] + wide(small_got[:, pl.ds(column, 128)])
        out[pl.ds(256, 32), :] = jnp.zeros((32, 1024), jnp.bfloat16)
        out[pl.ds(256, 16), pl.ds(0, 128)] = low(sums)


def first_back_kernel(pos, grad_qkv, weight, partial, partial_low):
    for tile in row_blocks(1024, 256):
        made = dot_of(grad_qkv[...], weight[tile, :], 1, 1)
        partial[:, tile] = made
        partial_low[:, tile] = low(made)


def inputs_back_kernel(
    pos, inputs, partial, other, grad_hidden, vectors, out, sums, grads
):
    total = [0.0] * 2
    half = out.shape[0]
    for rows in row_blocks(2 * half):
        grad = partial[rows, :] + wide(other[rows, :])
        grads[rows, :] = grad
        unit, _ = unit_of(wide(inputs[rows, :]))
        total = [one + down(term) for one, term in zip(total, (grad * unit, grad))]
    for n in range(2):
        sums[n : n + 1, :] = total[n]
    for n in range(half // 128):
        rows = pl.ds(pl.multiple_of(pos[0] * half + n * 128, 128), 128)
        unit, inverse = unit_of(wide(inputs[rows, :]))
        state = grad_hidden[rows, :] + norm_back(grads[rows, :], unit, inverse, vectors[0:1, :])
        out[pl.ds(n * 128, 128), :] = low(state)


def output_kernel(
    pos, hidden, branch, other, vectors, gate, grad_out, grad_two, out, sums
):
    total = [0.0] * 2
    half = out.shape[0]
    for rows in row_blocks(2 * half):
        made = branch[rows, :] + wide(other[rows, :]) + vectors[9:10, :]
        terms = (wide(grad_out[rows, :]) * gate[rows, :] * made, wide(grad_two[rows, :]))
        total = [one + down(term) for one, term in zip(total, terms)]
    for n in range(2):
        sums[n : n + 1, :] = total[n]
    for n in range(half // 128):
        rows = pl.ds(pl.multiple_of(pos[0] * half + n * 128, 128), 128)
        made = branch[rows, :] + wide(other[rows, :]) + vectors[9:10, :]
        state = hidden[rows, :] + made * vectors[3:4, :] * gate[rows, :]
        out[pl.ds(n * 128, 128), :] = low(state)


def small_kernel(pos, first, second, last, attention, units, keep, give):
    core = pos[0]
    order = [(first, 0), (second, 0), (second, 1), (last, 0), (first, 1)]
    order += [None, None, (second, 2), (second, 3), (last, 1)]
    give[...] = jnp.zeros_like(give)
    for at_y in range(2):
        for over in range(2):
            chip = 2 * at_y + (pos[1] if over == 0 else 1 - pos[1])
            own = pl.ds(pl.multiple_of((2 * chip + core) * 128, 128), 128)
            here = pl.multiple_of(chip * 128, 128)
            lines = [None if item is None else item[0][item[1] : item[1] + 1, own] for item in order]
            lines[5] = attention[:, pl.ds(here, 128)]
            lines[6] = attention[:, pl.ds(pl.multiple_of(1024 + chip * 128, 128), 128)]
            for j in range(4):
                column = pl.multiple_of(chip * 512 + j * 128, 128)
                lines.append(units[:, pl.ds(column, 128)])
            block = jnp.concatenate(lines + [jnp.zeros((2, 128), jnp.float32)], axis=0)
            if over == 0:
                keep[at_y, :, :] = block
            else:
                give[:, pl.ds(at_y * 128, 128)] = low(block)


def finish_kernel(pos, qkv, qkv_got, fc1, fc1_got, out_qkv, out_fc1):
    core = pos[0]
    rows = pl.ds(pl.multiple_of(core * 128, 128), 128)
    for j in range(12):
        here = pl.ds(j * 128, 128)
        mine = pl.multiple_of((2 * j + core) * 128, 128)
        theirs = pl.multiple_of((2 * j + 1 - core) * 128, 128)
        out_qkv[:, pl.ds(mine, 128)] = qkv[rows, here].astype(jnp.float32)
        out_qkv[:, pl.ds(theirs, 128)] = qkv_got[:, here].astype(jnp.float32)
    for j in range(4):
        here = pl.ds(j * 512, 512)
        mine = pl.multiple_of((2 * j + core) * 512, 512)
        theirs = pl.multiple_of((2 * j + 1 - core) * 512, 512)
        out_fc1[:, pl.ds(mine, 512)] = fc1[rows, here].astype(jnp.float32)
        out_fc1[:, pl.ds(theirs, 512)] = fc1_got[:, here].astype(jnp.float32)


def add_low(one, two):
    return (one.astype(jnp.float32) + two.astype(jnp.float32)).astype(jnp.bfloat16)


def pairs_along_z(values):
    return lax.ppermute(values, "seq", [(0, 1), (1, 0), (2, 3), (3, 2)])


def mirror_along_z(values):
    return lax.ppermute(values, "seq", [(0, 3), (1, 2), (2, 1), (3, 0)])


def line_in(values):
    return lax.ppermute(values, "seq", [(0, 1), (3, 2)])


def line_mid(values):
    return lax.ppermute(values, "seq", [(1, 2), (2, 1)])


def line_out(values):
    return lax.ppermute(values, "seq", [(1, 0), (2, 3)])


def inner():
    at_z = lax.axis_index("seq")
    return ((at_z == 1) | (at_z == 2)).astype(jnp.int32)


def z_first(values):
    half = values.shape[0] // 2
    keep = lax.dynamic_slice_in_dim(values, inner() * half, half, 0)
    give = lax.dynamic_slice_in_dim(values, (1 - inner()) * half, half, 0)
    return keep, pairs_along_z(give)


def z_second(state):
    total = add_low(*state)
    return total, mirror_along_z(total)


def z_third(state):
    total = add_low(*state)
    return total, pairs_along_z(total)


def z_last(state):
    return joined(*state, inner(), 0)


def image_moves(back):
    seq = lax.axis_size("seq")
    rounds = []
    for turn in range(2):
        moves = []
        for chip in range(lax.axis_size("dp") // 2):
            for core in range(2):
                for quarter in range(seq):
                    slot = (quarter + turn) % 2
                    source = (2 * chip + core) * seq + quarter
                    target = (2 * chip + quarter // 2) * seq + 2 * core + slot
                    moves.append((target, source) if back else (source, target))
        rounds.append(moves)
    return rounds


def to_images(first, second, *earlier):
    at_z = lax.axis_index("seq")
    first, second = after((first, second), *earlier)
    got = []
    for turn, moves in enumerate(image_moves(False)):
        slot = (at_z + turn) % 2
        sent = [lax.dynamic_index_in_dim(item, slot, 0, False) for item in (first, second)]
        got.append(lax.ppermute(jnp.concatenate(sent, axis=0), ("dp", "seq"), moves))
    return jnp.concatenate(got, axis=0)


def from_images(values):
    at_z = lax.axis_index("seq")
    pieces = values.reshape(2, values.shape[0] // 2, values.shape[1])
    got = []
    for turn, moves in enumerate(image_moves(True)):
        sent = lax.dynamic_index_in_dim(pieces, (at_z + turn) % 2, 0, False)
        got.append(lax.ppermute(sent, ("dp", "seq"), moves))
    return got


def slots_of(got):
    even = lax.axis_index("seq") % 2 == 0
    return jnp.stack([jnp.where(even, got[0], got[1]), jnp.where(even, got[1], got[0])])


def image_plan(
    tokens, group_count, pad_mask, w_qkv, w_proj, w_fc1, w_fc2, fc1_bias, scales, shifts, cotangent
):
    slot_count, _, width = tokens.shape
    length = pad_mask.shape[1]
    half = length // 2
    f32, bf16 = jnp.float32, jnp.bfloat16
    core, at_x, at_y = place()
    at_z = lax.axis_index("seq")
    pos = jnp.stack([core, at_x, at_y, at_z]).astype(jnp.int32)

    alive = jnp.arange(slot_count, dtype=jnp.int32) < group_count[0]
    mask_own = jnp.where(alive[:, None], pad_mask, 0).astype(f32)
    mine_qkv, mine_rest, give = local_call(
        cut_kernel, [((144, 1536), bf16), ((128, 4608), bf16), ((144, 3584), bf16)],
        pos, w_qkv, w_fc1, w_proj, w_fc2, scales, shifts, fc1_bias.reshape(4, 128), mask_own,
    )
    got = swap(give, CORE)
    qkv_blocks = (mine_qkv, got[:, :1536])
    qkv_first = (swap(mine_qkv, ALONG_X), swap(qkv_blocks[1], ALONG_Y))
    rest = after(got[:128, 1536:], qkv_first[1])
    rest_blocks = (
        mine_rest,
        jnp.concatenate([rest, w_proj[:, 512:], w_fc2[256:384], w_fc2[384:]], axis=1),
    )
    mask_both = joined(
        mask_own,
        got[128:136, 128:256].reshape(4, slot_count, 128).transpose(1, 0, 2).reshape(
            slot_count, length
        ).astype(f32),
        core, 0,
    )
    mask_row = lax.dynamic_index_in_dim(mask_both, at_z, 0, False)
    token_gate = mask_row[:, None]

    def links(sent, order=(ALONG_X, ALONG_Y)):
        return swap(sent[0], order[0]), swap(sent[1], order[1])

    def second_link(blocks, got):
        near_a, near_b = (jnp.concatenate(pair, axis=0) for pair in zip(blocks, got))
        far_a, far_b = links((near_a, near_b), (ALONG_Y, ALONG_X))
        return near_a, far_a, near_b, far_b

    def columns_of(blocks, start, stop):
        return [block[:, start:stop] for block in blocks]

    rest_first = links(rest_blocks)
    both = to_images(tokens, cotangent, *rest_blocks)
    qkv_parts = second_link(qkv_blocks, qkv_first)
    rest_first = after(rest_first, qkv_parts[0], qkv_parts[2])
    fc1_parts = second_link(columns_of(rest_blocks, 0, 2560), columns_of(rest_first, 0, 2560))
    rest_first = after(rest_first, fc1_parts[0], fc1_parts[2])
    fc2_parts = second_link(columns_of(rest_blocks, 2560, 4608), columns_of(rest_first, 2560, 4608))

    full = (length, width)
    qkv_w, vectors, bias, inputs, grad_out, normed_one, qkv, attended = local_call(
        front_kernel,
        [
            ((width, 1536), bf16), ((16, width), f32), ((1, 2048), f32), (full, bf16),
            (full, bf16), (full, bf16), ((length, 1536), bf16), ((length, 512), bf16),
        ],
        pos, both, swap(both, CORE), *after(qkv_parts, fc2_parts[0], fc2_parts[2]),
        mask_row[None, :],
    )
    halves = [((half, width), bf16)] * 2
    fc1_w, proj_w, partial, upper, lower = local_call(
        proj_kernel,
        [((width, 2048), bf16), ((512, width), bf16), (full, f32)] + halves,
        pos, attended, *fc1_parts,
    )
    hidden, branch_one, normed_two, slope, activated, grad_two, far_a, far_b = local_call(
        middle_kernel,
        [
            (full, f32), (full, f32), (full, bf16), ((length, 2048), f32),
            ((length, 2048), bf16), (full, bf16), ((1024, 512), bf16), ((1024, 512), bf16),
        ],
        pos, inputs, partial, swap(upper, CORE), swap(lower, CORE), vectors, bias, token_gate,
        fc1_w, grad_out,
    )

    def fold(left, right, got, *earlier):
        block = (left.shape[1] // 4, right.shape[1] // 2)
        got_a, got_b = after(got, *earlier)
        keep_a, give_a, keep_b, give_b = local_call(
            fold_kernel, [(block, bf16)] * 4, pos, left, right, got_a, got_b
        )
        return (keep_a, keep_b), (give_a, give_b)

    def half_of(keep, got):
        return [add_low(one, two) for one, two in zip(keep, got)]

    fc2_got = links((far_a, far_b))
    grad_pre, unit_sums, partial, upper, lower, far_a, far_b, branch_two, branch_low = local_call(
        units_back_kernel,
        [((length, 2048), bf16), ((1, 2048), f32), (full, f32)]
        + halves
        + [((512, 1024), bf16), ((512, 1024), bf16), (full, f32), (full, bf16)],
        pos, *fc2_parts, grad_two, slope, activated, normed_two, fc1_w,
        scratch=[((2048, width), bf16)],
    )
    others = [swap(item, CORE) for item in (upper, lower)]
    branch_other = swap(branch_low, CORE)
    output, last_sums = local_call(
        output_kernel, [((half, width), bf16), ((2, width), f32)],
        pos, hidden, branch_two, branch_other, vectors, token_gate, grad_out,
        grad_two,
    )
    out_got = from_images(output)
    fc2_keep, fc2_give = fold(activated, grad_two, fc2_got, output)
    fc2_again = links(fc2_give, (ALONG_Y, ALONG_X))
    fc1_got = links(after((far_a, far_b), *fc2_give))
    grad_hidden, grad_one, grad_attended, second_sums = local_call(
        norm_back_kernel, [(full, f32), (full, bf16), ((length, 512), bf16), ((4, width), f32)],
        pos, grad_out, partial, *after(others, *fc2_give), hidden, branch_one, vectors,
        token_gate, proj_w,
    )
    fc2_half = jnp.concatenate(half_of(fc2_keep, after(fc2_again, grad_attended, *out_got)), axis=1)
    fc2_in = line_in(fc2_half)
    grad_qkv_rows, attention_sums, far_a, far_b = local_call(
        attend_back_kernel,
        [
            ((length, 1536), bf16), ((1, 1536), f32), ((512, 1024), bf16), ((512, 1024), bf16),
        ],
        pos, after(qkv, fc2_half), token_gate, grad_attended, normed_one, attended, grad_one,
    )
    partial, partial_low = local_call(
        first_back_kernel, [(full, f32), (full, bf16)], pos, grad_qkv_rows, qkv_w
    )
    fc1_keep, fc1_give = fold(normed_two, grad_pre, fc1_got, partial_low)
    fc1_again = links(fc1_give, (ALONG_Y, ALONG_X))
    last_got = links(after((far_a, far_b), *fc1_give))
    fc2_sum = add_low(fc2_half, after(fc2_in, *fc1_give))
    fc2_mid = line_mid(fc2_sum)
    grad_input, first_sums = local_call(
        inputs_back_kernel, [((half, width), bf16), ((2, width), f32)],
        pos, inputs, partial, after(swap(partial_low, CORE), fc2_sum), grad_hidden, vectors,
        scratch=[(full, f32)],
    )
    in_got = from_images(grad_input)
    small_keep, small_give = local_call(
        small_kernel, [((2, 16, 128), f32), ((16, 1024), bf16)],
        pos, first_sums, second_sums, last_sums, attention_sums, unit_sums,
    )
    small_got = swap(small_give, ALONG_X)

    fc1_half = jnp.concatenate(half_of(fc1_keep, after(fc1_again, small_give)), axis=1)
    fc1_in = line_in(fc1_half)
    fc2_total = add_low(fc2_sum, after(fc2_mid, fc1_half))
    fc2_out = line_out(fc2_total)
    last_got, small_got = after((last_got, small_got), fc2_total, *in_got)
    wide_block, block = ((288, 1024), bf16), ((256, 1024), bf16)
    keep_a, give_a, keep_b, give_b = local_call(
        last_fold_kernel, [wide_block, wide_block, block, block],
        pos, normed_one, attended, grad_qkv_rows, grad_one, *last_got, small_keep, small_got,
    )
    last_again = links((give_a, give_b), (ALONG_Y, ALONG_X))
    fc1_sum = add_low(fc1_half, after(fc1_in, give_a, give_b))
    fc1_mid = line_mid(fc1_sum)
    last_half = half_of((keep_a, keep_b), after(last_again, fc1_sum))
    last_state = [z_first(item) for item in last_half]
    fc1_total = add_low(fc1_sum, after(fc1_mid, last_state[0][0], last_state[1][0]))
    fc1_out = line_out(fc1_total)
    last_state = [z_second(item) for item in after(last_state, fc1_total)]
    last_state = [z_third(item) for item in last_state]
    late = (last_state[0][0], last_state[1][0])

    def line_end(total, out):
        return jnp.where(inner() == 1, total, out)

    grad_fc2 = line_end(fc2_total, after(fc2_out, *late)).astype(f32)
    fc1_rows = line_end(fc1_total, after(fc1_out, grad_fc2))

    def core_give(values):
        return lax.dynamic_slice_in_dim(values, (1 - core) * 128, 128, 0)

    fc1_core = swap(core_give(fc1_rows), CORE)
    last_rows = [z_last(item) for item in after(last_state, fc1_rows)]
    small = last_rows[0][256:272, :128].astype(f32)
    qkv_rows = jnp.concatenate([last_rows[0][:256, :768], last_rows[1][:, :768]], axis=1)
    qkv_core = swap(core_give(qkv_rows), CORE)
    grad_proj = jnp.concatenate(
        [part[rows : rows + 128, 768:] for part in last_rows for rows in (0, 128)], axis=1
    ).astype(f32)
    grad_qkv, grad_fc1 = local_call(
        finish_kernel, [((128, 3072), f32), ((128, 4096), f32)],
        pos, qkv_rows, qkv_core, fc1_rows, fc1_core,
    )
    grad_scales = small[:4]
    grad_shifts = small[4:10]
    grad_bias = small[10:14].reshape(512)
    return (
        slots_of(out_got),
        slots_of(in_got),
        grad_qkv,
        grad_proj,
        grad_fc1,
        grad_fc2,
        grad_bias,
        grad_scales,
        grad_shifts,
    )


def on_device(*arrays):
    tokens = arrays[0]
    whole_images = 2 * tokens.shape[0] == lax.axis_size("seq")
    if lax.axis_size("dp") == 8 and lax.axis_size("seq") == 4 and whole_images:
        return image_plan(*arrays)
    return general_plan(*arrays)


def solution(mesh):
    return jax.shard_map(
        on_device,
        mesh=mesh,
        in_specs=(
            P("dp", "seq", None),
            P("dp"),
            P("dp", None),
            P("dp", None),
            P("dp", None),
            P("dp", None),
            P("dp", None),
            P("dp"),
            P(None, "dp"),
            P(None, "dp"),
            P("dp", "seq", None),
        ),
        out_specs=(
            P("dp", "seq", None),
            P("dp", "seq", None),
            P("dp", None),
            P("dp", None),
            P("dp", None),
            P("dp", None),
            P("dp"),
            P(None, "dp"),
            P(None, "dp"),
        ),
        check_vma=False,
    )
```

```python
import jax
import jax.numpy as jnp
from jax import lax
from jax.experimental import pallas as pl
from jax.experimental.pallas import tpu as pltpu
from jax.sharding import PartitionSpec as P

HD = 64


EPSILON = 1e-06
ROOT_HALF = 0.7071067811865476
INV_ROOT_TWO_PI = 0.3989422804014327


def layer_norm(values, gain, shift):
    mean_row = jnp.mean(values, axis=-1, keepdims=True)
    centred = values - mean_row
    inverse = lax.rsqrt(jnp.mean(centred * centred, axis=-1, keepdims=True) + EPSILON)
    unit_rows = centred * inverse
    return (unit_rows * gain + shift, unit_rows, inverse)


def norm_back(grad_normed, unit_rows, inverse, gain):
    scaled = grad_normed * gain
    centre = jnp.mean(scaled, axis=-1, keepdims=True)
    along = jnp.mean(scaled * unit_rows, axis=-1, keepdims=True)
    return inverse * (scaled - centre - unit_rows * along)


def gelu_exact(values):
    return 0.5 * values * (1.0 + lax.erf(values * ROOT_HALF))


def gelu_slope(values):
    return (
        0.5 * (1.0 + lax.erf(values * ROOT_HALF))
        + values * jnp.exp(-0.5 * values * values) * INV_ROOT_TWO_PI
    )


def token_sum(values):
    return jnp.sum(values, axis=(0, 1))


def general_plan(
    tokens, group_count, pad_mask, w_qkv, w_proj, w_fc1, w_fc2, fc1_bias, scales, shifts, cotangent
):
    slot_count, piece, width = tokens.shape
    seq_total = pad_mask.shape[1]
    part_width = width // lax.axis_size("seq")
    head_count = part_width // HD
    factor = HD ** (-0.5)
    alive = jnp.arange(slot_count, dtype=jnp.int32) < group_count[0]
    key_mask = jnp.where(alive[:, None], pad_mask, 0).astype(jnp.float32)
    query_mask = lax.dynamic_slice_in_dim(key_mask, lax.axis_index("seq") * piece, piece, 1)[
        :, :, None
    ]
    full_qkv, full_proj, full_fc1, full_fc2, full_bias, full_scales, full_shifts = (
        lax.all_gather(w_qkv, "dp", axis=0, tiled=True),
        lax.all_gather(w_proj, "dp", axis=0, tiled=True),
        lax.all_gather(w_fc1, "dp", axis=0, tiled=True),
        lax.all_gather(w_fc2, "dp", axis=0, tiled=True),
        lax.all_gather(fc1_bias, "dp", axis=0, tiled=True),
        lax.all_gather(scales, "dp", axis=1, tiled=True),
        lax.all_gather(shifts, "dp", axis=1, tiled=True),
    )
    gains = full_scales.astype(jnp.float32)
    offsets = full_shifts.astype(jnp.float32)
    hidden_bias = full_bias.astype(jnp.float32)
    inputs = tokens.astype(jnp.float32)
    normed_one, unit_one, inverse_one = layer_norm(inputs, gains[0], offsets[0])
    normed_one = normed_one.astype(jnp.bfloat16)
    projected = jnp.dot(normed_one, full_qkv, preferred_element_type=jnp.float32)
    queries = (projected[:, :, :width] + offsets[1]).astype(jnp.bfloat16)
    key_rows = projected[:, :, width : 2 * width].astype(jnp.bfloat16)
    value_rows = (projected[:, :, 2 * width :] + offsets[2]).astype(jnp.bfloat16)
    head_query, head_key, head_value = (
        lax.all_to_all(queries, "seq", split_axis=2, concat_axis=1, tiled=True),
        lax.all_to_all(key_rows, "seq", split_axis=2, concat_axis=1, tiled=True),
        lax.all_to_all(value_rows, "seq", split_axis=2, concat_axis=1, tiled=True),
    )
    head_shape = (slot_count, seq_total, head_count, HD)
    query_heads = head_query.reshape(head_shape)
    key_heads = head_key.reshape(head_shape)
    value_heads = head_value.reshape(head_shape)

    def scores_of():
        raw = (
            jnp.einsum(
                "bqhe,bkhe->bhqk", query_heads, key_heads, preferred_element_type=jnp.float32
            )
            * factor
        )
        return jnp.where(key_mask[:, None, None, :] > 0, raw, -1e30)

    scores = scores_of()
    top = jnp.max(scores, axis=-1, keepdims=True)
    log_total = top + jnp.log(jnp.sum(jnp.exp(scores - top), axis=-1, keepdims=True))
    probs_low = jnp.exp(scores - log_total).astype(jnp.bfloat16)
    attended = jnp.einsum(
        "bhqk,bkhe->bqhe", probs_low, value_heads, preferred_element_type=jnp.float32
    )
    attended = attended.astype(jnp.bfloat16).reshape(slot_count, seq_total, part_width)
    mixed = lax.all_to_all(attended, "seq", split_axis=1, concat_axis=2, tiled=True)
    branch_one = jnp.dot(mixed, full_proj, preferred_element_type=jnp.float32) + offsets[3]
    hidden_state = inputs + branch_one * gains[1] * query_mask
    normed_two, unit_two, inverse_two = layer_norm(hidden_state, gains[2], offsets[4])
    normed_two = normed_two.astype(jnp.bfloat16)
    pre_act = jnp.dot(normed_two, full_fc1, preferred_element_type=jnp.float32) + hidden_bias
    activated = gelu_exact(pre_act).astype(jnp.bfloat16)
    branch_two = jnp.dot(activated, full_fc2, preferred_element_type=jnp.float32) + offsets[5]
    output = (hidden_state + branch_two * gains[3] * query_mask).astype(jnp.bfloat16)
    back_qkv, back_proj, back_fc1, back_fc2, back_gains = (
        full_qkv,
        full_proj,
        full_fc1,
        full_fc2,
        gains,
    )
    grad_out = cotangent.astype(jnp.float32)
    layer_gain_two = token_sum(grad_out * query_mask * branch_two)
    grad_branch_two = (grad_out * back_gains[3] * query_mask).astype(jnp.bfloat16)
    shift_five = token_sum(grad_branch_two.astype(jnp.float32))
    grad_fc2 = jnp.einsum(
        "spf,spd->fd", activated, grad_branch_two, preferred_element_type=jnp.float32
    )
    grad_act = jnp.einsum(
        "spd,fd->spf", grad_branch_two, back_fc2, preferred_element_type=jnp.float32
    )
    grad_pre = (grad_act * gelu_slope(pre_act)).astype(jnp.bfloat16)
    grad_hidden_bias = token_sum(grad_pre.astype(jnp.float32))
    grad_fc1 = jnp.einsum("spd,spf->df", normed_two, grad_pre, preferred_element_type=jnp.float32)
    grad_normed_two = jnp.einsum(
        "spf,df->spd", grad_pre, back_fc1, preferred_element_type=jnp.float32
    )
    norm_gain_two = token_sum(grad_normed_two * unit_two)
    norm_shift_two = token_sum(grad_normed_two)
    grad_hidden = grad_out + norm_back(grad_normed_two, unit_two, inverse_two, back_gains[2])
    layer_gain_one = token_sum(grad_hidden * query_mask * branch_one)
    grad_branch_one = (grad_hidden * back_gains[1] * query_mask).astype(jnp.bfloat16)
    shift_proj = token_sum(grad_branch_one.astype(jnp.float32))
    grad_proj = jnp.einsum(
        "spd,spe->de", mixed, grad_branch_one, preferred_element_type=jnp.float32
    )
    grad_mixed = jnp.einsum(
        "spe,de->spd", grad_branch_one, back_proj, preferred_element_type=jnp.float32
    )
    grad_mixed = grad_mixed.astype(jnp.bfloat16)
    grad_attended = lax.all_to_all(
        grad_mixed, "seq", split_axis=2, concat_axis=1, tiled=True
    ).reshape(head_shape)
    probs = jnp.exp(scores_of() - log_total)
    probs_again = probs.astype(jnp.bfloat16)
    grad_probs = jnp.einsum(
        "bqhe,bkhe->bhqk", grad_attended, value_heads, preferred_element_type=jnp.float32
    )
    row_dot = jnp.sum(grad_probs * probs, axis=-1, keepdims=True)
    grad_scores = (probs * (grad_probs - row_dot)).astype(jnp.bfloat16)
    flat_shape = (slot_count, seq_total, part_width)
    grad_query = (
        jnp.einsum("bhqk,bkhe->bqhe", grad_scores, key_heads, preferred_element_type=jnp.float32)
        * factor
    )
    grad_key = (
        jnp.einsum("bhqk,bqhe->bkhe", grad_scores, query_heads, preferred_element_type=jnp.float32)
        * factor
    )
    grad_value = jnp.einsum(
        "bhqk,bqhe->bkhe", probs_again, grad_attended, preferred_element_type=jnp.float32
    )
    grad_query = grad_query.astype(jnp.bfloat16).reshape(flat_shape)
    grad_key = grad_key.astype(jnp.bfloat16).reshape(flat_shape)
    grad_value = grad_value.astype(jnp.bfloat16).reshape(flat_shape)
    token_query, token_key, token_value = (
        lax.all_to_all(grad_query, "seq", split_axis=1, concat_axis=2, tiled=True),
        lax.all_to_all(grad_key, "seq", split_axis=1, concat_axis=2, tiled=True),
        lax.all_to_all(grad_value, "seq", split_axis=1, concat_axis=2, tiled=True),
    )
    grad_joined = jnp.concatenate([token_query, token_key, token_value], axis=2)
    grad_qkv = jnp.einsum(
        "spd,spe->de", normed_one, grad_joined, preferred_element_type=jnp.float32
    )
    grad_normed_one = jnp.einsum(
        "spe,de->spd", grad_joined, back_qkv, preferred_element_type=jnp.float32
    )
    norm_gain_one = token_sum(grad_normed_one * unit_one)
    norm_shift_one = token_sum(grad_normed_one)
    grad_input = (
        grad_hidden + norm_back(grad_normed_one, unit_one, inverse_one, back_gains[0])
    ).astype(jnp.bfloat16)
    gain_terms = jnp.stack([norm_gain_one, layer_gain_one, norm_gain_two, layer_gain_two])
    shift_terms = jnp.stack(
        [
            norm_shift_one,
            token_sum(token_query.astype(jnp.float32)),
            token_sum(token_value.astype(jnp.float32)),
            shift_proj,
            norm_shift_two,
            shift_five,
        ]
    )
    shares = (
        lax.psum_scatter(
            grad_qkv.astype(jnp.bfloat16), "dp", scatter_dimension=0, tiled=True
        ).astype(jnp.float32),
        lax.psum_scatter(
            grad_proj.astype(jnp.bfloat16), "dp", scatter_dimension=0, tiled=True
        ).astype(jnp.float32),
        lax.psum_scatter(
            grad_fc1.astype(jnp.bfloat16), "dp", scatter_dimension=0, tiled=True
        ).astype(jnp.float32),
        lax.psum_scatter(
            grad_fc2.astype(jnp.bfloat16), "dp", scatter_dimension=0, tiled=True
        ).astype(jnp.float32),
        lax.psum_scatter(
            grad_hidden_bias.astype(jnp.bfloat16), "dp", scatter_dimension=0, tiled=True
        ).astype(jnp.float32),
        lax.psum_scatter(
            gain_terms.astype(jnp.bfloat16), "dp", scatter_dimension=1, tiled=True
        ).astype(jnp.float32),
        lax.psum_scatter(
            shift_terms.astype(jnp.bfloat16), "dp", scatter_dimension=1, tiled=True
        ).astype(jnp.float32),
    )
    totals = (
        lax.psum(shares[0].astype(jnp.bfloat16), "seq").astype(jnp.float32),
        lax.psum(shares[1].astype(jnp.bfloat16), "seq").astype(jnp.float32),
        lax.psum(shares[2].astype(jnp.bfloat16), "seq").astype(jnp.float32),
        lax.psum(shares[3].astype(jnp.bfloat16), "seq").astype(jnp.float32),
        lax.psum(shares[4].astype(jnp.bfloat16), "seq").astype(jnp.float32),
        lax.psum(shares[5].astype(jnp.bfloat16), "seq").astype(jnp.float32),
        lax.psum(shares[6].astype(jnp.bfloat16), "seq").astype(jnp.float32),
    )
    return (
        output,
        grad_input,
        totals[0],
        totals[1],
        totals[2],
        totals[3],
        totals[4],
        totals[5],
        totals[6],
    )


CORE, ALONG_X, ALONG_Y = 1, 2, 4
NEGATIVE = -1e30


def swap(values, bit):
    size = lax.axis_size("dp")
    return lax.ppermute(values, "dp", [(i, i ^ bit) for i in range(size)])


def after(values, *earlier):
    return lax.optimization_barrier((values, earlier))[0]


def place():
    index = lax.axis_index("dp")
    return index % 2, (index // 2) % 2, index // 4


def joined(mine, theirs, bit, axis):
    low = jnp.where(bit == 0, mine, theirs)
    high = jnp.where(bit == 0, theirs, mine)
    return jnp.concatenate([low, high], axis=axis)


def local_call(kernel, outs, position, *arrays, scratch=(), room=40):
    return pl.pallas_call(
        kernel,
        out_shape=[jax.ShapeDtypeStruct(shape, kind) for shape, kind in outs],
        in_specs=[pl.BlockSpec(memory_space=pltpu.SMEM)]
        + [pl.BlockSpec(memory_space=pltpu.VMEM)] * len(arrays),
        out_specs=[pl.BlockSpec(memory_space=pltpu.VMEM)] * len(outs),
        scratch_shapes=[pltpu.VMEM(shape, kind) for shape, kind in scratch],
        compiler_params=pltpu.CompilerParams(vmem_limit_bytes=room * 1024 * 1024),
        cost_estimate=pl.CostEstimate(flops=1 << 20, bytes_accessed=1 << 16, transcendentals=0),
    )(position, *arrays)


def cut_kernel(pos, qkv, fc1, proj, scales, shifts, bias, mask, mine, give):
    core = pos[0]
    for j in range(12):
        here = pl.ds(j * 128, 128)
        mine[:, here] = qkv[:, pl.ds(pl.multiple_of((2 * j + core) * 128, 128), 128)]
        give[:, here] = qkv[:, pl.ds(pl.multiple_of((2 * j + 1 - core) * 128, 128), 128)]
    for j in range(4):
        here = pl.ds(1664 + j * 512, 512)
        mine[:, here] = fc1[:, pl.ds(pl.multiple_of((2 * j + core) * 512, 512), 512)]
        give[:, here] = fc1[:, pl.ds(pl.multiple_of((2 * j + 1 - core) * 512, 512), 512)]
    mine[:, pl.ds(3712, 512)] = proj[:, pl.ds(0, 512)]
    wide = [item[...].astype(jnp.float32) for item in (scales, shifts, bias)]
    small = jnp.concatenate(wide + [jnp.zeros((114, 128), jnp.float32)], axis=0)
    masks = [mask[:, j * 128 : j * 128 + 128] for j in range(mask.shape[1] // 128)]
    masks = jnp.concatenate(masks + [jnp.zeros((120, 128), jnp.float32)], axis=0)
    mine[:, pl.ds(1536, 128)] = small.astype(jnp.bfloat16)
    give[:, pl.ds(1536, 128)] = small.astype(jnp.bfloat16)
    give[:, pl.ds(3712, 128)] = masks.astype(jnp.bfloat16)


def chips_of(pos):
    chip = 2 * pos[2] + pos[1]
    along_x = 2 * pos[2] + 1 - pos[1]
    along_y = 2 * (1 - pos[2]) + pos[1]
    across = 2 * (1 - pos[2]) + 1 - pos[1]
    return (chip, along_x, along_y, across), (chip, along_y, along_x, across)


def dot_of(left, right, left_dim, right_dim):
    return lax.dot_general(
        left, right, (((left_dim,), (right_dim,)), ((), ())), preferred_element_type=jnp.float32
    )


def low(values):
    return values.astype(jnp.bfloat16)


def wide(values):
    return values.astype(jnp.float32)


def down(values):
    return jnp.sum(values, axis=0, keepdims=True)


def unit_of(values):
    centred = values - jnp.mean(values, axis=1, keepdims=True)
    inverse = lax.rsqrt(jnp.mean(centred * centred, axis=1, keepdims=True) + EPSILON)
    return centred * inverse, inverse


def row_blocks(count, size=128):
    return [pl.ds(n * size, size) for n in range(count // size)]


def join_parts(pos, owners, near_a, far_a, near_b, far_b):
    for part, chips, near, far in zip((0, 1), chips_of(pos), (near_a, near_b), (far_a, far_b)):
        for n in range(4):
            yield part, chips[n], owners[part], (near, far)[n // 2], n % 2


def front_kernel(
    pos, mine, theirs, near_a, far_a, near_b, far_b, mask,
    weight, vectors, bias, inputs, grad_out, normed, qkv, attended,
):
    core = pos[0]
    for part, chip, owner, block, n in join_parts(
        pos, (core, 1 - core), near_a, far_a, near_b, far_b
    ):
        row = pl.multiple_of((2 * chip + owner) * 128, 128)
        weight[pl.ds(row, 128), :] = block[pl.ds(n * 128, 128), pl.ds(0, 1536)]
        small = wide(block[pl.ds(n * 128, 16), pl.ds(1536, 128)])
        vectors[:, pl.ds(row, 128)] = small
        if part == 0:
            for j in range(4):
                column = pl.multiple_of(chip * 512 + j * 128, 128)
                bias[:, pl.ds(column, 128)] = small[10 + j : 11 + j]
    half = mine.shape[0] // 2
    piece = half // 2
    for there, block in ((core, mine), (1 - core, theirs)):
        for turn in range(2):
            first = there * half + lax.rem(pos[3] + turn, 2) * piece
            rows = pl.ds(pl.multiple_of(first, piece), piece)
            inputs[rows, :] = block[pl.ds(turn * half, piece), :]
            grad_out[rows, :] = block[pl.ds(turn * half + piece, piece), :]
    for rows in row_blocks(2 * half):
        unit, _ = unit_of(wide(inputs[rows, :]))
        normed[rows, :] = low(unit * vectors[0:1, :] + vectors[4:5, :])
    for kind, shift in enumerate((5, None, 6)):
        made = dot_of(normed[...], weight[:, pl.ds(kind * 512, 512)], 1, 0)
        for chip in range(4):
            piece = made[:, chip * 128 : chip * 128 + 128]
            if shift is not None:
                column = pl.multiple_of((2 * chip + core) * 128, 128)
                piece = piece + vectors[shift : shift + 1, pl.ds(column, 128)]
            qkv[:, pl.ds(kind * 512 + chip * 128, 128)] = low(piece)
    lane = lax.broadcasted_iota(jnp.int32, (2 * half, 128), 1)
    live = mask[...] > 0
    for pair in range(4):
        query = qkv[:, pl.ds(pair * 128, 128)] * jnp.bfloat16(HD ** (-0.5))
        key = qkv[:, pl.ds(512 + pair * 128, 128)]
        value = qkv[:, pl.ds(1024 + pair * 128, 128)]
        got = []
        for head in range(2):
            chosen = (lane // HD) == head
            scores = dot_of(jnp.where(chosen, query, jnp.zeros_like(query)), key, 1, 1)
            scores = jnp.where(live, scores, NEGATIVE)
            expo = jnp.exp(scores - jnp.max(scores, axis=1, keepdims=True))
            probs = expo * (1.0 / jnp.sum(expo, axis=1, keepdims=True))
            got.append(dot_of(low(probs), value, 1, 0))
        attended[:, pl.ds(pair * 128, 128)] = low(jnp.where(lane < HD, got[0], got[1]))


def put_halves(values, tile, upper, lower):
    half = values.shape[0] // 2
    upper[:, tile] = low(values[:half])
    lower[:, tile] = low(values[half:])


def of_halves(upper, lower, n, size=128):
    count = upper.shape[0] // size
    return wide((upper, lower)[n // count][pl.ds((n % count) * size, size), :])


def proj_kernel(pos, attended, near_a, far_a, near_b, far_b, fc1, proj, partial, upper, lower):
    core = pos[0]
    for part, chip, owner, block, n in join_parts(
        pos, (core, 1 - core), near_a, far_a, near_b, far_b
    ):
        here = pl.ds(n * 128, 128)
        row = pl.multiple_of((2 * chip + owner) * 128, 128)
        fc1[pl.ds(row, 128), :] = block[here, pl.ds(0, 2048)]
        row = pl.multiple_of(chip * 128, 128)
        proj[pl.ds(row, 128), pl.ds(part * 512, 512)] = block[here, pl.ds(2048, 512)]
    for tile in row_blocks(1024, 256):
        made = dot_of(attended[...], proj[:, tile], 1, 0)
        partial[:, tile] = made
        put_halves(made, tile, upper, lower)


def far_chips(pos):
    return (1 - pos[1], 3 - pos[1]), (2 * (1 - pos[2]), 2 * (1 - pos[2]) + 1)


def second_chips(pos):
    own = 2 * pos[2] + pos[1]
    over_y = 2 * (1 - pos[2]) + pos[1]
    over_x = 2 * pos[2] + 1 - pos[1]
    return ((own, pos[2]), (over_y, 1 - pos[2])), ((own, pos[1]), (over_x, 1 - pos[1]))


def chip_columns(ref, chip, count):
    return ref[:, pl.ds(pl.multiple_of(chip * count, count), count)]


def far_products(pos, left, right, outs):
    rows = left.shape[1] // 4
    cut = right.shape[1] // 2
    for part, chips in enumerate(far_chips(pos)):
        for n in range(2):
            made = dot_of(
                chip_columns(left, chips[n], rows), right[:, pl.ds(part * cut, cut)], 0, 0
            )
            outs[part][pl.ds(n * rows, rows), :] = low(made)


def middle_kernel(
    pos, inputs, partial, upper, lower, vectors, bias, gate, fc1, grad_out,
    hidden, branch, normed, slope, activated, grad_two, far_a, far_b,
):
    for n, rows in enumerate(row_blocks(inputs.shape[0])):
        made = partial[rows, :] + of_halves(upper, lower, n) + vectors[7:8, :]
        branch[rows, :] = made
        state = wide(inputs[rows, :]) + made * vectors[1:2, :] * gate[rows, :]
        hidden[rows, :] = state
        unit, _ = unit_of(state)
        normed[rows, :] = low(unit * vectors[2:3, :] + vectors[8:9, :])
        grad_two[rows, :] = low(wide(grad_out[rows, :]) * vectors[3:4, :] * gate[rows, :])

    def units(n, _):
        tile = pl.ds(pl.multiple_of(n * 256, 256), 256)
        pre = dot_of(normed[...], fc1[:, tile], 1, 0) + bias[:, tile]
        bell = 0.5 * (1.0 + lax.erf(pre * ROOT_HALF))
        activated[:, tile] = low(pre * bell)
        slope[:, tile] = bell + pre * jnp.exp(-0.5 * pre * pre) * INV_ROOT_TWO_PI
        return 0

    lax.fori_loop(0, 8, units, 0)
    far_products(pos, activated, grad_two, (far_a, far_b))


def units_back_kernel(
    pos, near_a, far_a, near_b, far_b, grad_two, slope, activated, normed, fc1,
    grad_pre, sums, partial, upper, lower, out_a, out_b, branch, branch_low, fc2,
):
    for part, chip, _, block, n in join_parts(pos, (0, 0), near_a, far_a, near_b, far_b):
        row = pl.multiple_of(chip * 512 + part * 256, 256)
        fc2[pl.ds(row, 256), :] = block[pl.ds(n * 256, 256), :]

    def units(n, _):
        tile = pl.ds(pl.multiple_of(n * 256, 256), 256)
        made = low(dot_of(grad_two[...], fc2[tile, :], 1, 1) * slope[:, tile])
        grad_pre[:, tile] = made
        sums[:, tile] = down(wide(made))
        return 0

    lax.fori_loop(0, 8, units, 0)
    for tile in row_blocks(1024, 256):
        made = dot_of(grad_pre[...], fc1[tile, :], 1, 1)
        partial[:, tile] = made
        put_halves(made, tile, upper, lower)
    far_products(pos, normed, grad_pre, (out_a, out_b))
    half = branch.shape[0]
    mine = pl.ds(pl.multiple_of(pos[0] * half, half), half)
    theirs = pl.ds(pl.multiple_of((1 - pos[0]) * half, half), half)
    for tile in row_blocks(1024, 256):
        branch[:, tile] = dot_of(activated[mine, :], fc2[:, tile], 1, 0)
        branch_low[:, tile] = low(dot_of(activated[theirs, :], fc2[:, tile], 1, 0))


def norm_back_kernel(
    pos, grad_out, partial, upper, lower, hidden, branch, vectors, gate, proj,
    grad_hidden, grad_one, grad_attended, sums,
):
    total = [0.0] * 4
    for n, rows in enumerate(row_blocks(hidden.shape[0])):
        grad = partial[rows, :] + of_halves(upper, lower, n)
        unit, inverse = unit_of(hidden[rows, :])
        state = wide(grad_out[rows, :]) + norm_back(grad, unit, inverse, vectors[2:3, :])
        grad_hidden[rows, :] = state
        gated = state * gate[rows, :]
        made = low(gated * vectors[1:2, :])
        grad_one[rows, :] = made
        terms = (gated * branch[rows, :], grad * unit, wide(made), grad)
        total = [one + down(term) for one, term in zip(total, terms)]
    for n in range(4):
        sums[n : n + 1, :] = total[n]
    grad_attended[...] = low(dot_of(grad_one[...], proj[...], 1, 1))


def fold_kernel(pos, left, right, got_a, got_b, keep_a, give_a, keep_b, give_b):
    rows = left.shape[1] // 4
    cut = right.shape[1] // 2
    outs = ((keep_a, give_a), (keep_b, give_b))
    for part, chips in enumerate(second_chips(pos)):
        for n in range(2):
            chip, arrived = chips[n]
            made = dot_of(chip_columns(left, chip, rows), right[:, pl.ds(part * cut, cut)], 0, 0)
            there = pl.ds(pl.multiple_of(arrived * rows, rows), rows)
            outs[part][n][...] = low(made + wide((got_a, got_b)[part][there, :]))


def pair_products(normed, attended, grad_qkv, grad_one, chip, part):
    first = dot_of(chip_columns(normed, chip, 256), grad_qkv[:, pl.ds(part * 768, 768)], 0, 0)
    second = dot_of(chip_columns(attended, chip, 128), grad_one[:, pl.ds(part * 512, 512)], 0, 0)
    return first, second[:, :256], second[:, 256:]


def attend_back_kernel(
    pos, qkv, mask, grad, normed, attended, grad_one, out, sums, far_a, far_b
):
    length = qkv.shape[0]
    lane = lax.broadcasted_iota(jnp.int32, (length, 128), 1)
    live = mask[...] > 0
    factor = HD ** (-0.5)
    for pair in range(4):
        spans = [pl.ds(offset + pair * 128, 128) for offset in (0, 512, 1024)]
        query, key, value = (qkv[:, span] for span in spans)
        grad_pair = grad[:, pl.ds(pair * 128, 128)]
        grad_query, grad_key, grad_value = [], 0.0, 0.0
        for head in range(2):
            chosen = (lane // HD) == head
            query_one = jnp.where(chosen, query, jnp.zeros_like(query))
            grad_head = jnp.where(chosen, grad_pair, jnp.zeros_like(grad_pair))
            scores = dot_of(key, query_one, 1, 1) * factor
            scores = jnp.where(live, scores, NEGATIVE)
            expo = jnp.exp(scores - jnp.max(scores, axis=0, keepdims=True))
            probs = expo * (1.0 / jnp.sum(expo, axis=0, keepdims=True))
            grad_probs = dot_of(value, grad_head, 1, 1)
            along = jnp.sum(grad_probs * probs, axis=0, keepdims=True)
            grad_scores = low(probs * (grad_probs - along))
            grad_value += dot_of(low(probs), grad_head, 1, 0)
            grad_key += dot_of(grad_scores, query_one, 1, 0)
            grad_query.append(dot_of(grad_scores, key, 0, 0))
        made = jnp.where(lane < HD, grad_query[0], grad_query[1]) * factor
        for span, item in zip(spans, (made, grad_key * factor, grad_value)):
            item = low(item)
            out[:, span] = item
            sums[:, span] = down(wide(item))
    for part, chips in enumerate(far_chips(pos)):
        for n in range(2):
            first, left, right = pair_products(normed, attended, out, grad_one, chips[n], part)
            target = (far_a, far_b)[part]
            target[pl.ds(n * 256, 256), pl.ds(0, 768)] = low(first)
            target[pl.ds(n * 256, 128), pl.ds(768, 256)] = low(left)
            target[pl.ds(n * 256 + 128, 128), pl.ds(768, 256)] = low(right)


def last_fold_kernel(
    pos, normed, attended, grad_qkv, grad_one, got_a, got_b, small, small_got,
    keep_a, give_a, keep_b, give_b,
):
    outs = ((keep_a, give_a), (keep_b, give_b))
    for part, chips in enumerate(second_chips(pos)):
        got = (got_a, got_b)[part]
        for n in range(2):
            chip, arrived = chips[n]
            first, left, right = pair_products(normed, attended, grad_qkv, grad_one, chip, part)
            top = pl.ds(pl.multiple_of(arrived * 256, 256), 256)
            upper = pl.ds(pl.multiple_of(arrived * 256, 256), 128)
            lower = pl.ds(pl.multiple_of(arrived * 256 + 128, 128), 128)
            side = pl.ds(768, 256)
            out = outs[part][n]
            out[pl.ds(0, 256), pl.ds(0, 768)] = low(first + wide(got[top, pl.ds(0, 768)]))
            out[pl.ds(0, 128), side] = low(left + wide(got[upper, side]))
            out[pl.ds(128, 128), side] = low(right + wide(got[lower, side]))
    for out, at_y in ((keep_a, pos[2]), (give_a, 1 - pos[2])):
        column = pl.multiple_of(at_y * 128, 128)
        sums = small[at_y] + wide(small_got[:, pl.ds(column, 128)])
        out[pl.ds(256, 32), :] = jnp.zeros((32, 1024), jnp.bfloat16)
        out[pl.ds(256, 16), pl.ds(0, 128)] = low(sums)


def first_back_kernel(pos, grad_qkv, weight, last, partial, upper, lower):
    half = lower.shape[0]
    for tile in row_blocks(1024, 256):
        made = dot_of(grad_qkv[...], weight[tile, :], 1, 1)
        partial[:, tile] = made
        upper[pl.ds(0, half), tile] = low(made[:half])
        lower[:, tile] = low(made[half:])
    upper[pl.ds(half, 16), :] = low(jnp.broadcast_to(last[0:1, :], (16, 1024)))


def inputs_back_kernel(
    pos, inputs, partial, upper, lower, grad_hidden, vectors, out, sums, grads
):
    total = [0.0] * 2
    half = out.shape[0]
    for n, rows in enumerate(row_blocks(2 * half)):
        there = (upper, lower)[n * 128 // half]
        grad = partial[rows, :] + wide(there[pl.ds((n * 128) % half, 128), :])
        grads[rows, :] = grad
        unit, _ = unit_of(wide(inputs[rows, :]))
        total = [one + down(term) for one, term in zip(total, (grad * unit, grad))]
    for n in range(2):
        sums[n : n + 1, :] = total[n]
    sums[2:3, :] = wide(upper[pl.ds(half, 16), :])[0:1]
    for n in range(half // 128):
        rows = pl.ds(pl.multiple_of(pos[0] * half + n * 128, 128), 128)
        unit, inverse = unit_of(wide(inputs[rows, :]))
        state = grad_hidden[rows, :] + norm_back(grads[rows, :], unit, inverse, vectors[0:1, :])
        out[pl.ds(n * 128, 128), :] = low(state)


def output_kernel(
    pos, hidden, branch, other, vectors, gate, grad_out, grad_two, out, sums
):
    half = out.shape[0]
    gain_sum, shift_sum = 0.0, 0.0
    for n in range(half // 128):
        here = pl.ds(n * 128, 128)
        rows = pl.ds(pl.multiple_of(pos[0] * half + n * 128, 128), 128)
        made = branch[here, :] + wide(other[here, :]) + vectors[9:10, :]
        out[here, :] = low(hidden[rows, :] + made * vectors[3:4, :] * gate[rows, :])
        gain_sum += down(wide(grad_out[rows, :]) * gate[rows, :] * made)
    for rows in row_blocks(2 * half):
        shift_sum += down(wide(grad_two[rows, :]))
    sums[0:1, :] = gain_sum
    sums[1:2, :] = shift_sum


def small_kernel(pos, first, second, last, attention, units, keep, give):
    core = pos[0]
    order = [(first, 0), (second, 0), (second, 1), (last, 0), (first, 1)]
    order += [None, None, (second, 2), (second, 3), (last, 1)]
    give[...] = jnp.zeros_like(give)
    for at_y in range(2):
        for over in range(2):
            chip = 2 * at_y + (pos[1] if over == 0 else 1 - pos[1])
            own = pl.ds(pl.multiple_of((2 * chip + core) * 128, 128), 128)
            here = pl.multiple_of(chip * 128, 128)
            lines = [None if item is None else item[0][item[1] : item[1] + 1, own] for item in order]
            lines[3] = lines[3] + first[2:3, own]
            lines[5] = attention[:, pl.ds(here, 128)]
            lines[6] = attention[:, pl.ds(pl.multiple_of(1024 + chip * 128, 128), 128)]
            for j in range(4):
                column = pl.multiple_of(chip * 512 + j * 128, 128)
                lines.append(units[:, pl.ds(column, 128)])
            block = jnp.concatenate(lines + [jnp.zeros((2, 128), jnp.float32)], axis=0)
            if over == 0:
                keep[at_y, :, :] = block
            else:
                give[:, pl.ds(at_y * 128, 128)] = low(block)


def finish_qkv_kernel(pos, mine, theirs, out):
    core = pos[0]
    rows = pl.ds(pl.multiple_of(core * 128, 128), 128)
    for j in range(12):
        here = pl.ds(j * 128, 128)
        out[:, pl.ds(pl.multiple_of((2 * j + core) * 128, 128), 128)] = wide(mine[rows, here])
        out[:, pl.ds(pl.multiple_of((2 * j + 1 - core) * 128, 128), 128)] = wide(theirs[:, here])


def finish_fc1_kernel(pos, mine, theirs, out):
    core = pos[0]
    rows = pl.ds(pl.multiple_of(core * 128, 128), 128)
    for j in range(4):
        here = pl.ds(j * 512, 512)
        out[:, pl.ds(pl.multiple_of((2 * j + core) * 512, 512), 512)] = wide(mine[rows, here])
        out[:, pl.ds(pl.multiple_of((2 * j + 1 - core) * 512, 512), 512)] = wide(theirs[:, here])


def add_low(one, two):
    return (one.astype(jnp.float32) + two.astype(jnp.float32)).astype(jnp.bfloat16)


def line_in(values):
    return lax.ppermute(values, "seq", [(0, 1), (3, 2)])


def line_mid(values):
    return lax.ppermute(values, "seq", [(1, 2), (2, 1)])


def line_out(values):
    return lax.ppermute(values, "seq", [(1, 0), (2, 3)])


def inner():
    at_z = lax.axis_index("seq")
    return ((at_z == 1) | (at_z == 2)).astype(jnp.int32)


def image_moves(back):
    seq = lax.axis_size("seq")
    rounds = []
    for turn in range(2):
        moves = []
        for chip in range(lax.axis_size("dp") // 2):
            for core in range(2):
                for quarter in range(seq):
                    slot = (quarter + turn) % 2
                    source = (2 * chip + core) * seq + quarter
                    target = (2 * chip + quarter // 2) * seq + 2 * core + slot
                    moves.append((target, source) if back else (source, target))
        rounds.append(moves)
    return rounds


def to_images(first, second, *earlier):
    at_z = lax.axis_index("seq")
    first, second = after((first, second), *earlier)
    got = []
    for turn, moves in enumerate(image_moves(False)):
        slot = (at_z + turn) % 2
        sent = [lax.dynamic_index_in_dim(item, slot, 0, False) for item in (first, second)]
        got.append(lax.ppermute(jnp.concatenate(sent, axis=0), ("dp", "seq"), moves))
    return jnp.concatenate(got, axis=0)


def from_images(values):
    at_z = lax.axis_index("seq")
    pieces = values.reshape(2, values.shape[0] // 2, values.shape[1])
    got = []
    for turn, moves in enumerate(image_moves(True)):
        sent = lax.dynamic_index_in_dim(pieces, (at_z + turn) % 2, 0, False)
        got.append(lax.ppermute(sent, ("dp", "seq"), moves))
    return got


def slots_of(got):
    even = lax.axis_index("seq") % 2 == 0
    return jnp.stack([jnp.where(even, got[0], got[1]), jnp.where(even, got[1], got[0])])


def image_plan(
    tokens, group_count, pad_mask, w_qkv, w_proj, w_fc1, w_fc2, fc1_bias, scales, shifts, cotangent
):
    slot_count, _, width = tokens.shape
    length = pad_mask.shape[1]
    half = length // 2
    f32, bf16 = jnp.float32, jnp.bfloat16
    core, at_x, at_y = place()
    at_z = lax.axis_index("seq")
    pos = jnp.stack([core, at_x, at_y, at_z]).astype(jnp.int32)

    alive = jnp.arange(slot_count, dtype=jnp.int32) < group_count[0]
    mask_own = jnp.where(alive[:, None], pad_mask, 0).astype(f32)
    mine, give = local_call(
        cut_kernel, [((128, 4224), bf16), ((128, 3840), bf16)],
        pos, w_qkv, w_fc1, w_proj, scales, shifts, fc1_bias.reshape(4, 128), mask_own, room=12,
    )
    got = swap(give, CORE)
    blocks = (mine, jnp.concatenate([got[:, :3712], w_proj[:, 512:]], axis=1))
    mask_both = joined(
        mask_own,
        got[:8, 3712:].reshape(4, slot_count, 128).transpose(1, 0, 2).reshape(
            slot_count, length
        ).astype(f32),
        core, 0,
    )
    mask_row = lax.dynamic_index_in_dim(mask_both, at_z, 0, False)
    token_gate = mask_row[:, None]

    def links(sent, order=(ALONG_X, ALONG_Y)):
        return swap(sent[0], order[0]), swap(sent[1], order[1])

    def second_link(blocks, got):
        near_a, near_b = (jnp.concatenate(pair, axis=0) for pair in zip(blocks, got))
        far_a, far_b = links((near_a, near_b), (ALONG_Y, ALONG_X))
        return near_a, far_a, near_b, far_b

    def lanes(pair, start, stop):
        return [item[:, start:stop] for item in pair]

    first = links(blocks)
    both = to_images(tokens, cotangent, blocks[1])
    qkv_parts = second_link(lanes(blocks, 0, 1664), lanes(first, 0, 1664))
    first = after(first, qkv_parts[0], qkv_parts[2])
    fc1_parts = second_link(lanes(blocks, 1664, 4224), lanes(first, 1664, 4224))
    fc2_blocks = after((w_fc2[:256], w_fc2[256:]), fc1_parts[0], fc1_parts[2])
    fc2_first = links(fc2_blocks)

    full = (length, width)
    qkv_w, vectors, bias, inputs, grad_out, normed_one, qkv, attended = local_call(
        front_kernel,
        [
            ((width, 1536), bf16), ((16, width), f32), ((1, 2048), f32), (full, bf16),
            (full, bf16), (full, bf16), ((length, 1536), bf16), ((length, 512), bf16),
        ],
        pos, both, swap(both, CORE), *after(qkv_parts, *fc2_blocks),
        mask_row[None, :], room=24,
    )
    halves = [((half, width), bf16)] * 2
    fc1_w, proj_w, partial, upper, lower = local_call(
        proj_kernel,
        [((width, 2048), bf16), ((512, width), bf16), (full, f32)] + halves,
        pos, attended, *fc1_parts, room=20,
    )
    fc2_parts = second_link(fc2_blocks, after(fc2_first, upper, lower))
    hidden, branch_one, normed_two, slope, activated, grad_two, far_a, far_b = local_call(
        middle_kernel,
        [
            (full, f32), (full, f32), (full, bf16), ((length, 2048), f32),
            ((length, 2048), bf16), (full, bf16), ((1024, 512), bf16), ((1024, 512), bf16),
        ],
        pos, inputs, partial, swap(upper, CORE), swap(lower, CORE), vectors, bias, token_gate,
        fc1_w, after(grad_out, fc2_parts[0], fc2_parts[2]), room=28,
    )

    def fold(left, right, got, *earlier):
        block = (left.shape[1] // 4, right.shape[1] // 2)
        got_a, got_b = after(got, *earlier)
        keep_a, give_a, keep_b, give_b = local_call(
            fold_kernel, [(block, bf16)] * 4, pos, left, right, got_a, got_b, room=14,
    )
        return (keep_a, keep_b), (give_a, give_b)

    def half_of(keep, got):
        return [add_low(one, two) for one, two in zip(keep, got)]

    fc2_got = links((far_a, far_b))
    grad_pre, unit_sums, partial, upper, lower, far_a, far_b, branch_two, branch_low = local_call(
        units_back_kernel,
        [((length, 2048), bf16), ((1, 2048), f32), (full, f32)]
        + halves
        + [((512, 1024), bf16), ((512, 1024), bf16), ((half, width), f32), ((half, width), bf16)],
        pos, *fc2_parts, grad_two, slope, activated, normed_two, fc1_w,
        scratch=[((2048, width), bf16)],
    )
    others = [swap(item, CORE) for item in (upper, lower)]
    branch_other = swap(branch_low, CORE)
    output, last_sums = local_call(
        output_kernel, [((half, width), bf16), ((2, width), f32)],
        pos, hidden, branch_two, branch_other, vectors, token_gate, grad_out,
        grad_two, room=14,
    )
    out_got = from_images(output)
    grad_hidden, grad_one, grad_attended, second_sums = local_call(
        norm_back_kernel, [(full, f32), (full, bf16), ((length, 512), bf16), ((4, width), f32)],
        pos, grad_out, partial, *after(others, output), hidden, branch_one, vectors, token_gate,
        proj_w, room=20,
    )
    fc2_keep, fc2_give = fold(activated, grad_two, fc2_got, grad_attended, *out_got)
    fc2_again = links(fc2_give, (ALONG_Y, ALONG_X))
    fc1_got = links(after((far_a, far_b), *fc2_give))
    grad_qkv_rows, attention_sums, far_a, far_b = local_call(
        attend_back_kernel,
        [
            ((length, 1536), bf16), ((1, 1536), f32), ((512, 1024), bf16), ((512, 1024), bf16),
        ],
        pos, after(qkv, *fc2_give), token_gate, grad_attended, normed_one, attended, grad_one, room=24,
    )
    fc2_half = jnp.concatenate(half_of(fc2_keep, after(fc2_again, grad_qkv_rows)), axis=1)
    fc2_in = line_in(fc2_half)
    partial, upper, lower = local_call(
        first_back_kernel, [(full, f32), ((half + 16, width), bf16), ((half, width), bf16)],
        pos, after(grad_qkv_rows, fc2_half), qkv_w, last_sums, room=16,
    )
    grad_input, first_sums = local_call(
        inputs_back_kernel, [((half, width), bf16), ((3, width), f32)],
        pos, inputs, partial, swap(upper, CORE), swap(lower, CORE), grad_hidden, vectors,
        scratch=[(full, f32)], room=16,
    )
    in_got = from_images(grad_input)
    small_keep, small_give = local_call(
        small_kernel, [((2, 16, 128), f32), ((16, 1024), bf16)],
        pos, first_sums, second_sums, last_sums, attention_sums, unit_sums, room=6,
    )
    fc1_keep, fc1_give = fold(normed_two, grad_pre, fc1_got, small_give)
    fc1_give = (fc1_give[0], jnp.concatenate([fc1_give[1], small_give], axis=0))
    fc1_again = links(fc1_give, (ALONG_Y, ALONG_X))
    last_got = links(after((far_a, far_b), *fc1_give))
    fc2_sum = add_low(fc2_half, after(fc2_in, *fc1_give, *in_got))
    fc2_mid = line_mid(fc2_sum)

    small_got = fc1_again[1][256:]
    fc1_again = (fc1_again[0], fc1_again[1][:256])
    fc1_half = half_of(fc1_keep, after(fc1_again, fc2_sum))
    fc1_in = [line_in(item) for item in fc1_half]
    fc2_total = add_low(fc2_sum, after(fc2_mid, *fc1_half))
    fc2_out = line_out(fc2_total)
    fc1_sum, fc1_mid, fc1_total, fc1_out = [None] * 2, [None] * 2, [None] * 2, [None] * 2
    fc1_sum[0] = add_low(fc1_half[0], after(fc1_in[0], fc2_total))
    fc1_mid[0] = line_mid(fc1_sum[0])
    last_got = after(last_got, fc1_sum[0])
    wide_block, block = ((288, 1024), bf16), ((256, 1024), bf16)
    keep_a, give_a, keep_b, give_b = local_call(
        last_fold_kernel, [wide_block, wide_block, block, block],
        pos, normed_one, attended, grad_qkv_rows, grad_one, *last_got, small_keep, small_got, room=16,
    )
    last_again = links((give_a, give_b), (ALONG_Y, ALONG_X))
    fc1_sum[1] = add_low(fc1_half[1], after(fc1_in[1], give_a, give_b))
    fc1_mid[1] = line_mid(fc1_sum[1])
    fc1_total[0] = add_low(fc1_sum[0], after(fc1_mid[0], fc1_sum[1]))
    fc1_out[0] = line_out(fc1_total[0])
    last_half = half_of((keep_a, keep_b), after(last_again, fc1_total[0]))
    last_in = [line_in(item) for item in last_half]

    def line_end(total, out):
        return jnp.where(inner() == 1, total, out)

    def core_give(values):
        return lax.dynamic_slice_in_dim(values, (1 - core) * 128, 128, 0)

    fc1_total[1] = add_low(fc1_sum[1], after(fc1_mid[1], *last_half))
    fc1_out[1] = line_out(fc1_total[1])
    grad_fc2 = line_end(fc2_total, after(fc2_out, fc1_total[1])).astype(f32)
    last_sum, last_mid, last_total, last_out = [None] * 2, [None] * 2, [None] * 2, [None] * 2
    arrived, fc1_out[0] = after((last_in[1], fc1_out[0]), grad_fc2)
    last_sum[1] = add_low(last_half[1], arrived)
    last_mid[1] = line_mid(last_sum[1])
    arrived, fc1_out[1] = after((last_in[0], fc1_out[1]), last_sum[1])
    last_sum[0] = add_low(last_half[0], arrived)
    last_mid[0] = line_mid(last_sum[0])
    last_total[1] = add_low(last_sum[1], after(last_mid[1], last_sum[0]))
    last_out[1] = line_out(last_total[1])
    fc1_rows = [line_end(*pair) for pair in zip(fc1_total, after(fc1_out, last_total[1]))]
    fc1_rows = jnp.concatenate(fc1_rows, axis=1)
    last_total[0] = add_low(last_sum[0], after(last_mid[0], fc1_rows))
    last_out[0] = line_out(last_total[0])
    (grad_fc1,) = local_call(
        finish_fc1_kernel, [((128, 4096), f32)],
        pos, fc1_rows, after(swap(core_give(fc1_rows), CORE), last_total[0]), room=10,
    )
    last_out = after(last_out, grad_fc1)
    last_rows = [line_end(*pair) for pair in zip(last_total, last_out)]
    small = last_rows[0][256:272, :128].astype(f32)
    qkv_rows = jnp.concatenate([last_rows[0][:256, :768], last_rows[1][:, :768]], axis=1)
    qkv_core = swap(core_give(qkv_rows), CORE)
    grad_proj = jnp.concatenate(
        [part[rows : rows + 128, 768:] for part in last_rows for rows in (0, 128)], axis=1
    ).astype(f32)
    (grad_qkv,) = local_call(
        finish_qkv_kernel, [((128, 3072), f32)], pos, qkv_rows, qkv_core, room=10
    )
    grad_scales = small[:4]
    grad_shifts = small[4:10]
    grad_bias = small[10:14].reshape(512)
    return (
        slots_of(out_got),
        slots_of(in_got),
        grad_qkv,
        grad_proj,
        grad_fc1,
        grad_fc2,
        grad_bias,
        grad_scales,
        grad_shifts,
    )


def on_device(*arrays):
    tokens = arrays[0]
    whole_images = 2 * tokens.shape[0] == lax.axis_size("seq")
    if lax.axis_size("dp") == 8 and lax.axis_size("seq") == 4 and whole_images:
        return image_plan(*arrays)
    return general_plan(*arrays)


def solution(mesh):
    return jax.shard_map(
        on_device,
        mesh=mesh,
        in_specs=(
            P("dp", "seq", None),
            P("dp"),
            P("dp", None),
            P("dp", None),
            P("dp", None),
            P("dp", None),
            P("dp", None),
            P("dp"),
            P(None, "dp"),
            P(None, "dp"),
            P("dp", "seq", None),
        ),
        out_specs=(
            P("dp", "seq", None),
            P("dp", "seq", None),
            P("dp", None),
            P("dp", None),
            P("dp", None),
            P("dp", None),
            P("dp"),
            P(None, "dp"),
            P(None, "dp"),
        ),
        check_vma=False,
    )
```

```python
import jax
import jax.numpy as jnp
from jax import lax
from jax.experimental import pallas as pl
from jax.experimental.pallas import tpu as pltpu
from jax.sharding import PartitionSpec as P

HD = 64


EPSILON = 1e-06
ROOT_HALF = 0.7071067811865476
INV_ROOT_TWO_PI = 0.3989422804014327


def layer_norm(values, gain, shift):
    mean_row = jnp.mean(values, axis=-1, keepdims=True)
    centred = values - mean_row
    inverse = lax.rsqrt(jnp.mean(centred * centred, axis=-1, keepdims=True) + EPSILON)
    unit_rows = centred * inverse
    return (unit_rows * gain + shift, unit_rows, inverse)


def norm_back(grad_normed, unit_rows, inverse, gain):
    scaled = grad_normed * gain
    centre = jnp.mean(scaled, axis=-1, keepdims=True)
    along = jnp.mean(scaled * unit_rows, axis=-1, keepdims=True)
    return inverse * (scaled - centre - unit_rows * along)


def gelu_exact(values):
    return 0.5 * values * (1.0 + lax.erf(values * ROOT_HALF))


def gelu_slope(values):
    return (
        0.5 * (1.0 + lax.erf(values * ROOT_HALF))
        + values * jnp.exp(-0.5 * values * values) * INV_ROOT_TWO_PI
    )


def token_sum(values):
    return jnp.sum(values, axis=(0, 1))


def general_plan(
    tokens, group_count, pad_mask, w_qkv, w_proj, w_fc1, w_fc2, fc1_bias, scales, shifts, cotangent
):
    slot_count, piece, width = tokens.shape
    seq_total = pad_mask.shape[1]
    part_width = width // lax.axis_size("seq")
    head_count = part_width // HD
    factor = HD ** (-0.5)
    alive = jnp.arange(slot_count, dtype=jnp.int32) < group_count[0]
    key_mask = jnp.where(alive[:, None], pad_mask, 0).astype(jnp.float32)
    query_mask = lax.dynamic_slice_in_dim(key_mask, lax.axis_index("seq") * piece, piece, 1)[
        :, :, None
    ]
    full_qkv, full_proj, full_fc1, full_fc2, full_bias, full_scales, full_shifts = (
        lax.all_gather(w_qkv, "dp", axis=0, tiled=True),
        lax.all_gather(w_proj, "dp", axis=0, tiled=True),
        lax.all_gather(w_fc1, "dp", axis=0, tiled=True),
        lax.all_gather(w_fc2, "dp", axis=0, tiled=True),
        lax.all_gather(fc1_bias, "dp", axis=0, tiled=True),
        lax.all_gather(scales, "dp", axis=1, tiled=True),
        lax.all_gather(shifts, "dp", axis=1, tiled=True),
    )
    gains = full_scales.astype(jnp.float32)
    offsets = full_shifts.astype(jnp.float32)
    hidden_bias = full_bias.astype(jnp.float32)
    inputs = tokens.astype(jnp.float32)
    normed_one, unit_one, inverse_one = layer_norm(inputs, gains[0], offsets[0])
    normed_one = normed_one.astype(jnp.bfloat16)
    projected = jnp.dot(normed_one, full_qkv, preferred_element_type=jnp.float32)
    queries = (projected[:, :, :width] + offsets[1]).astype(jnp.bfloat16)
    key_rows = projected[:, :, width : 2 * width].astype(jnp.bfloat16)
    value_rows = (projected[:, :, 2 * width :] + offsets[2]).astype(jnp.bfloat16)
    head_query, head_key, head_value = (
        lax.all_to_all(queries, "seq", split_axis=2, concat_axis=1, tiled=True),
        lax.all_to_all(key_rows, "seq", split_axis=2, concat_axis=1, tiled=True),
        lax.all_to_all(value_rows, "seq", split_axis=2, concat_axis=1, tiled=True),
    )
    head_shape = (slot_count, seq_total, head_count, HD)
    query_heads = head_query.reshape(head_shape)
    key_heads = head_key.reshape(head_shape)
    value_heads = head_value.reshape(head_shape)

    def scores_of():
        raw = (
            jnp.einsum(
                "bqhe,bkhe->bhqk", query_heads, key_heads, preferred_element_type=jnp.float32
            )
            * factor
        )
        return jnp.where(key_mask[:, None, None, :] > 0, raw, -1e30)

    scores = scores_of()
    top = jnp.max(scores, axis=-1, keepdims=True)
    log_total = top + jnp.log(jnp.sum(jnp.exp(scores - top), axis=-1, keepdims=True))
    probs_low = jnp.exp(scores - log_total).astype(jnp.bfloat16)
    attended = jnp.einsum(
        "bhqk,bkhe->bqhe", probs_low, value_heads, preferred_element_type=jnp.float32
    )
    attended = attended.astype(jnp.bfloat16).reshape(slot_count, seq_total, part_width)
    mixed = lax.all_to_all(attended, "seq", split_axis=1, concat_axis=2, tiled=True)
    branch_one = jnp.dot(mixed, full_proj, preferred_element_type=jnp.float32) + offsets[3]
    hidden_state = inputs + branch_one * gains[1] * query_mask
    normed_two, unit_two, inverse_two = layer_norm(hidden_state, gains[2], offsets[4])
    normed_two = normed_two.astype(jnp.bfloat16)
    pre_act = jnp.dot(normed_two, full_fc1, preferred_element_type=jnp.float32) + hidden_bias
    activated = gelu_exact(pre_act).astype(jnp.bfloat16)
    branch_two = jnp.dot(activated, full_fc2, preferred_element_type=jnp.float32) + offsets[5]
    output = (hidden_state + branch_two * gains[3] * query_mask).astype(jnp.bfloat16)
    back_qkv, back_proj, back_fc1, back_fc2, back_gains = (
        full_qkv,
        full_proj,
        full_fc1,
        full_fc2,
        gains,
    )
    grad_out = cotangent.astype(jnp.float32)
    layer_gain_two = token_sum(grad_out * query_mask * branch_two)
    grad_branch_two = (grad_out * back_gains[3] * query_mask).astype(jnp.bfloat16)
    shift_five = token_sum(grad_branch_two.astype(jnp.float32))
    grad_fc2 = jnp.einsum(
        "spf,spd->fd", activated, grad_branch_two, preferred_element_type=jnp.float32
    )
    grad_act = jnp.einsum(
        "spd,fd->spf", grad_branch_two, back_fc2, preferred_element_type=jnp.float32
    )
    grad_pre = (grad_act * gelu_slope(pre_act)).astype(jnp.bfloat16)
    grad_hidden_bias = token_sum(grad_pre.astype(jnp.float32))
    grad_fc1 = jnp.einsum("spd,spf->df", normed_two, grad_pre, preferred_element_type=jnp.float32)
    grad_normed_two = jnp.einsum(
        "spf,df->spd", grad_pre, back_fc1, preferred_element_type=jnp.float32
    )
    norm_gain_two = token_sum(grad_normed_two * unit_two)
    norm_shift_two = token_sum(grad_normed_two)
    grad_hidden = grad_out + norm_back(grad_normed_two, unit_two, inverse_two, back_gains[2])
    layer_gain_one = token_sum(grad_hidden * query_mask * branch_one)
    grad_branch_one = (grad_hidden * back_gains[1] * query_mask).astype(jnp.bfloat16)
    shift_proj = token_sum(grad_branch_one.astype(jnp.float32))
    grad_proj = jnp.einsum(
        "spd,spe->de", mixed, grad_branch_one, preferred_element_type=jnp.float32
    )
    grad_mixed = jnp.einsum(
        "spe,de->spd", grad_branch_one, back_proj, preferred_element_type=jnp.float32
    )
    grad_mixed = grad_mixed.astype(jnp.bfloat16)
    grad_attended = lax.all_to_all(
        grad_mixed, "seq", split_axis=2, concat_axis=1, tiled=True
    ).reshape(head_shape)
    probs = jnp.exp(scores_of() - log_total)
    probs_again = probs.astype(jnp.bfloat16)
    grad_probs = jnp.einsum(
        "bqhe,bkhe->bhqk", grad_attended, value_heads, preferred_element_type=jnp.float32
    )
    row_dot = jnp.sum(grad_probs * probs, axis=-1, keepdims=True)
    grad_scores = (probs * (grad_probs - row_dot)).astype(jnp.bfloat16)
    flat_shape = (slot_count, seq_total, part_width)
    grad_query = (
        jnp.einsum("bhqk,bkhe->bqhe", grad_scores, key_heads, preferred_element_type=jnp.float32)
        * factor
    )
    grad_key = (
        jnp.einsum("bhqk,bqhe->bkhe", grad_scores, query_heads, preferred_element_type=jnp.float32)
        * factor
    )
    grad_value = jnp.einsum(
        "bhqk,bqhe->bkhe", probs_again, grad_attended, preferred_element_type=jnp.float32
    )
    grad_query = grad_query.astype(jnp.bfloat16).reshape(flat_shape)
    grad_key = grad_key.astype(jnp.bfloat16).reshape(flat_shape)
    grad_value = grad_value.astype(jnp.bfloat16).reshape(flat_shape)
    token_query, token_key, token_value = (
        lax.all_to_all(grad_query, "seq", split_axis=1, concat_axis=2, tiled=True),
        lax.all_to_all(grad_key, "seq", split_axis=1, concat_axis=2, tiled=True),
        lax.all_to_all(grad_value, "seq", split_axis=1, concat_axis=2, tiled=True),
    )
    grad_joined = jnp.concatenate([token_query, token_key, token_value], axis=2)
    grad_qkv = jnp.einsum(
        "spd,spe->de", normed_one, grad_joined, preferred_element_type=jnp.float32
    )
    grad_normed_one = jnp.einsum(
        "spe,de->spd", grad_joined, back_qkv, preferred_element_type=jnp.float32
    )
    norm_gain_one = token_sum(grad_normed_one * unit_one)
    norm_shift_one = token_sum(grad_normed_one)
    grad_input = (
        grad_hidden + norm_back(grad_normed_one, unit_one, inverse_one, back_gains[0])
    ).astype(jnp.bfloat16)
    gain_terms = jnp.stack([norm_gain_one, layer_gain_one, norm_gain_two, layer_gain_two])
    shift_terms = jnp.stack(
        [
            norm_shift_one,
            token_sum(token_query.astype(jnp.float32)),
            token_sum(token_value.astype(jnp.float32)),
            shift_proj,
            norm_shift_two,
            shift_five,
        ]
    )
    shares = (
        lax.psum_scatter(
            grad_qkv.astype(jnp.bfloat16), "dp", scatter_dimension=0, tiled=True
        ).astype(jnp.float32),
        lax.psum_scatter(
            grad_proj.astype(jnp.bfloat16), "dp", scatter_dimension=0, tiled=True
        ).astype(jnp.float32),
        lax.psum_scatter(
            grad_fc1.astype(jnp.bfloat16), "dp", scatter_dimension=0, tiled=True
        ).astype(jnp.float32),
        lax.psum_scatter(
            grad_fc2.astype(jnp.bfloat16), "dp", scatter_dimension=0, tiled=True
        ).astype(jnp.float32),
        lax.psum_scatter(
            grad_hidden_bias.astype(jnp.bfloat16), "dp", scatter_dimension=0, tiled=True
        ).astype(jnp.float32),
        lax.psum_scatter(
            gain_terms.astype(jnp.bfloat16), "dp", scatter_dimension=1, tiled=True
        ).astype(jnp.float32),
        lax.psum_scatter(
            shift_terms.astype(jnp.bfloat16), "dp", scatter_dimension=1, tiled=True
        ).astype(jnp.float32),
    )
    totals = (
        lax.psum(shares[0].astype(jnp.bfloat16), "seq").astype(jnp.float32),
        lax.psum(shares[1].astype(jnp.bfloat16), "seq").astype(jnp.float32),
        lax.psum(shares[2].astype(jnp.bfloat16), "seq").astype(jnp.float32),
        lax.psum(shares[3].astype(jnp.bfloat16), "seq").astype(jnp.float32),
        lax.psum(shares[4].astype(jnp.bfloat16), "seq").astype(jnp.float32),
        lax.psum(shares[5].astype(jnp.bfloat16), "seq").astype(jnp.float32),
        lax.psum(shares[6].astype(jnp.bfloat16), "seq").astype(jnp.float32),
    )
    return (
        output,
        grad_input,
        totals[0],
        totals[1],
        totals[2],
        totals[3],
        totals[4],
        totals[5],
        totals[6],
    )


CORE, ALONG_X, ALONG_Y = 1, 2, 4
NEGATIVE = -1e30


def swap(values, bit):
    size = lax.axis_size("dp")
    return lax.ppermute(values, "dp", [(i, i ^ bit) for i in range(size)])


def after(values, *earlier):
    return lax.optimization_barrier((values, earlier))[0]


def place():
    index = lax.axis_index("dp")
    return index % 2, (index // 2) % 2, index // 4


def joined(mine, theirs, bit, axis):
    low = jnp.where(bit == 0, mine, theirs)
    high = jnp.where(bit == 0, theirs, mine)
    return jnp.concatenate([low, high], axis=axis)


def local_call(kernel, outs, position, *arrays, scratch=(), room=40, outside=(), copies=0):
    return pl.pallas_call(
        kernel,
        out_shape=[jax.ShapeDtypeStruct(shape, kind) for shape, kind in outs],
        in_specs=[pl.BlockSpec(memory_space=pltpu.SMEM)]
        + [
            pl.BlockSpec(memory_space=pl.ANY if n in outside else pltpu.VMEM)
            for n in range(len(arrays))
        ],
        out_specs=[pl.BlockSpec(memory_space=pltpu.VMEM)] * len(outs),
        scratch_shapes=[pltpu.VMEM(shape, kind) for shape, kind in scratch]
        + [pltpu.SemaphoreType.DMA((copies,))] * (copies > 0),
        compiler_params=pltpu.CompilerParams(vmem_limit_bytes=room * 1024 * 1024),
        cost_estimate=pl.CostEstimate(flops=1 << 20, bytes_accessed=1 << 16, transcendentals=0),
    )(position, *arrays)


def cut_kernel(pos, qkv, fc1, proj, scales, shifts, bias, mask, mine, give):
    core = pos[0]
    for j in range(12):
        here = pl.ds(j * 128, 128)
        mine[:, here] = qkv[:, pl.ds(pl.multiple_of((2 * j + core) * 128, 128), 128)]
        give[:, here] = qkv[:, pl.ds(pl.multiple_of((2 * j + 1 - core) * 128, 128), 128)]
    for j in range(4):
        here = pl.ds(1664 + j * 512, 512)
        mine[:, here] = fc1[:, pl.ds(pl.multiple_of((2 * j + core) * 512, 512), 512)]
        give[:, here] = fc1[:, pl.ds(pl.multiple_of((2 * j + 1 - core) * 512, 512), 512)]
    mine[:, pl.ds(3712, 512)] = proj[:, pl.ds(0, 512)]
    wide = [item[...].astype(jnp.float32) for item in (scales, shifts, bias)]
    small = jnp.concatenate(wide + [jnp.zeros((114, 128), jnp.float32)], axis=0)
    masks = [mask[:, j * 128 : j * 128 + 128] for j in range(mask.shape[1] // 128)]
    masks = jnp.concatenate(masks + [jnp.zeros((120, 128), jnp.float32)], axis=0)
    mine[:, pl.ds(1536, 128)] = small.astype(jnp.bfloat16)
    give[:, pl.ds(1536, 128)] = small.astype(jnp.bfloat16)
    give[:, pl.ds(3712, 128)] = masks.astype(jnp.bfloat16)


def chips_of(pos):
    chip = 2 * pos[2] + pos[1]
    along_x = 2 * pos[2] + 1 - pos[1]
    along_y = 2 * (1 - pos[2]) + pos[1]
    across = 2 * (1 - pos[2]) + 1 - pos[1]
    return (chip, along_x, along_y, across), (chip, along_y, along_x, across)


def dot_of(left, right, left_dim, right_dim):
    return lax.dot_general(
        left, right, (((left_dim,), (right_dim,)), ((), ())), preferred_element_type=jnp.float32
    )


def low(values):
    return values.astype(jnp.bfloat16)


def wide(values):
    return values.astype(jnp.float32)


def down(values):
    return jnp.sum(values, axis=0, keepdims=True)


def unit_of(values):
    centred = values - jnp.mean(values, axis=1, keepdims=True)
    inverse = lax.rsqrt(jnp.mean(centred * centred, axis=1, keepdims=True) + EPSILON)
    return centred * inverse, inverse


def row_blocks(count, size=128):
    return [pl.ds(n * size, size) for n in range(count // size)]


def join_parts(pos, owners, near_a, far_a, near_b, far_b):
    for part, chips, near, far in zip((0, 1), chips_of(pos), (near_a, near_b), (far_a, far_b)):
        for n in range(4):
            yield part, chips[n], owners[part], (near, far)[n // 2], n % 2


def front_kernel(
    pos, mine, theirs, near_a, far_a, near_b, far_b, mask, gate,
    weight, vectors, bias, inputs, grad_out, grad_two, normed, qkv, attended,
):
    core = pos[0]
    for part, chip, owner, block, n in join_parts(
        pos, (core, 1 - core), near_a, far_a, near_b, far_b
    ):
        row = pl.multiple_of((2 * chip + owner) * 128, 128)
        weight[pl.ds(row, 128), :] = block[pl.ds(n * 128, 128), pl.ds(0, 1536)]
        small = wide(block[pl.ds(n * 128, 16), pl.ds(1536, 128)])
        vectors[:, pl.ds(row, 128)] = small
        if part == 0:
            for j in range(4):
                column = pl.multiple_of(chip * 512 + j * 128, 128)
                bias[:, pl.ds(column, 128)] = small[10 + j : 11 + j]
    half = mine.shape[0] // 2
    piece = half // 2
    for there, block in ((core, mine), (1 - core, theirs)):
        for turn in range(2):
            first = there * half + lax.rem(pos[3] + turn, 2) * piece
            rows = pl.ds(pl.multiple_of(first, piece), piece)
            inputs[rows, :] = block[pl.ds(turn * half, piece), :]
            grad_out[rows, :] = block[pl.ds(turn * half + piece, piece), :]
    for rows in row_blocks(2 * half):
        unit, _ = unit_of(wide(inputs[rows, :]))
        normed[rows, :] = low(unit * vectors[0:1, :] + vectors[4:5, :])
        grad_two[rows, :] = low(wide(grad_out[rows, :]) * vectors[3:4, :] * gate[rows, :])
    for kind, shift in enumerate((5, None, 6)):
        made = dot_of(normed[...], weight[:, pl.ds(kind * 512, 512)], 1, 0)
        for chip in range(4):
            piece = made[:, chip * 128 : chip * 128 + 128]
            if shift is not None:
                column = pl.multiple_of((2 * chip + core) * 128, 128)
                piece = piece + vectors[shift : shift + 1, pl.ds(column, 128)]
            qkv[:, pl.ds(kind * 512 + chip * 128, 128)] = low(piece)
    lane = lax.broadcasted_iota(jnp.int32, (2 * half, 128), 1)
    live = mask[...] > 0
    for pair in range(4):
        query = qkv[:, pl.ds(pair * 128, 128)] * jnp.bfloat16(HD ** (-0.5))
        key = qkv[:, pl.ds(512 + pair * 128, 128)]
        value = qkv[:, pl.ds(1024 + pair * 128, 128)]
        got = []
        for head in range(2):
            chosen = (lane // HD) == head
            scores = dot_of(jnp.where(chosen, query, jnp.zeros_like(query)), key, 1, 1)
            scores = jnp.where(live, scores, NEGATIVE)
            expo = jnp.exp(scores - jnp.max(scores, axis=1, keepdims=True))
            probs = expo * (1.0 / jnp.sum(expo, axis=1, keepdims=True))
            got.append(dot_of(low(probs), value, 1, 0))
        attended[:, pl.ds(pair * 128, 128)] = low(jnp.where(lane < HD, got[0], got[1]))


def put_halves(values, tile, upper, lower):
    half = values.shape[0] // 2
    upper[:, tile] = low(values[:half])
    lower[:, tile] = low(values[half:])


def of_halves(upper, lower, n, size=128):
    count = upper.shape[0] // size
    return wide((upper, lower)[n // count][pl.ds((n % count) * size, size), :])


def start_copies(pairs, semaphores):
    started = []
    for n, (source, target) in enumerate(pairs):
        started.append(pltpu.make_async_copy(source, target, semaphores.at[n]))
        started[-1].start()
    return started


def proj_kernel(
    pos, attended, near_a, far_a, near_b, far_b, proj, upper, lower, semaphores
):
    pairs = []
    for part, chip, _, block, n in join_parts(pos, (0, 0), near_a, far_a, near_b, far_b):
        row = pl.multiple_of(chip * 128, 128)
        target = proj.at[pl.ds(row, 128), pl.ds(part * 512, 512)]
        pairs.append((block.at[pl.ds(n * 128, 128), pl.ds(2048, 512)], target))
    for copy in start_copies(pairs, semaphores):
        copy.wait()
    for tile in row_blocks(1024, 256):
        put_halves(dot_of(attended[...], proj[:, tile], 1, 0), tile, upper, lower)


def far_chips(pos):
    return (1 - pos[1], 3 - pos[1]), (2 * (1 - pos[2]), 2 * (1 - pos[2]) + 1)


def second_chips(pos):
    own = 2 * pos[2] + pos[1]
    over_y = 2 * (1 - pos[2]) + pos[1]
    over_x = 2 * pos[2] + 1 - pos[1]
    return ((own, pos[2]), (over_y, 1 - pos[2])), ((own, pos[1]), (over_x, 1 - pos[1]))


def chip_columns(ref, chip, count):
    return ref[:, pl.ds(pl.multiple_of(chip * count, count), count)]


def far_products(pos, left, right, outs):
    rows = left.shape[1] // 4
    cut = right.shape[1] // 2
    for part, chips in enumerate(far_chips(pos)):
        for n in range(2):
            made = dot_of(
                chip_columns(left, chips[n], rows), right[:, pl.ds(part * cut, cut)], 0, 0
            )
            outs[part][pl.ds(n * rows, rows), :] = low(made)


def fc1_copies(pos, near_a, far_a, near_b, far_b, fc1):
    pairs = []
    for _, chip, owner, block, n in join_parts(
        pos, (pos[0], 1 - pos[0]), near_a, far_a, near_b, far_b
    ):
        row = pl.multiple_of((2 * chip + owner) * 128, 128)
        source = block.at[pl.ds(n * 128, 128), pl.ds(0, 2048)]
        pairs.append((source, fc1.at[pl.ds(row, 128), :]))
    return pairs


def middle_kernel(
    pos, inputs, own_upper, own_lower, upper, lower, vectors, bias, gate, near_a, far_a, near_b,
    far_b, grad_two, hidden, normed, slope, activated, out_a, out_b, fc1, semaphores,
):
    pairs = fc1_copies(pos, near_a, far_a, near_b, far_b, fc1)
    started = start_copies(pairs, semaphores)
    for n, rows in enumerate(row_blocks(inputs.shape[0])):
        made = of_halves(own_upper, own_lower, n) + of_halves(upper, lower, n) + vectors[7:8, :]
        state = wide(inputs[rows, :]) + made * vectors[1:2, :] * gate[rows, :]
        hidden[rows, :] = state
        unit, _ = unit_of(state)
        normed[rows, :] = low(unit * vectors[2:3, :] + vectors[8:9, :])
    for copy in started:
        copy.wait()

    def units(n, _):
        tile = pl.ds(pl.multiple_of(n * 256, 256), 256)
        pre = dot_of(normed[...], fc1[:, tile], 1, 0) + bias[:, tile]
        bell = 0.5 * (1.0 + lax.erf(pre * ROOT_HALF))
        activated[:, tile] = low(pre * bell)
        slope[:, tile] = low(bell + pre * jnp.exp(-0.5 * pre * pre) * INV_ROOT_TWO_PI)
        return 0

    lax.fori_loop(0, 8, units, 0)
    far_products(pos, activated, grad_two, (out_a, out_b))


def units_back_kernel(
    pos, near_a, far_a, near_b, far_b, grad_two, slope, activated, normed,
    fc1_near_a, fc1_far_a, fc1_near_b, fc1_far_b,
    grad_pre, sums, partial, upper, lower, out_a, out_b, branch, branch_low, fc2, fc1, semaphores,
):
    started = start_copies(
        fc1_copies(pos, fc1_near_a, fc1_far_a, fc1_near_b, fc1_far_b, fc1), semaphores
    )
    for part, chip, _, block, n in join_parts(pos, (0, 0), near_a, far_a, near_b, far_b):
        row = pl.multiple_of(chip * 512 + part * 256, 256)
        fc2[pl.ds(row, 256), :] = block[pl.ds(n * 256, 256), :]

    def units(n, _):
        tile = pl.ds(pl.multiple_of(n * 256, 256), 256)
        made = low(dot_of(grad_two[...], fc2[tile, :], 1, 1) * wide(slope[:, tile]))
        grad_pre[:, tile] = made
        sums[:, tile] = down(wide(made))
        return 0

    lax.fori_loop(0, 8, units, 0)
    for copy in started:
        copy.wait()
    for tile in row_blocks(1024, 256):
        made = dot_of(grad_pre[...], fc1[tile, :], 1, 1)
        partial[:, tile] = made
        put_halves(made, tile, upper, lower)
    far_products(pos, normed, grad_pre, (out_a, out_b))
    half = branch.shape[0]
    mine = pl.ds(pl.multiple_of(pos[0] * half, half), half)
    theirs = pl.ds(pl.multiple_of((1 - pos[0]) * half, half), half)
    for tile in row_blocks(1024, 256):
        branch[:, tile] = dot_of(activated[mine, :], fc2[:, tile], 1, 0)
        branch_low[:, tile] = low(dot_of(activated[theirs, :], fc2[:, tile], 1, 0))


def proj_product(attended, grad_one, chip, part):
    return dot_of(chip_columns(attended, chip, 128), grad_one[:, pl.ds(part * 512, 512)], 0, 0)


def norm_back_kernel(
    pos, grad_out, partial, upper, lower, hidden, own_upper, own_lower, their_upper, their_lower,
    vectors, gate, proj, attended,
    fc1_a, fc1_b, grad_hidden, grad_one, grad_attended, sums, far_a, far_b,
):
    total = [0.0] * 4
    for n, rows in enumerate(row_blocks(hidden.shape[0])):
        grad = partial[rows, :] + of_halves(upper, lower, n)
        unit, inverse = unit_of(hidden[rows, :])
        state = wide(grad_out[rows, :]) + norm_back(grad, unit, inverse, vectors[2:3, :])
        grad_hidden[rows, :] = state
        gated = state * gate[rows, :]
        made = low(gated * vectors[1:2, :])
        grad_one[rows, :] = made
        branch = of_halves(own_upper, own_lower, n) + of_halves(their_upper, their_lower, n)
        terms = (gated * (branch + vectors[7:8, :]), grad * unit, wide(made), grad)
        total = [one + down(term) for one, term in zip(total, terms)]
    for n in range(4):
        sums[n : n + 1, :] = total[n]
    grad_attended[...] = low(dot_of(grad_one[...], proj[...], 1, 1))
    for part, chips in enumerate(far_chips(pos)):
        out = (far_a, far_b)[part]
        out[pl.ds(0, 512), :] = (fc1_a, fc1_b)[part][...]
        for n in range(2):
            made = low(proj_product(attended, grad_one, chips[n], part))
            here = pl.ds(512 + n * 64, 64)
            out[here, pl.ds(0, 512)] = made[:64]
            out[here, pl.ds(512, 512)] = made[64:]


def fold_kernel(pos, left, right, got_a, got_b, keep_a, give_a, keep_b, give_b):
    rows = left.shape[1] // 4
    cut = right.shape[1] // 2
    outs = ((keep_a, give_a), (keep_b, give_b))
    for part, chips in enumerate(second_chips(pos)):
        for n in range(2):
            chip, arrived = chips[n]
            made = dot_of(chip_columns(left, chip, rows), right[:, pl.ds(part * cut, cut)], 0, 0)
            there = pl.ds(pl.multiple_of(arrived * rows, rows), rows)
            outs[part][n][...] = low(made + wide((got_a, got_b)[part][there, :]))


def fc1_fold_kernel(
    pos, left, right, attended, grad_one, small, got_a, got_b, keep_a, give_a, keep_b, give_b
):
    outs = ((keep_a, give_a), (keep_b, give_b))
    for part, chips in enumerate(second_chips(pos)):
        got = (got_a, got_b)[part]
        for n in range(2):
            chip, arrived = chips[n]
            out = outs[part][n]
            made = dot_of(chip_columns(left, chip, 256), right[:, pl.ds(part * 1024, 1024)], 0, 0)
            there = pl.ds(pl.multiple_of(arrived * 256, 256), 256)
            out[pl.ds(0, 256), :] = low(made + wide(got[there, :]))
            made = proj_product(attended, grad_one, chip, part)
            there = pl.ds(pl.multiple_of(512 + arrived * 64, 64), 64)
            arrived_rows = wide(got[there, :])
            here = pl.ds(256, 64)
            out[here, pl.ds(0, 512)] = low(made[:64] + arrived_rows[:, :512])
            out[here, pl.ds(512, 512)] = low(made[64:] + arrived_rows[:, 512:])
    give_b[pl.ds(320, 16), :] = small[...]


def attend_back_kernel(
    pos, qkv, mask, grad, normed, out, sums, far_a, far_b
):
    length = qkv.shape[0]
    lane = lax.broadcasted_iota(jnp.int32, (length, 128), 1)
    live = mask[...] > 0
    factor = HD ** (-0.5)
    for pair in range(4):
        spans = [pl.ds(offset + pair * 128, 128) for offset in (0, 512, 1024)]
        query, key, value = (qkv[:, span] for span in spans)
        grad_pair = grad[:, pl.ds(pair * 128, 128)]
        grad_query, grad_key, grad_value = [], 0.0, 0.0
        for head in range(2):
            chosen = (lane // HD) == head
            query_one = jnp.where(chosen, query, jnp.zeros_like(query))
            grad_head = jnp.where(chosen, grad_pair, jnp.zeros_like(grad_pair))
            scores = dot_of(key, query_one, 1, 1) * factor
            scores = jnp.where(live, scores, NEGATIVE)
            expo = jnp.exp(scores - jnp.max(scores, axis=0, keepdims=True))
            probs = expo * (1.0 / jnp.sum(expo, axis=0, keepdims=True))
            grad_probs = dot_of(value, grad_head, 1, 1)
            along = jnp.sum(grad_probs * probs, axis=0, keepdims=True)
            grad_scores = low(probs * (grad_probs - along))
            grad_value += dot_of(low(probs), grad_head, 1, 0)
            grad_key += dot_of(grad_scores, query_one, 1, 0)
            grad_query.append(dot_of(grad_scores, key, 0, 0))
        made = jnp.where(lane < HD, grad_query[0], grad_query[1]) * factor
        for span, item in zip(spans, (made, grad_key * factor, grad_value)):
            item = low(item)
            out[:, span] = item
            sums[:, span] = down(wide(item))
    far_products(pos, normed, out, (far_a, far_b))


def last_fold_kernel(
    pos, normed, grad_qkv, got_a, got_b, small, small_got, keep_a, give_a, keep_b, give_b
):
    outs = ((keep_a, give_a), (keep_b, give_b))
    for part, chips in enumerate(second_chips(pos)):
        for n in range(2):
            chip, arrived = chips[n]
            made = dot_of(
                chip_columns(normed, chip, 256), grad_qkv[:, pl.ds(part * 768, 768)], 0, 0
            )
            there = pl.ds(pl.multiple_of(arrived * 256, 256), 256)
            outs[part][n][pl.ds(0, 256), :] = low(made + wide((got_a, got_b)[part][there, :]))
    for out, at_y in ((keep_a, pos[2]), (give_a, 1 - pos[2])):
        column = pl.multiple_of(at_y * 128, 128)
        sums = small[at_y] + wide(small_got[:, pl.ds(column, 128)])
        out[pl.ds(256, 32), :] = jnp.zeros((32, 768), jnp.bfloat16)
        out[pl.ds(256, 16), pl.ds(0, 128)] = low(sums)


def first_back_kernel(pos, grad_qkv, weight, last, partial, upper, lower):
    half = lower.shape[0]
    for tile in row_blocks(1024, 256):
        made = dot_of(grad_qkv[...], weight[tile, :], 1, 1)
        partial[:, tile] = made
        upper[pl.ds(0, half), tile] = low(made[:half])
        lower[:, tile] = low(made[half:])
    upper[pl.ds(half, 16), :] = low(jnp.broadcast_to(last[0:1, :], (16, 1024)))


def inputs_back_kernel(
    pos, inputs, partial, upper, lower, grad_hidden, vectors, out, sums, grads
):
    total = [0.0] * 2
    half = out.shape[0]
    for n, rows in enumerate(row_blocks(2 * half)):
        there = (upper, lower)[n * 128 // half]
        grad = partial[rows, :] + wide(there[pl.ds((n * 128) % half, 128), :])
        grads[rows, :] = grad
        unit, _ = unit_of(wide(inputs[rows, :]))
        total = [one + down(term) for one, term in zip(total, (grad * unit, grad))]
    for n in range(2):
        sums[n : n + 1, :] = total[n]
    sums[2:3, :] = wide(upper[pl.ds(half, 16), :])[0:1]
    for n in range(half // 128):
        rows = pl.ds(pl.multiple_of(pos[0] * half + n * 128, 128), 128)
        unit, inverse = unit_of(wide(inputs[rows, :]))
        state = grad_hidden[rows, :] + norm_back(grads[rows, :], unit, inverse, vectors[0:1, :])
        out[pl.ds(n * 128, 128), :] = low(state)


def output_kernel(
    pos, hidden, branch, other, vectors, gate, grad_out, grad_two, out, sums
):
    half = out.shape[0]
    gain_sum, shift_sum = 0.0, 0.0
    for n in range(half // 128):
        here = pl.ds(n * 128, 128)
        rows = pl.ds(pl.multiple_of(pos[0] * half + n * 128, 128), 128)
        made = branch[here, :] + wide(other[here, :]) + vectors[9:10, :]
        out[here, :] = low(hidden[rows, :] + made * vectors[3:4, :] * gate[rows, :])
        gain_sum += down(wide(grad_out[rows, :]) * gate[rows, :] * made)
    for rows in row_blocks(2 * half):
        shift_sum += down(wide(grad_two[rows, :]))
    sums[0:1, :] = gain_sum
    sums[1:2, :] = shift_sum


def small_kernel(pos, first, second, last, attention, units, keep, give):
    core = pos[0]
    order = [(first, 0), (second, 0), (second, 1), (last, 0), (first, 1)]
    order += [None, None, (second, 2), (second, 3), (last, 1)]
    give[...] = jnp.zeros_like(give)
    for at_y in range(2):
        for over in range(2):
            chip = 2 * at_y + (pos[1] if over == 0 else 1 - pos[1])
            own = pl.ds(pl.multiple_of((2 * chip + core) * 128, 128), 128)
            here = pl.multiple_of(chip * 128, 128)
            lines = [None if item is None else item[0][item[1] : item[1] + 1, own] for item in order]
            lines[3] = lines[3] + first[2:3, own]
            lines[5] = attention[:, pl.ds(here, 128)]
            lines[6] = attention[:, pl.ds(pl.multiple_of(1024 + chip * 128, 128), 128)]
            for j in range(4):
                column = pl.multiple_of(chip * 512 + j * 128, 128)
                lines.append(units[:, pl.ds(column, 128)])
            block = jnp.concatenate(lines + [jnp.zeros((2, 128), jnp.float32)], axis=0)
            if over == 0:
                keep[at_y, :, :] = block
            else:
                give[:, pl.ds(at_y * 128, 128)] = low(block)


def finish_qkv_kernel(pos, mine, theirs, out):
    core = pos[0]
    rows = pl.ds(pl.multiple_of(core * 128, 128), 128)
    for j in range(12):
        here = pl.ds(j * 128, 128)
        out[:, pl.ds(pl.multiple_of((2 * j + core) * 128, 128), 128)] = wide(mine[rows, here])
        out[:, pl.ds(pl.multiple_of((2 * j + 1 - core) * 128, 128), 128)] = wide(theirs[:, here])


def finish_fc1_kernel(pos, mine, theirs, out):
    core = pos[0]
    rows = pl.ds(pl.multiple_of(core * 128, 128), 128)
    for j in range(4):
        here = pl.ds(j * 512, 512)
        out[:, pl.ds(pl.multiple_of((2 * j + core) * 512, 512), 512)] = wide(mine[rows, here])
        out[:, pl.ds(pl.multiple_of((2 * j + 1 - core) * 512, 512), 512)] = wide(theirs[:, here])


def add_low(one, two):
    return (one.astype(jnp.float32) + two.astype(jnp.float32)).astype(jnp.bfloat16)


def line_in(values):
    return lax.ppermute(values, "seq", [(0, 1), (3, 2)])


def line_mid(values):
    return lax.ppermute(values, "seq", [(1, 2), (2, 1)])


def line_out(values):
    return lax.ppermute(values, "seq", [(1, 0), (2, 3)])


def inner():
    at_z = lax.axis_index("seq")
    return ((at_z == 1) | (at_z == 2)).astype(jnp.int32)


def image_moves(back):
    seq = lax.axis_size("seq")
    rounds = []
    for turn in range(2):
        moves = []
        for chip in range(lax.axis_size("dp") // 2):
            for core in range(2):
                for quarter in range(seq):
                    slot = (quarter + turn) % 2
                    source = (2 * chip + core) * seq + quarter
                    target = (2 * chip + quarter // 2) * seq + 2 * core + slot
                    moves.append((target, source) if back else (source, target))
        rounds.append(moves)
    return rounds


def to_images(first, second, *earlier):
    at_z = lax.axis_index("seq")
    first, second = after((first, second), *earlier)
    got = []
    for turn, moves in enumerate(image_moves(False)):
        slot = (at_z + turn) % 2
        sent = [lax.dynamic_index_in_dim(item, slot, 0, False) for item in (first, second)]
        got.append(lax.ppermute(jnp.concatenate(sent, axis=0), ("dp", "seq"), moves))
    return jnp.concatenate(got, axis=0)


def from_images(values):
    at_z = lax.axis_index("seq")
    pieces = values.reshape(2, values.shape[0] // 2, values.shape[1])
    got = []
    for turn, moves in enumerate(image_moves(True)):
        sent = lax.dynamic_index_in_dim(pieces, (at_z + turn) % 2, 0, False)
        got.append(lax.ppermute(sent, ("dp", "seq"), moves))
    return got


def slots_of(got):
    even = lax.axis_index("seq") % 2 == 0
    return jnp.stack([jnp.where(even, got[0], got[1]), jnp.where(even, got[1], got[0])])


def image_plan(
    tokens, group_count, pad_mask, w_qkv, w_proj, w_fc1, w_fc2, fc1_bias, scales, shifts, cotangent
):
    slot_count, _, width = tokens.shape
    length = pad_mask.shape[1]
    half = length // 2
    f32, bf16 = jnp.float32, jnp.bfloat16
    core, at_x, at_y = place()
    at_z = lax.axis_index("seq")
    pos = jnp.stack([core, at_x, at_y, at_z]).astype(jnp.int32)

    alive = jnp.arange(slot_count, dtype=jnp.int32) < group_count[0]
    mask_own = jnp.where(alive[:, None], pad_mask, 0).astype(f32)
    mine, give = local_call(
        cut_kernel, [((128, 4224), bf16), ((128, 3840), bf16)],
        pos, w_qkv, w_fc1, w_proj, scales, shifts, fc1_bias.reshape(4, 128), mask_own, room=12,
    )
    got = swap(give, CORE)
    blocks = (mine, jnp.concatenate([got[:, :3712], w_proj[:, 512:]], axis=1))
    mask_both = joined(
        mask_own,
        got[:8, 3712:].reshape(4, slot_count, 128).transpose(1, 0, 2).reshape(
            slot_count, length
        ).astype(f32),
        core, 0,
    )
    mask_row = lax.dynamic_index_in_dim(mask_both, at_z, 0, False)
    token_gate = mask_row[:, None]

    def links(sent, order=(ALONG_X, ALONG_Y)):
        return swap(sent[0], order[0]), swap(sent[1], order[1])

    def second_link(blocks, got):
        near_a, near_b = (jnp.concatenate(pair, axis=0) for pair in zip(blocks, got))
        far_a, far_b = links((near_a, near_b), (ALONG_Y, ALONG_X))
        return near_a, far_a, near_b, far_b

    def lanes(pair, start, stop):
        return [item[:, start:stop] for item in pair]

    first = links(blocks)
    fc2_blocks = after((w_fc2[:256], w_fc2[256:]), blocks[1])
    fc2_first = links(fc2_blocks)
    both = to_images(tokens, cotangent, blocks[1])
    qkv_parts = second_link(lanes(blocks, 0, 1664), lanes(first, 0, 1664))
    first = after(first, qkv_parts[0], qkv_parts[2])
    fc1_parts = second_link(lanes(blocks, 1664, 4224), lanes(first, 1664, 4224))
    fc2_parts = second_link(fc2_blocks, after(fc2_first, fc1_parts[0], fc1_parts[2]))

    full = (length, width)
    qkv_w, vectors, bias, inputs, grad_out, grad_two, normed_one, qkv, attended = local_call(
        front_kernel,
        [
            ((width, 1536), bf16), ((16, width), f32), ((1, 2048), f32), (full, bf16),
            (full, bf16), (full, bf16), (full, bf16), ((length, 1536), bf16),
            ((length, 512), bf16),
        ],
        pos, both, swap(both, CORE), *after(qkv_parts, fc2_parts[0], fc2_parts[2]),
        mask_row[None, :], token_gate, room=24,
    )
    halves = [((half, width), bf16)] * 2
    proj_w, *one_own = local_call(
        proj_kernel, [((512, width), bf16)] + halves,
        pos, attended, *fc1_parts, room=14, outside=(1, 2, 3, 4), copies=8,
    )
    one_other = [swap(item, CORE) for item in one_own]
    hidden, normed_two, slope, activated, far_a, far_b = local_call(
        middle_kernel,
        [
            (full, f32), (full, bf16), ((length, 2048), bf16), ((length, 2048), bf16),
            ((1024, 512), bf16), ((1024, 512), bf16),
        ],
        pos, inputs, *one_own, *one_other, vectors, bias, token_gate, *fc1_parts, grad_two,
        scratch=[((width, 2048), bf16)], room=30, outside=(8, 9, 10, 11), copies=8,
    )

    def fold(left, right, got, *earlier):
        block = (left.shape[1] // 4, right.shape[1] // 2)
        got_a, got_b = after(got, *earlier)
        keep_a, give_a, keep_b, give_b = local_call(
            fold_kernel, [(block, bf16)] * 4, pos, left, right, got_a, got_b, room=14,
    )
        return (keep_a, keep_b), (give_a, give_b)

    def half_of(keep, got):
        return [add_low(one, two) for one, two in zip(keep, got)]

    fc2_got = links((far_a, far_b))
    grad_pre, unit_sums, partial, upper, lower, far_a, far_b, branch_two, branch_low = local_call(
        units_back_kernel,
        [((length, 2048), bf16), ((1, 2048), f32), (full, f32)]
        + halves
        + [((512, 1024), bf16), ((512, 1024), bf16), ((half, width), f32), ((half, width), bf16)],
        pos, *fc2_parts, grad_two, slope, activated, normed_two, *fc1_parts,
        scratch=[((2048, width), bf16), ((width, 2048), bf16)], outside=(8, 9, 10, 11), copies=8,
    )
    others = [swap(item, CORE) for item in (upper, lower)]
    branch_other = swap(branch_low, CORE)
    output, last_sums = local_call(
        output_kernel, [((half, width), bf16), ((2, width), f32)],
        pos, hidden, branch_two, branch_other, vectors, token_gate, grad_out,
        grad_two, room=14,
    )
    out_got = from_images(output)
    fc1_far = ((640, 1024), bf16)
    grad_hidden, grad_one, grad_attended, second_sums, far_a, far_b = local_call(
        norm_back_kernel,
        [
            (full, f32), (full, bf16), ((length, 512), bf16), ((4, width), f32), fc1_far, fc1_far,
        ],
        pos, grad_out, partial, *after(others, output), hidden, *one_own, *one_other, vectors,
        token_gate, proj_w, attended, far_a, far_b, room=24,
    )
    fc2_keep, fc2_give = fold(activated, grad_two, fc2_got, grad_attended, out_got[0])
    fc2_again = links(fc2_give, (ALONG_Y, ALONG_X))
    fc1_got = links(after((far_a, far_b), *fc2_give))
    grad_qkv_rows, attention_sums, far_a, far_b = local_call(
        attend_back_kernel,
        [
            ((length, 1536), bf16), ((1, 1536), f32), ((512, 768), bf16), ((512, 768), bf16),
        ],
        pos, after(qkv, *fc2_give), token_gate, grad_attended, normed_one, room=24,
    )
    fc2_half = jnp.concatenate(half_of(fc2_keep, after(fc2_again, grad_qkv_rows, out_got[1])), axis=1)
    fc2_in = line_in(fc2_half)
    partial, upper, lower = local_call(
        first_back_kernel, [(full, f32), ((half + 16, width), bf16), ((half, width), bf16)],
        pos, after(grad_qkv_rows, fc2_half), qkv_w, last_sums, room=16,
    )
    grad_input, first_sums = local_call(
        inputs_back_kernel, [((half, width), bf16), ((3, width), f32)],
        pos, inputs, partial, swap(upper, CORE), swap(lower, CORE), grad_hidden, vectors,
        scratch=[(full, f32)], room=16,
    )
    in_got = from_images(grad_input)
    small_keep, small_give = local_call(
        small_kernel, [((2, 16, 128), f32), ((16, 1024), bf16)],
        pos, first_sums, second_sums, last_sums, attention_sums, unit_sums, room=6,
    )
    fc1_block = ((320, 1024), bf16)
    keep_a, give_a, keep_b, give_b = local_call(
        fc1_fold_kernel, [fc1_block, fc1_block, fc1_block, ((336, 1024), bf16)],
        pos, normed_two, grad_pre, attended, grad_one, small_give, *fc1_got, room=20,
    )
    fc1_keep, fc1_give = (keep_a, keep_b), (give_a, give_b)
    fc1_again = links(fc1_give, (ALONG_Y, ALONG_X))
    last_got = links(after((far_a, far_b), *fc1_give))
    fc2_sum = add_low(fc2_half, after(fc2_in, *fc1_give, *in_got))
    fc2_mid = line_mid(fc2_sum)

    small_got = fc1_again[1][320:]
    fc1_again = (fc1_again[0], fc1_again[1][:320])
    fc1_half = half_of(fc1_keep, after(fc1_again, fc2_sum))
    fc1_in = [line_in(item) for item in fc1_half]
    fc2_total = add_low(fc2_sum, after(fc2_mid, *fc1_half))
    fc2_out = line_out(fc2_total)
    fc1_sum, fc1_mid, fc1_total, fc1_out = [None] * 2, [None] * 2, [None] * 2, [None] * 2
    fc1_sum[0] = add_low(fc1_half[0], after(fc1_in[0], fc2_total))
    fc1_mid[0] = line_mid(fc1_sum[0])
    last_got = after(last_got, fc1_sum[0])
    wide_block, block = ((288, 768), bf16), ((256, 768), bf16)
    keep_a, give_a, keep_b, give_b = local_call(
        last_fold_kernel, [wide_block, wide_block, block, block],
        pos, normed_one, grad_qkv_rows, *last_got, small_keep, small_got, room=16,
    )
    last_again = links((give_a, give_b), (ALONG_Y, ALONG_X))
    fc1_sum[1] = add_low(fc1_half[1], after(fc1_in[1], give_a, give_b))
    fc1_mid[1] = line_mid(fc1_sum[1])
    last_again, fc2_out = after((last_again, fc2_out), fc1_sum[1])
    last_half = half_of((keep_a, keep_b), last_again)
    last_in = [None, line_in(last_half[1])]
    fc1_total[0] = add_low(fc1_sum[0], after(fc1_mid[0], *last_half))
    fc1_out[0] = line_out(fc1_total[0])

    def line_end(total, out):
        return jnp.where(inner() == 1, total, out)

    def core_give(values):
        return lax.dynamic_slice_in_dim(values, (1 - core) * 128, 128, 0)

    fc1_total[1] = add_low(fc1_sum[1], after(fc1_mid[1], fc1_total[0]))
    fc1_out[1] = line_out(fc1_total[1])
    grad_fc2 = line_end(fc2_total, after(fc2_out, fc1_total[1])).astype(f32)
    last_sum, last_mid, last_total, last_out = [None] * 2, [None] * 2, [None] * 2, [None] * 2
    arrived, fc1_out[0] = after((last_in[1], fc1_out[0]), grad_fc2)
    last_sum[1] = add_low(last_half[1], arrived)
    last_mid[1] = line_mid(last_sum[1])
    last_in[0] = line_in(after(last_half[0], last_sum[1]))
    arrived, fc1_out[1] = after((last_in[0], fc1_out[1]), last_sum[1])
    last_sum[0] = add_low(last_half[0], arrived)
    last_mid[0] = line_mid(last_sum[0])
    last_total[1] = add_low(last_sum[1], after(last_mid[1], last_sum[0]))
    last_out[1] = line_out(last_total[1])
    fc1_rows = [line_end(*pair) for pair in zip(fc1_total, after(fc1_out, last_total[1]))]
    grad_proj = jnp.concatenate(
        [
            jnp.concatenate([item[256:, :512], item[256:, 512:]], axis=0) for item in fc1_rows
        ],
        axis=1,
    ).astype(f32)
    fc1_rows = jnp.concatenate([item[:256] for item in fc1_rows], axis=1)
    last_total[0] = add_low(last_sum[0], after(last_mid[0], fc1_rows))
    last_out[0] = line_out(last_total[0])
    (grad_fc1,) = local_call(
        finish_fc1_kernel, [((128, 4096), f32)],
        pos, fc1_rows, after(swap(core_give(fc1_rows), CORE), last_total[0]), room=10,
    )
    last_out = after(last_out, grad_fc1)
    last_rows = [line_end(*pair) for pair in zip(last_total, last_out)]
    small = last_rows[0][256:272, :128].astype(f32)
    qkv_rows = jnp.concatenate([last_rows[0][:256], last_rows[1]], axis=1)
    qkv_core = swap(core_give(qkv_rows), CORE)
    (grad_qkv,) = local_call(
        finish_qkv_kernel, [((128, 3072), f32)], pos, qkv_rows, qkv_core, room=10
    )
    grad_scales = small[:4]
    grad_shifts = small[4:10]
    grad_bias = small[10:14].reshape(512)
    return (
        slots_of(out_got),
        slots_of(in_got),
        grad_qkv,
        grad_proj,
        grad_fc1,
        grad_fc2,
        grad_bias,
        grad_scales,
        grad_shifts,
    )


def on_device(*arrays):
    tokens = arrays[0]
    whole_images = 2 * tokens.shape[0] == lax.axis_size("seq")
    if lax.axis_size("dp") == 8 and lax.axis_size("seq") == 4 and whole_images:
        return image_plan(*arrays)
    return general_plan(*arrays)


def solution(mesh):
    return jax.shard_map(
        on_device,
        mesh=mesh,
        in_specs=(
            P("dp", "seq", None),
            P("dp"),
            P("dp", None),
            P("dp", None),
            P("dp", None),
            P("dp", None),
            P("dp", None),
            P("dp"),
            P(None, "dp"),
            P(None, "dp"),
            P("dp", "seq", None),
        ),
        out_specs=(
            P("dp", "seq", None),
            P("dp", "seq", None),
            P("dp", None),
            P("dp", None),
            P("dp", None),
            P("dp", None),
            P("dp"),
            P(None, "dp"),
            P(None, "dp"),
        ),
        check_vma=False,
    )
```

```python
import jax
import jax.numpy as jnp
from jax import lax
from jax.experimental import pallas as pl
from jax.experimental.pallas import tpu as pltpu
from jax.sharding import PartitionSpec as P

HD = 64


EPSILON = 1e-06
ROOT_HALF = 0.7071067811865476
INV_ROOT_TWO_PI = 0.3989422804014327


def layer_norm(values, gain, shift):
    mean_row = jnp.mean(values, axis=-1, keepdims=True)
    centred = values - mean_row
    inverse = lax.rsqrt(jnp.mean(centred * centred, axis=-1, keepdims=True) + EPSILON)
    unit_rows = centred * inverse
    return (unit_rows * gain + shift, unit_rows, inverse)


def norm_back(grad_normed, unit_rows, inverse, gain):
    scaled = grad_normed * gain
    centre = jnp.mean(scaled, axis=-1, keepdims=True)
    along = jnp.mean(scaled * unit_rows, axis=-1, keepdims=True)
    return inverse * (scaled - centre - unit_rows * along)


def gelu_exact(values):
    return 0.5 * values * (1.0 + lax.erf(values * ROOT_HALF))


def gelu_slope(values):
    return (
        0.5 * (1.0 + lax.erf(values * ROOT_HALF))
        + values * jnp.exp(-0.5 * values * values) * INV_ROOT_TWO_PI
    )


def token_sum(values):
    return jnp.sum(values, axis=(0, 1))


def general_plan(
    tokens, group_count, pad_mask, w_qkv, w_proj, w_fc1, w_fc2, fc1_bias, scales, shifts, cotangent
):
    slot_count, piece, width = tokens.shape
    seq_total = pad_mask.shape[1]
    part_width = width // lax.axis_size("seq")
    head_count = part_width // HD
    factor = HD ** (-0.5)
    alive = jnp.arange(slot_count, dtype=jnp.int32) < group_count[0]
    key_mask = jnp.where(alive[:, None], pad_mask, 0).astype(jnp.float32)
    query_mask = lax.dynamic_slice_in_dim(key_mask, lax.axis_index("seq") * piece, piece, 1)[
        :, :, None
    ]
    full_qkv, full_proj, full_fc1, full_fc2, full_bias, full_scales, full_shifts = (
        lax.all_gather(w_qkv, "dp", axis=0, tiled=True),
        lax.all_gather(w_proj, "dp", axis=0, tiled=True),
        lax.all_gather(w_fc1, "dp", axis=0, tiled=True),
        lax.all_gather(w_fc2, "dp", axis=0, tiled=True),
        lax.all_gather(fc1_bias, "dp", axis=0, tiled=True),
        lax.all_gather(scales, "dp", axis=1, tiled=True),
        lax.all_gather(shifts, "dp", axis=1, tiled=True),
    )
    gains = full_scales.astype(jnp.float32)
    offsets = full_shifts.astype(jnp.float32)
    hidden_bias = full_bias.astype(jnp.float32)
    inputs = tokens.astype(jnp.float32)
    normed_one, unit_one, inverse_one = layer_norm(inputs, gains[0], offsets[0])
    normed_one = normed_one.astype(jnp.bfloat16)
    projected = jnp.dot(normed_one, full_qkv, preferred_element_type=jnp.float32)
    queries = (projected[:, :, :width] + offsets[1]).astype(jnp.bfloat16)
    key_rows = projected[:, :, width : 2 * width].astype(jnp.bfloat16)
    value_rows = (projected[:, :, 2 * width :] + offsets[2]).astype(jnp.bfloat16)
    head_query, head_key, head_value = (
        lax.all_to_all(queries, "seq", split_axis=2, concat_axis=1, tiled=True),
        lax.all_to_all(key_rows, "seq", split_axis=2, concat_axis=1, tiled=True),
        lax.all_to_all(value_rows, "seq", split_axis=2, concat_axis=1, tiled=True),
    )
    head_shape = (slot_count, seq_total, head_count, HD)
    query_heads = head_query.reshape(head_shape)
    key_heads = head_key.reshape(head_shape)
    value_heads = head_value.reshape(head_shape)

    def scores_of():
        raw = (
            jnp.einsum(
                "bqhe,bkhe->bhqk", query_heads, key_heads, preferred_element_type=jnp.float32
            )
            * factor
        )
        return jnp.where(key_mask[:, None, None, :] > 0, raw, -1e30)

    scores = scores_of()
    top = jnp.max(scores, axis=-1, keepdims=True)
    log_total = top + jnp.log(jnp.sum(jnp.exp(scores - top), axis=-1, keepdims=True))
    probs_low = jnp.exp(scores - log_total).astype(jnp.bfloat16)
    attended = jnp.einsum(
        "bhqk,bkhe->bqhe", probs_low, value_heads, preferred_element_type=jnp.float32
    )
    attended = attended.astype(jnp.bfloat16).reshape(slot_count, seq_total, part_width)
    mixed = lax.all_to_all(attended, "seq", split_axis=1, concat_axis=2, tiled=True)
    branch_one = jnp.dot(mixed, full_proj, preferred_element_type=jnp.float32) + offsets[3]
    hidden_state = inputs + branch_one * gains[1] * query_mask
    normed_two, unit_two, inverse_two = layer_norm(hidden_state, gains[2], offsets[4])
    normed_two = normed_two.astype(jnp.bfloat16)
    pre_act = jnp.dot(normed_two, full_fc1, preferred_element_type=jnp.float32) + hidden_bias
    activated = gelu_exact(pre_act).astype(jnp.bfloat16)
    branch_two = jnp.dot(activated, full_fc2, preferred_element_type=jnp.float32) + offsets[5]
    output = (hidden_state + branch_two * gains[3] * query_mask).astype(jnp.bfloat16)
    back_qkv, back_proj, back_fc1, back_fc2, back_gains = (
        full_qkv,
        full_proj,
        full_fc1,
        full_fc2,
        gains,
    )
    grad_out = cotangent.astype(jnp.float32)
    layer_gain_two = token_sum(grad_out * query_mask * branch_two)
    grad_branch_two = (grad_out * back_gains[3] * query_mask).astype(jnp.bfloat16)
    shift_five = token_sum(grad_branch_two.astype(jnp.float32))
    grad_fc2 = jnp.einsum(
        "spf,spd->fd", activated, grad_branch_two, preferred_element_type=jnp.float32
    )
    grad_act = jnp.einsum(
        "spd,fd->spf", grad_branch_two, back_fc2, preferred_element_type=jnp.float32
    )
    grad_pre = (grad_act * gelu_slope(pre_act)).astype(jnp.bfloat16)
    grad_hidden_bias = token_sum(grad_pre.astype(jnp.float32))
    grad_fc1 = jnp.einsum("spd,spf->df", normed_two, grad_pre, preferred_element_type=jnp.float32)
    grad_normed_two = jnp.einsum(
        "spf,df->spd", grad_pre, back_fc1, preferred_element_type=jnp.float32
    )
    norm_gain_two = token_sum(grad_normed_two * unit_two)
    norm_shift_two = token_sum(grad_normed_two)
    grad_hidden = grad_out + norm_back(grad_normed_two, unit_two, inverse_two, back_gains[2])
    layer_gain_one = token_sum(grad_hidden * query_mask * branch_one)
    grad_branch_one = (grad_hidden * back_gains[1] * query_mask).astype(jnp.bfloat16)
    shift_proj = token_sum(grad_branch_one.astype(jnp.float32))
    grad_proj = jnp.einsum(
        "spd,spe->de", mixed, grad_branch_one, preferred_element_type=jnp.float32
    )
    grad_mixed = jnp.einsum(
        "spe,de->spd", grad_branch_one, back_proj, preferred_element_type=jnp.float32
    )
    grad_mixed = grad_mixed.astype(jnp.bfloat16)
    grad_attended = lax.all_to_all(
        grad_mixed, "seq", split_axis=2, concat_axis=1, tiled=True
    ).reshape(head_shape)
    probs = jnp.exp(scores_of() - log_total)
    probs_again = probs.astype(jnp.bfloat16)
    grad_probs = jnp.einsum(
        "bqhe,bkhe->bhqk", grad_attended, value_heads, preferred_element_type=jnp.float32
    )
    row_dot = jnp.sum(grad_probs * probs, axis=-1, keepdims=True)
    grad_scores = (probs * (grad_probs - row_dot)).astype(jnp.bfloat16)
    flat_shape = (slot_count, seq_total, part_width)
    grad_query = (
        jnp.einsum("bhqk,bkhe->bqhe", grad_scores, key_heads, preferred_element_type=jnp.float32)
        * factor
    )
    grad_key = (
        jnp.einsum("bhqk,bqhe->bkhe", grad_scores, query_heads, preferred_element_type=jnp.float32)
        * factor
    )
    grad_value = jnp.einsum(
        "bhqk,bqhe->bkhe", probs_again, grad_attended, preferred_element_type=jnp.float32
    )
    grad_query = grad_query.astype(jnp.bfloat16).reshape(flat_shape)
    grad_key = grad_key.astype(jnp.bfloat16).reshape(flat_shape)
    grad_value = grad_value.astype(jnp.bfloat16).reshape(flat_shape)
    token_query, token_key, token_value = (
        lax.all_to_all(grad_query, "seq", split_axis=1, concat_axis=2, tiled=True),
        lax.all_to_all(grad_key, "seq", split_axis=1, concat_axis=2, tiled=True),
        lax.all_to_all(grad_value, "seq", split_axis=1, concat_axis=2, tiled=True),
    )
    grad_joined = jnp.concatenate([token_query, token_key, token_value], axis=2)
    grad_qkv = jnp.einsum(
        "spd,spe->de", normed_one, grad_joined, preferred_element_type=jnp.float32
    )
    grad_normed_one = jnp.einsum(
        "spe,de->spd", grad_joined, back_qkv, preferred_element_type=jnp.float32
    )
    norm_gain_one = token_sum(grad_normed_one * unit_one)
    norm_shift_one = token_sum(grad_normed_one)
    grad_input = (
        grad_hidden + norm_back(grad_normed_one, unit_one, inverse_one, back_gains[0])
    ).astype(jnp.bfloat16)
    gain_terms = jnp.stack([norm_gain_one, layer_gain_one, norm_gain_two, layer_gain_two])
    shift_terms = jnp.stack(
        [
            norm_shift_one,
            token_sum(token_query.astype(jnp.float32)),
            token_sum(token_value.astype(jnp.float32)),
            shift_proj,
            norm_shift_two,
            shift_five,
        ]
    )
    shares = (
        lax.psum_scatter(
            grad_qkv.astype(jnp.bfloat16), "dp", scatter_dimension=0, tiled=True
        ).astype(jnp.float32),
        lax.psum_scatter(
            grad_proj.astype(jnp.bfloat16), "dp", scatter_dimension=0, tiled=True
        ).astype(jnp.float32),
        lax.psum_scatter(
            grad_fc1.astype(jnp.bfloat16), "dp", scatter_dimension=0, tiled=True
        ).astype(jnp.float32),
        lax.psum_scatter(
            grad_fc2.astype(jnp.bfloat16), "dp", scatter_dimension=0, tiled=True
        ).astype(jnp.float32),
        lax.psum_scatter(
            grad_hidden_bias.astype(jnp.bfloat16), "dp", scatter_dimension=0, tiled=True
        ).astype(jnp.float32),
        lax.psum_scatter(
            gain_terms.astype(jnp.bfloat16), "dp", scatter_dimension=1, tiled=True
        ).astype(jnp.float32),
        lax.psum_scatter(
            shift_terms.astype(jnp.bfloat16), "dp", scatter_dimension=1, tiled=True
        ).astype(jnp.float32),
    )
    totals = (
        lax.psum(shares[0].astype(jnp.bfloat16), "seq").astype(jnp.float32),
        lax.psum(shares[1].astype(jnp.bfloat16), "seq").astype(jnp.float32),
        lax.psum(shares[2].astype(jnp.bfloat16), "seq").astype(jnp.float32),
        lax.psum(shares[3].astype(jnp.bfloat16), "seq").astype(jnp.float32),
        lax.psum(shares[4].astype(jnp.bfloat16), "seq").astype(jnp.float32),
        lax.psum(shares[5].astype(jnp.bfloat16), "seq").astype(jnp.float32),
        lax.psum(shares[6].astype(jnp.bfloat16), "seq").astype(jnp.float32),
    )
    return (
        output,
        grad_input,
        totals[0],
        totals[1],
        totals[2],
        totals[3],
        totals[4],
        totals[5],
        totals[6],
    )


CORE, ALONG_X, ALONG_Y = 1, 2, 4
NEGATIVE = -1e30


def swap(values, bit):
    size = lax.axis_size("dp")
    return lax.ppermute(values, "dp", [(i, i ^ bit) for i in range(size)])


def after(values, *earlier):
    return lax.optimization_barrier((values, earlier))[0]


def place():
    index = lax.axis_index("dp")
    return index % 2, (index // 2) % 2, index // 4


def joined(mine, theirs, bit, axis):
    low = jnp.where(bit == 0, mine, theirs)
    high = jnp.where(bit == 0, theirs, mine)
    return jnp.concatenate([low, high], axis=axis)


def local_call(kernel, outs, position, *arrays, scratch=(), room=40, outside=(), copies=0):
    return pl.pallas_call(
        kernel,
        out_shape=[jax.ShapeDtypeStruct(shape, kind) for shape, kind in outs],
        in_specs=[pl.BlockSpec(memory_space=pltpu.SMEM)]
        + [
            pl.BlockSpec(memory_space=pl.ANY if n in outside else pltpu.VMEM)
            for n in range(len(arrays))
        ],
        out_specs=[pl.BlockSpec(memory_space=pltpu.VMEM)] * len(outs),
        scratch_shapes=[pltpu.VMEM(shape, kind) for shape, kind in scratch]
        + [pltpu.SemaphoreType.DMA((copies,))] * (copies > 0),
        compiler_params=pltpu.CompilerParams(vmem_limit_bytes=room * 1024 * 1024),
        cost_estimate=pl.CostEstimate(flops=1 << 20, bytes_accessed=1 << 16, transcendentals=0),
    )(position, *arrays)


def start_copies(pairs, semaphores):
    started = []
    for n, (source, target) in enumerate(pairs):
        started.append(pltpu.make_async_copy(source, target, semaphores.at[n]))
        started[-1].start()
    return started


def cut_kernel(count, qkv, fc1, proj, scales, shifts, bias, pad_mask, mine, give, semaphores):
    own = lax.rem(lax.axis_index("dp"), 2)
    pairs = []
    for out, core in ((give, 1 - own), (mine, own)):
        for j in range(12):
            column = pl.multiple_of((2 * j + core) * 128, 128)
            pairs.append((qkv.at[:, pl.ds(column, 128)], out.at[:, pl.ds(j * 128, 128)]))
        for j in range(4):
            column = pl.multiple_of((2 * j + core) * 512, 512)
            pairs.append((fc1.at[:, pl.ds(column, 512)], out.at[:, pl.ds(1664 + j * 512, 512)]))
    pairs.append((proj.at[:, pl.ds(0, 512)], mine.at[:, pl.ds(3712, 512)]))
    started = start_copies(pairs, semaphores)
    wide = [item[...].astype(jnp.float32) for item in (scales, shifts, bias)]
    small = jnp.concatenate(wide + [jnp.zeros((114, 128), jnp.float32)], axis=0)
    slot = lax.broadcasted_iota(jnp.int32, pad_mask.shape, 0)
    mask = jnp.where(slot < count[0], pad_mask[...], 0).astype(jnp.float32)
    masks = [mask[:, j * 128 : j * 128 + 128] for j in range(mask.shape[1] // 128)]
    masks = jnp.concatenate(masks + [jnp.zeros((120, 128), jnp.float32)], axis=0)
    mine[:, pl.ds(1536, 128)] = small.astype(jnp.bfloat16)
    give[:, pl.ds(1536, 128)] = small.astype(jnp.bfloat16)
    give[:, pl.ds(3712, 128)] = masks.astype(jnp.bfloat16)
    for copy in started:
        copy.wait()


def chips_of(pos):
    chip = 2 * pos[2] + pos[1]
    along_x = 2 * pos[2] + 1 - pos[1]
    along_y = 2 * (1 - pos[2]) + pos[1]
    across = 2 * (1 - pos[2]) + 1 - pos[1]
    return (chip, along_x, along_y, across), (chip, along_y, along_x, across)


def dot_of(left, right, left_dim, right_dim):
    return lax.dot_general(
        left, right, (((left_dim,), (right_dim,)), ((), ())), preferred_element_type=jnp.float32
    )


def low(values):
    return values.astype(jnp.bfloat16)


def wide(values):
    return values.astype(jnp.float32)


def down(values):
    return jnp.sum(values, axis=0, keepdims=True)


def unit_of(values):
    centred = values - jnp.mean(values, axis=1, keepdims=True)
    inverse = lax.rsqrt(jnp.mean(centred * centred, axis=1, keepdims=True) + EPSILON)
    return centred * inverse, inverse


def row_blocks(count, size=128):
    return [pl.ds(n * size, size) for n in range(count // size)]


def join_parts(pos, owners, near_a, far_a, near_b, far_b):
    for part, chips, near, far in zip((0, 1), chips_of(pos), (near_a, near_b), (far_a, far_b)):
        for n in range(4):
            yield part, chips[n], owners[part], (near, far)[n // 2], n % 2


def front_kernel(
    pos, mine, theirs, near_a, far_a, near_b, far_b, mask, gate,
    weight, vectors, bias, inputs, grad_out, grad_two, normed, qkv, attended,
):
    core = pos[0]
    for part, chip, owner, block, n in join_parts(
        pos, (core, 1 - core), near_a, far_a, near_b, far_b
    ):
        row = pl.multiple_of((2 * chip + owner) * 128, 128)
        weight[pl.ds(row, 128), :] = block[pl.ds(n * 128, 128), pl.ds(0, 1536)]
        small = wide(block[pl.ds(n * 128, 16), pl.ds(1536, 128)])
        vectors[:, pl.ds(row, 128)] = small
        if part == 0:
            for j in range(4):
                column = pl.multiple_of(chip * 512 + j * 128, 128)
                bias[:, pl.ds(column, 128)] = small[10 + j : 11 + j]
    half = mine.shape[0] // 2
    piece = half // 2
    for there, block in ((core, mine), (1 - core, theirs)):
        for turn in range(2):
            first = there * half + lax.rem(pos[3] + turn, 2) * piece
            rows = pl.ds(pl.multiple_of(first, piece), piece)
            inputs[rows, :] = block[pl.ds(turn * half, piece), :]
            grad_out[rows, :] = block[pl.ds(turn * half + piece, piece), :]
    for rows in row_blocks(2 * half):
        unit, _ = unit_of(wide(inputs[rows, :]))
        normed[rows, :] = low(unit * vectors[0:1, :] + vectors[4:5, :])
        grad_two[rows, :] = low(wide(grad_out[rows, :]) * vectors[3:4, :] * gate[rows, :])
    for kind, shift in enumerate((5, None, 6)):
        made = dot_of(normed[...], weight[:, pl.ds(kind * 512, 512)], 1, 0)
        for chip in range(4):
            piece = made[:, chip * 128 : chip * 128 + 128]
            if shift is not None:
                column = pl.multiple_of((2 * chip + core) * 128, 128)
                piece = piece + vectors[shift : shift + 1, pl.ds(column, 128)]
            qkv[:, pl.ds(kind * 512 + chip * 128, 128)] = low(piece)
    lane = lax.broadcasted_iota(jnp.int32, (2 * half, 128), 1)
    live = mask[...] > 0
    for pair in range(4):
        query = qkv[:, pl.ds(pair * 128, 128)] * jnp.bfloat16(HD ** (-0.5))
        key = qkv[:, pl.ds(512 + pair * 128, 128)]
        value = qkv[:, pl.ds(1024 + pair * 128, 128)]
        got = []
        for head in range(2):
            chosen = (lane // HD) == head
            scores = dot_of(jnp.where(chosen, query, jnp.zeros_like(query)), key, 1, 1)
            scores = jnp.where(live, scores, NEGATIVE)
            expo = jnp.exp(scores - jnp.max(scores, axis=1, keepdims=True))
            probs = expo * (1.0 / jnp.sum(expo, axis=1, keepdims=True))
            got.append(dot_of(low(probs), value, 1, 0))
        attended[:, pl.ds(pair * 128, 128)] = low(jnp.where(lane < HD, got[0], got[1]))


def put_halves(values, tile, upper, lower):
    half = values.shape[0] // 2
    upper[:, tile] = low(values[:half])
    lower[:, tile] = low(values[half:])


def of_halves(upper, lower, n, size=128):
    count = upper.shape[0] // size
    return wide((upper, lower)[n // count][pl.ds((n % count) * size, size), :])


def proj_kernel(
    pos, attended, near_a, far_a, near_b, far_b, proj, upper, lower, semaphores
):
    pairs = []
    for part, chip, _, block, n in join_parts(pos, (0, 0), near_a, far_a, near_b, far_b):
        row = pl.multiple_of(chip * 128, 128)
        target = proj.at[pl.ds(row, 128), pl.ds(part * 512, 512)]
        pairs.append((block.at[pl.ds(n * 128, 128), pl.ds(2048, 512)], target))
    for copy in start_copies(pairs, semaphores):
        copy.wait()
    for tile in row_blocks(1024, 256):
        put_halves(dot_of(attended[...], proj[:, tile], 1, 0), tile, upper, lower)


def far_chips(pos):
    return (1 - pos[1], 3 - pos[1]), (2 * (1 - pos[2]), 2 * (1 - pos[2]) + 1)


def second_chips(pos):
    own = 2 * pos[2] + pos[1]
    over_y = 2 * (1 - pos[2]) + pos[1]
    over_x = 2 * pos[2] + 1 - pos[1]
    return ((own, pos[2]), (over_y, 1 - pos[2])), ((own, pos[1]), (over_x, 1 - pos[1]))


def chip_columns(ref, chip, count):
    return ref[:, pl.ds(pl.multiple_of(chip * count, count), count)]


def far_products(pos, left, right, outs):
    rows = left.shape[1] // 4
    cut = right.shape[1] // 2
    for part, chips in enumerate(far_chips(pos)):
        for n in range(2):
            made = dot_of(
                chip_columns(left, chips[n], rows), right[:, pl.ds(part * cut, cut)], 0, 0
            )
            outs[part][pl.ds(n * rows, rows), :] = low(made)


def fc1_copies(pos, near_a, far_a, near_b, far_b, fc1):
    pairs = []
    for _, chip, owner, block, n in join_parts(
        pos, (pos[0], 1 - pos[0]), near_a, far_a, near_b, far_b
    ):
        row = pl.multiple_of((2 * chip + owner) * 128, 128)
        source = block.at[pl.ds(n * 128, 128), pl.ds(0, 2048)]
        pairs.append((source, fc1.at[pl.ds(row, 128), :]))
    return pairs


def middle_kernel(
    pos, inputs, own_upper, own_lower, upper, lower, vectors, bias, gate, near_a, far_a, near_b,
    far_b, grad_two, hidden, normed, slope, activated, out_a, out_b, fc1, semaphores,
):
    pairs = fc1_copies(pos, near_a, far_a, near_b, far_b, fc1)
    started = start_copies(pairs, semaphores)
    for n, rows in enumerate(row_blocks(inputs.shape[0])):
        made = of_halves(own_upper, own_lower, n) + of_halves(upper, lower, n) + vectors[7:8, :]
        state = wide(inputs[rows, :]) + made * vectors[1:2, :] * gate[rows, :]
        hidden[rows, :] = state
        unit, _ = unit_of(state)
        normed[rows, :] = low(unit * vectors[2:3, :] + vectors[8:9, :])
    for copy in started:
        copy.wait()

    def units(n, _):
        tile = pl.ds(pl.multiple_of(n * 256, 256), 256)
        pre = dot_of(normed[...], fc1[:, tile], 1, 0) + bias[:, tile]
        bell = 0.5 * (1.0 + lax.erf(pre * ROOT_HALF))
        activated[:, tile] = low(pre * bell)
        slope[:, tile] = low(bell + pre * jnp.exp(-0.5 * pre * pre) * INV_ROOT_TWO_PI)
        return 0

    lax.fori_loop(0, 8, units, 0)
    far_products(pos, activated, grad_two, (out_a, out_b))


def units_back_kernel(
    pos, near_a, far_a, near_b, far_b, grad_two, slope, activated, normed,
    fc1_near_a, fc1_far_a, fc1_near_b, fc1_far_b,
    grad_pre, sums, partial, upper, lower, out_a, out_b, branch, branch_low, fc2, fc1, semaphores,
):
    started = start_copies(
        fc1_copies(pos, fc1_near_a, fc1_far_a, fc1_near_b, fc1_far_b, fc1), semaphores
    )
    for part, chip, _, block, n in join_parts(pos, (0, 0), near_a, far_a, near_b, far_b):
        row = pl.multiple_of(chip * 512 + part * 256, 256)
        fc2[pl.ds(row, 256), :] = block[pl.ds(n * 256, 256), :]

    def units(n, _):
        tile = pl.ds(pl.multiple_of(n * 256, 256), 256)
        made = low(dot_of(grad_two[...], fc2[tile, :], 1, 1) * wide(slope[:, tile]))
        grad_pre[:, tile] = made
        sums[:, tile] = down(wide(made))
        return 0

    lax.fori_loop(0, 8, units, 0)
    for copy in started:
        copy.wait()
    for tile in row_blocks(1024, 256):
        made = dot_of(grad_pre[...], fc1[tile, :], 1, 1)
        partial[:, tile] = made
        put_halves(made, tile, upper, lower)
    far_products(pos, normed, grad_pre, (out_a, out_b))
    half = branch.shape[0]
    mine = pl.ds(pl.multiple_of(pos[0] * half, half), half)
    theirs = pl.ds(pl.multiple_of((1 - pos[0]) * half, half), half)
    for tile in row_blocks(1024, 256):
        branch[:, tile] = dot_of(activated[mine, :], fc2[:, tile], 1, 0)
        branch_low[:, tile] = low(dot_of(activated[theirs, :], fc2[:, tile], 1, 0))


def proj_product(attended, grad_one, chip, part):
    return dot_of(chip_columns(attended, chip, 128), grad_one[:, pl.ds(part * 512, 512)], 0, 0)


def norm_back_kernel(
    pos, grad_out, partial, upper, lower, hidden, own_upper, own_lower, their_upper, their_lower,
    vectors, gate, proj, attended,
    fc1_a, fc1_b, grad_hidden, grad_one, grad_attended, sums, far_a, far_b,
):
    total = [0.0] * 4
    for n, rows in enumerate(row_blocks(hidden.shape[0])):
        grad = partial[rows, :] + of_halves(upper, lower, n)
        unit, inverse = unit_of(hidden[rows, :])
        state = wide(grad_out[rows, :]) + norm_back(grad, unit, inverse, vectors[2:3, :])
        grad_hidden[rows, :] = state
        gated = state * gate[rows, :]
        made = low(gated * vectors[1:2, :])
        grad_one[rows, :] = made
        branch = of_halves(own_upper, own_lower, n) + of_halves(their_upper, their_lower, n)
        terms = (gated * (branch + vectors[7:8, :]), grad * unit, wide(made), grad)
        total = [one + down(term) for one, term in zip(total, terms)]
    for n in range(4):
        sums[n : n + 1, :] = total[n]
    grad_attended[...] = low(dot_of(grad_one[...], proj[...], 1, 1))
    for part, chips in enumerate(far_chips(pos)):
        out = (far_a, far_b)[part]
        out[pl.ds(0, 512), :] = (fc1_a, fc1_b)[part][...]
        for n in range(2):
            made = low(proj_product(attended, grad_one, chips[n], part))
            here = pl.ds(512 + n * 64, 64)
            out[here, pl.ds(0, 512)] = made[:64]
            out[here, pl.ds(512, 512)] = made[64:]


def fold_kernel(pos, left, right, got_a, got_b, keep_a, give_a, keep_b, give_b):
    rows = left.shape[1] // 4
    cut = right.shape[1] // 2
    outs = ((keep_a, give_a), (keep_b, give_b))
    for part, chips in enumerate(second_chips(pos)):
        for n in range(2):
            chip, arrived = chips[n]
            made = dot_of(chip_columns(left, chip, rows), right[:, pl.ds(part * cut, cut)], 0, 0)
            there = pl.ds(pl.multiple_of(arrived * rows, rows), rows)
            outs[part][n][...] = low(made + wide((got_a, got_b)[part][there, :]))


def fc1_fold_kernel(
    pos, left, right, attended, grad_one, small, got_a, got_b, keep_a, give_a, keep_b, give_b
):
    outs = ((keep_a, give_a), (keep_b, give_b))
    for part, chips in enumerate(second_chips(pos)):
        got = (got_a, got_b)[part]
        for n in range(2):
            chip, arrived = chips[n]
            out = outs[part][n]
            made = dot_of(chip_columns(left, chip, 256), right[:, pl.ds(part * 1024, 1024)], 0, 0)
            there = pl.ds(pl.multiple_of(arrived * 256, 256), 256)
            out[pl.ds(0, 256), :] = low(made + wide(got[there, :]))
            made = proj_product(attended, grad_one, chip, part)
            there = pl.ds(pl.multiple_of(512 + arrived * 64, 64), 64)
            arrived_rows = wide(got[there, :])
            here = pl.ds(256, 64)
            out[here, pl.ds(0, 512)] = low(made[:64] + arrived_rows[:, :512])
            out[here, pl.ds(512, 512)] = low(made[64:] + arrived_rows[:, 512:])
    give_b[pl.ds(320, 16), :] = small[...]


def attend_back_kernel(
    pos, qkv, mask, grad, normed, out, sums, far_a, far_b
):
    length = qkv.shape[0]
    lane = lax.broadcasted_iota(jnp.int32, (length, 128), 1)
    live = mask[...] > 0
    factor = HD ** (-0.5)
    for pair in range(4):
        spans = [pl.ds(offset + pair * 128, 128) for offset in (0, 512, 1024)]
        query, key, value = (qkv[:, span] for span in spans)
        grad_pair = grad[:, pl.ds(pair * 128, 128)]
        grad_query, grad_key, grad_value = [], 0.0, 0.0
        for head in range(2):
            chosen = (lane // HD) == head
            query_one = jnp.where(chosen, query, jnp.zeros_like(query))
            grad_head = jnp.where(chosen, grad_pair, jnp.zeros_like(grad_pair))
            scores = dot_of(key, query_one, 1, 1) * factor
            scores = jnp.where(live, scores, NEGATIVE)
            expo = jnp.exp(scores - jnp.max(scores, axis=0, keepdims=True))
            probs = expo * (1.0 / jnp.sum(expo, axis=0, keepdims=True))
            grad_probs = dot_of(value, grad_head, 1, 1)
            along = jnp.sum(grad_probs * probs, axis=0, keepdims=True)
            grad_scores = low(probs * (grad_probs - along))
            grad_value += dot_of(low(probs), grad_head, 1, 0)
            grad_key += dot_of(grad_scores, query_one, 1, 0)
            grad_query.append(dot_of(grad_scores, key, 0, 0))
        made = jnp.where(lane < HD, grad_query[0], grad_query[1]) * factor
        for span, item in zip(spans, (made, grad_key * factor, grad_value)):
            item = low(item)
            out[:, span] = item
            sums[:, span] = down(wide(item))
    far_products(pos, normed, out, (far_a, far_b))


def last_fold_kernel(
    pos, normed, grad_qkv, got_a, got_b, small, small_got, keep_a, give_a, keep_b, give_b
):
    outs = ((keep_a, give_a), (keep_b, give_b))
    for part, chips in enumerate(second_chips(pos)):
        for n in range(2):
            chip, arrived = chips[n]
            made = dot_of(
                chip_columns(normed, chip, 256), grad_qkv[:, pl.ds(part * 768, 768)], 0, 0
            )
            there = pl.ds(pl.multiple_of(arrived * 256, 256), 256)
            outs[part][n][pl.ds(0, 256), :] = low(made + wide((got_a, got_b)[part][there, :]))
    for out, at_y in ((keep_a, pos[2]), (give_a, 1 - pos[2])):
        column = pl.multiple_of(at_y * 128, 128)
        sums = small[at_y] + wide(small_got[:, pl.ds(column, 128)])
        out[pl.ds(256, 32), :] = jnp.zeros((32, 768), jnp.bfloat16)
        out[pl.ds(256, 16), pl.ds(0, 128)] = low(sums)


def first_back_kernel(pos, grad_qkv, weight, last, partial, upper, lower):
    half = lower.shape[0]
    for tile in row_blocks(1024, 256):
        made = dot_of(grad_qkv[...], weight[tile, :], 1, 1)
        partial[:, tile] = made
        upper[pl.ds(0, half), tile] = low(made[:half])
        lower[:, tile] = low(made[half:])
    upper[pl.ds(half, 16), :] = low(jnp.broadcast_to(last[0:1, :], (16, 1024)))


def inputs_back_kernel(
    pos, inputs, partial, upper, lower, grad_hidden, vectors, out, sums, grads
):
    total = [0.0] * 2
    half = out.shape[0]
    for n, rows in enumerate(row_blocks(2 * half)):
        there = (upper, lower)[n * 128 // half]
        grad = partial[rows, :] + wide(there[pl.ds((n * 128) % half, 128), :])
        grads[rows, :] = grad
        unit, _ = unit_of(wide(inputs[rows, :]))
        total = [one + down(term) for one, term in zip(total, (grad * unit, grad))]
    for n in range(2):
        sums[n : n + 1, :] = total[n]
    sums[2:3, :] = wide(upper[pl.ds(half, 16), :])[0:1]
    for n in range(half // 128):
        rows = pl.ds(pl.multiple_of(pos[0] * half + n * 128, 128), 128)
        unit, inverse = unit_of(wide(inputs[rows, :]))
        state = grad_hidden[rows, :] + norm_back(grads[rows, :], unit, inverse, vectors[0:1, :])
        out[pl.ds(n * 128, 128), :] = low(state)


def output_kernel(
    pos, hidden, branch, other, vectors, gate, grad_out, grad_two, out, sums
):
    half = out.shape[0]
    gain_sum, shift_sum = 0.0, 0.0
    for n in range(half // 128):
        here = pl.ds(n * 128, 128)
        rows = pl.ds(pl.multiple_of(pos[0] * half + n * 128, 128), 128)
        made = branch[here, :] + wide(other[here, :]) + vectors[9:10, :]
        out[here, :] = low(hidden[rows, :] + made * vectors[3:4, :] * gate[rows, :])
        gain_sum += down(wide(grad_out[rows, :]) * gate[rows, :] * made)
    for rows in row_blocks(2 * half):
        shift_sum += down(wide(grad_two[rows, :]))
    sums[0:1, :] = gain_sum
    sums[1:2, :] = shift_sum


def small_kernel(pos, first, second, last, attention, units, keep, give):
    core = pos[0]
    order = [(first, 0), (second, 0), (second, 1), (last, 0), (first, 1)]
    order += [None, None, (second, 2), (second, 3), (last, 1)]
    give[...] = jnp.zeros_like(give)
    for at_y in range(2):
        for over in range(2):
            chip = 2 * at_y + (pos[1] if over == 0 else 1 - pos[1])
            own = pl.ds(pl.multiple_of((2 * chip + core) * 128, 128), 128)
            here = pl.multiple_of(chip * 128, 128)
            lines = [None if item is None else item[0][item[1] : item[1] + 1, own] for item in order]
            lines[3] = lines[3] + first[2:3, own]
            lines[5] = attention[:, pl.ds(here, 128)]
            lines[6] = attention[:, pl.ds(pl.multiple_of(1024 + chip * 128, 128), 128)]
            for j in range(4):
                column = pl.multiple_of(chip * 512 + j * 128, 128)
                lines.append(units[:, pl.ds(column, 128)])
            block = jnp.concatenate(lines + [jnp.zeros((2, 128), jnp.float32)], axis=0)
            if over == 0:
                keep[at_y, :, :] = block
            else:
                give[:, pl.ds(at_y * 128, 128)] = low(block)


def finish_qkv_kernel(pos, mine, theirs, out):
    core = pos[0]
    rows = pl.ds(pl.multiple_of(core * 128, 128), 128)
    for j in range(12):
        here = pl.ds(j * 128, 128)
        out[:, pl.ds(pl.multiple_of((2 * j + core) * 128, 128), 128)] = wide(mine[rows, here])
        out[:, pl.ds(pl.multiple_of((2 * j + 1 - core) * 128, 128), 128)] = wide(theirs[:, here])


def finish_fc1_kernel(pos, mine, theirs, out):
    core = pos[0]
    rows = pl.ds(pl.multiple_of(core * 128, 128), 128)
    for j in range(4):
        here = pl.ds(j * 512, 512)
        out[:, pl.ds(pl.multiple_of((2 * j + core) * 512, 512), 512)] = wide(mine[rows, here])
        out[:, pl.ds(pl.multiple_of((2 * j + 1 - core) * 512, 512), 512)] = wide(theirs[:, here])


def add_low(one, two):
    return (one.astype(jnp.float32) + two.astype(jnp.float32)).astype(jnp.bfloat16)


def line_in(values):
    return lax.ppermute(values, "seq", [(0, 1), (3, 2)])


def line_mid(values):
    return lax.ppermute(values, "seq", [(1, 2), (2, 1)])


def line_out(values):
    return lax.ppermute(values, "seq", [(1, 0), (2, 3)])


def inner():
    at_z = lax.axis_index("seq")
    return ((at_z == 1) | (at_z == 2)).astype(jnp.int32)


def image_moves(back):
    seq = lax.axis_size("seq")
    rounds = []
    for turn in range(2):
        moves = []
        for chip in range(lax.axis_size("dp") // 2):
            for core in range(2):
                for quarter in range(seq):
                    slot = (quarter + turn) % 2
                    source = (2 * chip + core) * seq + quarter
                    target = (2 * chip + quarter // 2) * seq + 2 * core + slot
                    moves.append((target, source) if back else (source, target))
        rounds.append(moves)
    return rounds


def to_images(first, second, *earlier):
    at_z = lax.axis_index("seq")
    first, second = after((first, second), *earlier)
    got = []
    for turn, moves in enumerate(image_moves(False)):
        slot = (at_z + turn) % 2
        sent = [lax.dynamic_index_in_dim(item, slot, 0, False) for item in (first, second)]
        got.append(lax.ppermute(jnp.concatenate(sent, axis=0), ("dp", "seq"), moves))
    return jnp.concatenate(got, axis=0)


def from_images(values):
    at_z = lax.axis_index("seq")
    pieces = values.reshape(2, values.shape[0] // 2, values.shape[1])
    got = []
    for turn, moves in enumerate(image_moves(True)):
        sent = lax.dynamic_index_in_dim(pieces, (at_z + turn) % 2, 0, False)
        got.append(lax.ppermute(sent, ("dp", "seq"), moves))
    return got


def slots_of(got):
    even = lax.axis_index("seq") % 2 == 0
    return jnp.stack([jnp.where(even, got[0], got[1]), jnp.where(even, got[1], got[0])])


def image_plan(
    tokens, group_count, pad_mask, w_qkv, w_proj, w_fc1, w_fc2, fc1_bias, scales, shifts, cotangent
):
    slot_count, _, width = tokens.shape
    length = pad_mask.shape[1]
    half = length // 2
    f32, bf16 = jnp.float32, jnp.bfloat16
    core, at_x, at_y = place()
    at_z = lax.axis_index("seq")
    pos = jnp.stack([core, at_x, at_y, at_z]).astype(jnp.int32)

    alive = jnp.arange(slot_count, dtype=jnp.int32) < group_count[0]
    mask_own = jnp.where(alive[:, None], pad_mask, 0).astype(f32)
    mine, give = local_call(
        cut_kernel, [((128, 4224), bf16), ((128, 3840), bf16)],
        group_count, w_qkv, w_fc1, w_proj, scales, shifts, fc1_bias.reshape(4, 128), pad_mask, room=56,
        outside=(0, 1, 2), copies=33,
    )
    got = swap(give, CORE)
    blocks = (mine, jnp.concatenate([got[:, :3712], w_proj[:, 512:]], axis=1))
    mask_both = joined(
        mask_own,
        got[:8, 3712:].reshape(4, slot_count, 128).transpose(1, 0, 2).reshape(
            slot_count, length
        ).astype(f32),
        core, 0,
    )
    mask_row = lax.dynamic_index_in_dim(mask_both, at_z, 0, False)
    token_gate = mask_row[:, None]

    def links(sent, order=(ALONG_X, ALONG_Y)):
        return swap(sent[0], order[0]), swap(sent[1], order[1])

    def second_link(blocks, got):
        near_a, near_b = (jnp.concatenate(pair, axis=0) for pair in zip(blocks, got))
        far_a, far_b = links((near_a, near_b), (ALONG_Y, ALONG_X))
        return near_a, far_a, near_b, far_b

    def lanes(pair, start, stop):
        return [item[:, start:stop] for item in pair]

    first = links(blocks)
    fc2_rows = after(w_fc2, blocks[1])
    fc2_blocks = (fc2_rows[:256], fc2_rows[256:])
    fc2_first = links(fc2_blocks)
    both = to_images(tokens, cotangent, blocks[1])
    qkv_parts = second_link(lanes(blocks, 0, 1664), lanes(first, 0, 1664))
    first = after(first, qkv_parts[0], qkv_parts[2])
    fc1_parts = second_link(lanes(blocks, 1664, 4224), lanes(first, 1664, 4224))
    fc2_parts = second_link(fc2_blocks, after(fc2_first, fc1_parts[0], fc1_parts[2]))

    full = (length, width)
    qkv_w, vectors, bias, inputs, grad_out, grad_two, normed_one, qkv, attended = local_call(
        front_kernel,
        [
            ((width, 1536), bf16), ((16, width), f32), ((1, 2048), f32), (full, bf16),
            (full, bf16), (full, bf16), (full, bf16), ((length, 1536), bf16),
            ((length, 512), bf16),
        ],
        pos, both, swap(both, CORE), *after(qkv_parts, fc2_parts[0], fc2_parts[2]),
        mask_row[None, :], token_gate, room=24,
    )
    halves = [((half, width), bf16)] * 2
    proj_w, *one_own = local_call(
        proj_kernel, [((512, width), bf16)] + halves,
        pos, attended, *fc1_parts, room=14, outside=(1, 2, 3, 4), copies=8,
    )
    one_other = [swap(item, CORE) for item in one_own]
    hidden, normed_two, slope, activated, far_a, far_b = local_call(
        middle_kernel,
        [
            (full, f32), (full, bf16), ((length, 2048), bf16), ((length, 2048), bf16),
            ((1024, 512), bf16), ((1024, 512), bf16),
        ],
        pos, inputs, *one_own, *one_other, vectors, bias, token_gate, *fc1_parts, grad_two,
        scratch=[((width, 2048), bf16)], room=30, outside=(8, 9, 10, 11), copies=8,
    )

    def fold(left, right, got, *earlier):
        block = (left.shape[1] // 4, right.shape[1] // 2)
        got_a, got_b = after(got, *earlier)
        keep_a, give_a, keep_b, give_b = local_call(
            fold_kernel, [(block, bf16)] * 4, pos, left, right, got_a, got_b, room=14,
    )
        return (keep_a, keep_b), (give_a, give_b)

    def half_of(keep, got):
        return [add_low(one, two) for one, two in zip(keep, got)]

    fc2_got = links((far_a, far_b))
    grad_pre, unit_sums, partial, upper, lower, far_a, far_b, branch_two, branch_low = local_call(
        units_back_kernel,
        [((length, 2048), bf16), ((1, 2048), f32), (full, f32)]
        + halves
        + [((512, 1024), bf16), ((512, 1024), bf16), ((half, width), f32), ((half, width), bf16)],
        pos, *fc2_parts, grad_two, slope, activated, normed_two, *fc1_parts,
        scratch=[((2048, width), bf16), ((width, 2048), bf16)], outside=(8, 9, 10, 11), copies=8,
    )
    others = [swap(item, CORE) for item in (upper, lower)]
    branch_other = swap(branch_low, CORE)
    output, last_sums = local_call(
        output_kernel, [((half, width), bf16), ((2, width), f32)],
        pos, hidden, branch_two, branch_other, vectors, token_gate, grad_out,
        grad_two, room=14,
    )
    out_got = from_images(output)
    fc1_far = ((640, 1024), bf16)
    grad_hidden, grad_one, grad_attended, second_sums, far_a, far_b = local_call(
        norm_back_kernel,
        [
            (full, f32), (full, bf16), ((length, 512), bf16), ((4, width), f32), fc1_far, fc1_far,
        ],
        pos, grad_out, partial, *after(others, output), hidden, *one_own, *one_other, vectors,
        token_gate, proj_w, attended, far_a, far_b, room=24,
    )
    fc2_keep, fc2_give = fold(activated, grad_two, fc2_got, grad_attended, out_got[0])
    fc2_again = links(fc2_give, (ALONG_Y, ALONG_X))
    fc1_got = links(after((far_a, far_b), *fc2_give))
    grad_qkv_rows, attention_sums, far_a, far_b = local_call(
        attend_back_kernel,
        [
            ((length, 1536), bf16), ((1, 1536), f32), ((512, 768), bf16), ((512, 768), bf16),
        ],
        pos, after(qkv, *fc2_give), token_gate, grad_attended, normed_one, room=24,
    )
    fc2_half = jnp.concatenate(half_of(fc2_keep, after(fc2_again, grad_qkv_rows, out_got[1])), axis=1)
    fc2_in = line_in(fc2_half)
    partial, upper, lower = local_call(
        first_back_kernel, [(full, f32), ((half + 16, width), bf16), ((half, width), bf16)],
        pos, after(grad_qkv_rows, fc2_half), qkv_w, last_sums, room=16,
    )
    grad_input, first_sums = local_call(
        inputs_back_kernel, [((half, width), bf16), ((3, width), f32)],
        pos, inputs, partial, swap(upper, CORE), swap(lower, CORE), grad_hidden, vectors,
        scratch=[(full, f32)], room=16,
    )
    in_got = from_images(grad_input)
    small_keep, small_give = local_call(
        small_kernel, [((2, 16, 128), f32), ((16, 1024), bf16)],
        pos, first_sums, second_sums, last_sums, attention_sums, unit_sums, room=6,
    )
    fc1_block = ((320, 1024), bf16)
    keep_a, give_a, keep_b, give_b = local_call(
        fc1_fold_kernel, [fc1_block, fc1_block, fc1_block, ((336, 1024), bf16)],
        pos, normed_two, grad_pre, attended, grad_one, small_give, *fc1_got, room=20,
    )
    fc1_keep, fc1_give = (keep_a, keep_b), (give_a, give_b)
    fc1_again = links(fc1_give, (ALONG_Y, ALONG_X))
    last_got = links(after((far_a, far_b), *fc1_give))
    fc2_sum = add_low(fc2_half, after(fc2_in, *fc1_give, *in_got))
    fc2_mid = line_mid(fc2_sum)

    small_got = fc1_again[1][320:]
    fc1_again = (fc1_again[0], fc1_again[1][:320])
    fc1_half = half_of(fc1_keep, after(fc1_again, fc2_sum))
    fc1_in = [line_in(item) for item in fc1_half]
    fc2_total = add_low(fc2_sum, after(fc2_mid, *fc1_half))
    fc2_out = line_out(fc2_total)
    fc1_sum, fc1_mid, fc1_total, fc1_out = [None] * 2, [None] * 2, [None] * 2, [None] * 2
    fc1_sum[0] = add_low(fc1_half[0], after(fc1_in[0], fc2_total))
    fc1_mid[0] = line_mid(fc1_sum[0])
    last_got = after(last_got, fc1_sum[0])
    wide_block, block = ((288, 768), bf16), ((256, 768), bf16)
    keep_a, give_a, keep_b, give_b = local_call(
        last_fold_kernel, [wide_block, wide_block, block, block],
        pos, normed_one, grad_qkv_rows, *last_got, small_keep, small_got, room=16,
    )
    last_again = links((give_a, give_b), (ALONG_Y, ALONG_X))
    fc1_sum[1] = add_low(fc1_half[1], after(fc1_in[1], give_a, give_b))
    fc1_mid[1] = line_mid(fc1_sum[1])
    last_again, fc2_out = after((last_again, fc2_out), fc1_sum[1])
    last_half = half_of((keep_a, keep_b), last_again)
    last_in = [None, line_in(last_half[1])]
    fc1_total[0] = add_low(fc1_sum[0], after(fc1_mid[0], *last_half))
    fc1_out[0] = line_out(fc1_total[0])

    def line_end(total, out):
        return jnp.where(inner() == 1, total, out)

    def core_give(values):
        return lax.dynamic_slice_in_dim(values, (1 - core) * 128, 128, 0)

    fc1_total[1] = add_low(fc1_sum[1], after(fc1_mid[1], fc1_total[0]))
    fc1_out[1] = line_out(fc1_total[1])
    grad_fc2 = line_end(fc2_total, after(fc2_out, fc1_total[1])).astype(f32)
    last_sum, last_mid, last_total, last_out = [None] * 2, [None] * 2, [None] * 2, [None] * 2
    arrived, fc1_out[0] = after((last_in[1], fc1_out[0]), grad_fc2)
    last_sum[1] = add_low(last_half[1], arrived)
    last_mid[1] = line_mid(last_sum[1])
    last_in[0] = line_in(after(last_half[0], last_sum[1]))
    arrived, fc1_out[1] = after((last_in[0], fc1_out[1]), last_sum[1])
    last_sum[0] = add_low(last_half[0], arrived)
    last_mid[0] = line_mid(last_sum[0])
    last_total[1] = add_low(last_sum[1], after(last_mid[1], last_sum[0]))
    last_out[1] = line_out(last_total[1])
    fc1_rows = [line_end(*pair) for pair in zip(fc1_total, after(fc1_out, last_total[1]))]
    grad_proj = jnp.concatenate(
        [
            jnp.concatenate([item[256:, :512], item[256:, 512:]], axis=0) for item in fc1_rows
        ],
        axis=1,
    ).astype(f32)
    fc1_rows = jnp.concatenate([item[:256] for item in fc1_rows], axis=1)
    last_total[0] = add_low(last_sum[0], after(last_mid[0], fc1_rows))
    last_out[0] = line_out(last_total[0])
    (grad_fc1,) = local_call(
        finish_fc1_kernel, [((128, 4096), f32)],
        pos, fc1_rows, after(swap(core_give(fc1_rows), CORE), last_total[0]), room=10,
    )
    last_out = after(last_out, grad_fc1)
    last_rows = [line_end(*pair) for pair in zip(last_total, last_out)]
    small = last_rows[0][256:272, :128].astype(f32)
    qkv_rows = jnp.concatenate([last_rows[0][:256], last_rows[1]], axis=1)
    qkv_core = swap(core_give(qkv_rows), CORE)
    (grad_qkv,) = local_call(
        finish_qkv_kernel, [((128, 3072), f32)], pos, qkv_rows, qkv_core, room=10
    )
    grad_scales = small[:4]
    grad_shifts = small[4:10]
    grad_bias = small[10:14].reshape(512)
    return (
        slots_of(out_got),
        slots_of(in_got),
        grad_qkv,
        grad_proj,
        grad_fc1,
        grad_fc2,
        grad_bias,
        grad_scales,
        grad_shifts,
    )


def on_device(*arrays):
    tokens = arrays[0]
    whole_images = 2 * tokens.shape[0] == lax.axis_size("seq")
    if lax.axis_size("dp") == 8 and lax.axis_size("seq") == 4 and whole_images:
        return image_plan(*arrays)
    return general_plan(*arrays)


def solution(mesh):
    return jax.shard_map(
        on_device,
        mesh=mesh,
        in_specs=(
            P("dp", "seq", None),
            P("dp"),
            P("dp", None),
            P("dp", None),
            P("dp", None),
            P("dp", None),
            P("dp", None),
            P("dp"),
            P(None, "dp"),
            P(None, "dp"),
            P("dp", "seq", None),
        ),
        out_specs=(
            P("dp", "seq", None),
            P("dp", "seq", None),
            P("dp", None),
            P("dp", None),
            P("dp", None),
            P("dp", None),
            P("dp"),
            P(None, "dp"),
            P(None, "dp"),
        ),
        check_vma=False,
    )
```

```python
import jax
import jax.numpy as jnp
from jax import lax
from jax.experimental import pallas as pl
from jax.experimental.pallas import tpu as pltpu
from jax.sharding import PartitionSpec as P

HD = 64


EPSILON = 1e-06
ROOT_HALF = 0.7071067811865476
INV_ROOT_TWO_PI = 0.3989422804014327


def layer_norm(values, gain, shift):
    mean_row = jnp.mean(values, axis=-1, keepdims=True)
    centred = values - mean_row
    inverse = lax.rsqrt(jnp.mean(centred * centred, axis=-1, keepdims=True) + EPSILON)
    unit_rows = centred * inverse
    return (unit_rows * gain + shift, unit_rows, inverse)


def norm_back(grad_normed, unit_rows, inverse, gain):
    scaled = grad_normed * gain
    centre = jnp.mean(scaled, axis=-1, keepdims=True)
    along = jnp.mean(scaled * unit_rows, axis=-1, keepdims=True)
    return inverse * (scaled - centre - unit_rows * along)


def gelu_exact(values):
    return 0.5 * values * (1.0 + lax.erf(values * ROOT_HALF))


def gelu_slope(values):
    return (
        0.5 * (1.0 + lax.erf(values * ROOT_HALF))
        + values * jnp.exp(-0.5 * values * values) * INV_ROOT_TWO_PI
    )


def token_sum(values):
    return jnp.sum(values, axis=(0, 1))


def general_plan(
    tokens, group_count, pad_mask, w_qkv, w_proj, w_fc1, w_fc2, fc1_bias, scales, shifts, cotangent
):
    slot_count, piece, width = tokens.shape
    seq_total = pad_mask.shape[1]
    part_width = width // lax.axis_size("seq")
    head_count = part_width // HD
    factor = HD ** (-0.5)
    alive = jnp.arange(slot_count, dtype=jnp.int32) < group_count[0]
    key_mask = jnp.where(alive[:, None], pad_mask, 0).astype(jnp.float32)
    query_mask = lax.dynamic_slice_in_dim(key_mask, lax.axis_index("seq") * piece, piece, 1)[
        :, :, None
    ]
    full_qkv, full_proj, full_fc1, full_fc2, full_bias, full_scales, full_shifts = (
        lax.all_gather(w_qkv, "dp", axis=0, tiled=True),
        lax.all_gather(w_proj, "dp", axis=0, tiled=True),
        lax.all_gather(w_fc1, "dp", axis=0, tiled=True),
        lax.all_gather(w_fc2, "dp", axis=0, tiled=True),
        lax.all_gather(fc1_bias, "dp", axis=0, tiled=True),
        lax.all_gather(scales, "dp", axis=1, tiled=True),
        lax.all_gather(shifts, "dp", axis=1, tiled=True),
    )
    gains = full_scales.astype(jnp.float32)
    offsets = full_shifts.astype(jnp.float32)
    hidden_bias = full_bias.astype(jnp.float32)
    inputs = tokens.astype(jnp.float32)
    normed_one, unit_one, inverse_one = layer_norm(inputs, gains[0], offsets[0])
    normed_one = normed_one.astype(jnp.bfloat16)
    projected = jnp.dot(normed_one, full_qkv, preferred_element_type=jnp.float32)
    queries = (projected[:, :, :width] + offsets[1]).astype(jnp.bfloat16)
    key_rows = projected[:, :, width : 2 * width].astype(jnp.bfloat16)
    value_rows = (projected[:, :, 2 * width :] + offsets[2]).astype(jnp.bfloat16)
    head_query, head_key, head_value = (
        lax.all_to_all(queries, "seq", split_axis=2, concat_axis=1, tiled=True),
        lax.all_to_all(key_rows, "seq", split_axis=2, concat_axis=1, tiled=True),
        lax.all_to_all(value_rows, "seq", split_axis=2, concat_axis=1, tiled=True),
    )
    head_shape = (slot_count, seq_total, head_count, HD)
    query_heads = head_query.reshape(head_shape)
    key_heads = head_key.reshape(head_shape)
    value_heads = head_value.reshape(head_shape)

    def scores_of():
        raw = (
            jnp.einsum(
                "bqhe,bkhe->bhqk", query_heads, key_heads, preferred_element_type=jnp.float32
            )
            * factor
        )
        return jnp.where(key_mask[:, None, None, :] > 0, raw, -1e30)

    scores = scores_of()
    top = jnp.max(scores, axis=-1, keepdims=True)
    log_total = top + jnp.log(jnp.sum(jnp.exp(scores - top), axis=-1, keepdims=True))
    probs_low = jnp.exp(scores - log_total).astype(jnp.bfloat16)
    attended = jnp.einsum(
        "bhqk,bkhe->bqhe", probs_low, value_heads, preferred_element_type=jnp.float32
    )
    attended = attended.astype(jnp.bfloat16).reshape(slot_count, seq_total, part_width)
    mixed = lax.all_to_all(attended, "seq", split_axis=1, concat_axis=2, tiled=True)
    branch_one = jnp.dot(mixed, full_proj, preferred_element_type=jnp.float32) + offsets[3]
    hidden_state = inputs + branch_one * gains[1] * query_mask
    normed_two, unit_two, inverse_two = layer_norm(hidden_state, gains[2], offsets[4])
    normed_two = normed_two.astype(jnp.bfloat16)
    pre_act = jnp.dot(normed_two, full_fc1, preferred_element_type=jnp.float32) + hidden_bias
    activated = gelu_exact(pre_act).astype(jnp.bfloat16)
    branch_two = jnp.dot(activated, full_fc2, preferred_element_type=jnp.float32) + offsets[5]
    output = (hidden_state + branch_two * gains[3] * query_mask).astype(jnp.bfloat16)
    back_qkv, back_proj, back_fc1, back_fc2, back_gains = (
        full_qkv,
        full_proj,
        full_fc1,
        full_fc2,
        gains,
    )
    grad_out = cotangent.astype(jnp.float32)
    layer_gain_two = token_sum(grad_out * query_mask * branch_two)
    grad_branch_two = (grad_out * back_gains[3] * query_mask).astype(jnp.bfloat16)
    shift_five = token_sum(grad_branch_two.astype(jnp.float32))
    grad_fc2 = jnp.einsum(
        "spf,spd->fd", activated, grad_branch_two, preferred_element_type=jnp.float32
    )
    grad_act = jnp.einsum(
        "spd,fd->spf", grad_branch_two, back_fc2, preferred_element_type=jnp.float32
    )
    grad_pre = (grad_act * gelu_slope(pre_act)).astype(jnp.bfloat16)
    grad_hidden_bias = token_sum(grad_pre.astype(jnp.float32))
    grad_fc1 = jnp.einsum("spd,spf->df", normed_two, grad_pre, preferred_element_type=jnp.float32)
    grad_normed_two = jnp.einsum(
        "spf,df->spd", grad_pre, back_fc1, preferred_element_type=jnp.float32
    )
    norm_gain_two = token_sum(grad_normed_two * unit_two)
    norm_shift_two = token_sum(grad_normed_two)
    grad_hidden = grad_out + norm_back(grad_normed_two, unit_two, inverse_two, back_gains[2])
    layer_gain_one = token_sum(grad_hidden * query_mask * branch_one)
    grad_branch_one = (grad_hidden * back_gains[1] * query_mask).astype(jnp.bfloat16)
    shift_proj = token_sum(grad_branch_one.astype(jnp.float32))
    grad_proj = jnp.einsum(
        "spd,spe->de", mixed, grad_branch_one, preferred_element_type=jnp.float32
    )
    grad_mixed = jnp.einsum(
        "spe,de->spd", grad_branch_one, back_proj, preferred_element_type=jnp.float32
    )
    grad_mixed = grad_mixed.astype(jnp.bfloat16)
    grad_attended = lax.all_to_all(
        grad_mixed, "seq", split_axis=2, concat_axis=1, tiled=True
    ).reshape(head_shape)
    probs = jnp.exp(scores_of() - log_total)
    probs_again = probs.astype(jnp.bfloat16)
    grad_probs = jnp.einsum(
        "bqhe,bkhe->bhqk", grad_attended, value_heads, preferred_element_type=jnp.float32
    )
    row_dot = jnp.sum(grad_probs * probs, axis=-1, keepdims=True)
    grad_scores = (probs * (grad_probs - row_dot)).astype(jnp.bfloat16)
    flat_shape = (slot_count, seq_total, part_width)
    grad_query = (
        jnp.einsum("bhqk,bkhe->bqhe", grad_scores, key_heads, preferred_element_type=jnp.float32)
        * factor
    )
    grad_key = (
        jnp.einsum("bhqk,bqhe->bkhe", grad_scores, query_heads, preferred_element_type=jnp.float32)
        * factor
    )
    grad_value = jnp.einsum(
        "bhqk,bqhe->bkhe", probs_again, grad_attended, preferred_element_type=jnp.float32
    )
    grad_query = grad_query.astype(jnp.bfloat16).reshape(flat_shape)
    grad_key = grad_key.astype(jnp.bfloat16).reshape(flat_shape)
    grad_value = grad_value.astype(jnp.bfloat16).reshape(flat_shape)
    token_query, token_key, token_value = (
        lax.all_to_all(grad_query, "seq", split_axis=1, concat_axis=2, tiled=True),
        lax.all_to_all(grad_key, "seq", split_axis=1, concat_axis=2, tiled=True),
        lax.all_to_all(grad_value, "seq", split_axis=1, concat_axis=2, tiled=True),
    )
    grad_joined = jnp.concatenate([token_query, token_key, token_value], axis=2)
    grad_qkv = jnp.einsum(
        "spd,spe->de", normed_one, grad_joined, preferred_element_type=jnp.float32
    )
    grad_normed_one = jnp.einsum(
        "spe,de->spd", grad_joined, back_qkv, preferred_element_type=jnp.float32
    )
    norm_gain_one = token_sum(grad_normed_one * unit_one)
    norm_shift_one = token_sum(grad_normed_one)
    grad_input = (
        grad_hidden + norm_back(grad_normed_one, unit_one, inverse_one, back_gains[0])
    ).astype(jnp.bfloat16)
    gain_terms = jnp.stack([norm_gain_one, layer_gain_one, norm_gain_two, layer_gain_two])
    shift_terms = jnp.stack(
        [
            norm_shift_one,
            token_sum(token_query.astype(jnp.float32)),
            token_sum(token_value.astype(jnp.float32)),
            shift_proj,
            norm_shift_two,
            shift_five,
        ]
    )
    shares = (
        lax.psum_scatter(
            grad_qkv.astype(jnp.bfloat16), "dp", scatter_dimension=0, tiled=True
        ).astype(jnp.float32),
        lax.psum_scatter(
            grad_proj.astype(jnp.bfloat16), "dp", scatter_dimension=0, tiled=True
        ).astype(jnp.float32),
        lax.psum_scatter(
            grad_fc1.astype(jnp.bfloat16), "dp", scatter_dimension=0, tiled=True
        ).astype(jnp.float32),
        lax.psum_scatter(
            grad_fc2.astype(jnp.bfloat16), "dp", scatter_dimension=0, tiled=True
        ).astype(jnp.float32),
        lax.psum_scatter(
            grad_hidden_bias.astype(jnp.bfloat16), "dp", scatter_dimension=0, tiled=True
        ).astype(jnp.float32),
        lax.psum_scatter(
            gain_terms.astype(jnp.bfloat16), "dp", scatter_dimension=1, tiled=True
        ).astype(jnp.float32),
        lax.psum_scatter(
            shift_terms.astype(jnp.bfloat16), "dp", scatter_dimension=1, tiled=True
        ).astype(jnp.float32),
    )
    totals = (
        lax.psum(shares[0].astype(jnp.bfloat16), "seq").astype(jnp.float32),
        lax.psum(shares[1].astype(jnp.bfloat16), "seq").astype(jnp.float32),
        lax.psum(shares[2].astype(jnp.bfloat16), "seq").astype(jnp.float32),
        lax.psum(shares[3].astype(jnp.bfloat16), "seq").astype(jnp.float32),
        lax.psum(shares[4].astype(jnp.bfloat16), "seq").astype(jnp.float32),
        lax.psum(shares[5].astype(jnp.bfloat16), "seq").astype(jnp.float32),
        lax.psum(shares[6].astype(jnp.bfloat16), "seq").astype(jnp.float32),
    )
    return (
        output,
        grad_input,
        totals[0],
        totals[1],
        totals[2],
        totals[3],
        totals[4],
        totals[5],
        totals[6],
    )


CORE, ALONG_X, ALONG_Y = 1, 2, 4
NEGATIVE = -1e30


def swap(values, bit):
    size = lax.axis_size("dp")
    return lax.ppermute(values, "dp", [(i, i ^ bit) for i in range(size)])


def after(values, *earlier):
    return lax.optimization_barrier((values, earlier))[0]


def place():
    index = lax.axis_index("dp")
    return index % 2, (index // 2) % 2, index // 4


def joined(mine, theirs, bit, axis):
    low = jnp.where(bit == 0, mine, theirs)
    high = jnp.where(bit == 0, theirs, mine)
    return jnp.concatenate([low, high], axis=axis)


def local_call(kernel, outs, position, *arrays, scratch=(), room=40, outside=(), copies=0):
    return pl.pallas_call(
        kernel,
        out_shape=[jax.ShapeDtypeStruct(shape, kind) for shape, kind in outs],
        in_specs=[pl.BlockSpec(memory_space=pltpu.SMEM)]
        + [
            pl.BlockSpec(memory_space=pl.ANY if n in outside else pltpu.VMEM)
            for n in range(len(arrays))
        ],
        out_specs=[pl.BlockSpec(memory_space=pltpu.VMEM)] * len(outs),
        scratch_shapes=[pltpu.VMEM(shape, kind) for shape, kind in scratch]
        + [pltpu.SemaphoreType.DMA((copies,))] * (copies > 0),
        compiler_params=pltpu.CompilerParams(vmem_limit_bytes=room * 1024 * 1024),
        cost_estimate=pl.CostEstimate(flops=1 << 20, bytes_accessed=1 << 16, transcendentals=0),
    )(position, *arrays)


def start_copies(pairs, semaphores):
    started = []
    for n, (source, target) in enumerate(pairs):
        started.append(pltpu.make_async_copy(source, target, semaphores.at[n]))
        started[-1].start()
    return started


def cut_kernel(count, qkv, fc1, proj, scales, shifts, bias, pad_mask, mine, give, semaphores):
    own = lax.rem(lax.axis_index("dp"), 2)
    pairs = []
    for out, core in ((give, 1 - own), (mine, own)):
        for j in range(12):
            column = pl.multiple_of((2 * j + core) * 128, 128)
            pairs.append((qkv.at[:, pl.ds(column, 128)], out.at[:, pl.ds(j * 128, 128)]))
        for j in range(4):
            column = pl.multiple_of((2 * j + core) * 512, 512)
            pairs.append((fc1.at[:, pl.ds(column, 512)], out.at[:, pl.ds(1664 + j * 512, 512)]))
    pairs.append((proj.at[:, pl.ds(0, 512)], mine.at[:, pl.ds(3712, 512)]))
    started = start_copies(pairs, semaphores)
    wide = [item[...].astype(jnp.float32) for item in (scales, shifts, bias)]
    small = jnp.concatenate(wide + [jnp.zeros((114, 128), jnp.float32)], axis=0)
    slot = lax.broadcasted_iota(jnp.int32, pad_mask.shape, 0)
    mask = jnp.where(slot < count[0], pad_mask[...], 0).astype(jnp.float32)
    masks = [mask[:, j * 128 : j * 128 + 128] for j in range(mask.shape[1] // 128)]
    masks = jnp.concatenate(masks + [jnp.zeros((120, 128), jnp.float32)], axis=0)
    mine[:, pl.ds(1536, 128)] = small.astype(jnp.bfloat16)
    give[:, pl.ds(1536, 128)] = small.astype(jnp.bfloat16)
    give[:, pl.ds(3712, 128)] = masks.astype(jnp.bfloat16)
    for copy in started:
        copy.wait()


def chips_of(pos):
    chip = 2 * pos[2] + pos[1]
    along_x = 2 * pos[2] + 1 - pos[1]
    along_y = 2 * (1 - pos[2]) + pos[1]
    across = 2 * (1 - pos[2]) + 1 - pos[1]
    return (chip, along_x, along_y, across), (chip, along_y, along_x, across)


def dot_of(left, right, left_dim, right_dim):
    return lax.dot_general(
        left, right, (((left_dim,), (right_dim,)), ((), ())), preferred_element_type=jnp.float32
    )


def low(values):
    return values.astype(jnp.bfloat16)


def wide(values):
    return values.astype(jnp.float32)


def down(values):
    return jnp.sum(values, axis=0, keepdims=True)


def unit_of(values):
    centred = values - jnp.mean(values, axis=1, keepdims=True)
    inverse = lax.rsqrt(jnp.mean(centred * centred, axis=1, keepdims=True) + EPSILON)
    return centred * inverse, inverse


def row_blocks(count, size=128):
    return [pl.ds(n * size, size) for n in range(count // size)]


def join_parts(pos, owners, near_a, far_a, near_b, far_b):
    for part, chips, near, far in zip((0, 1), chips_of(pos), (near_a, near_b), (far_a, far_b)):
        for n in range(4):
            yield part, chips[n], owners[part], (near, far)[n // 2], n % 2


def front_kernel(
    pos, mine, theirs, near_a, far_a, near_b, far_b, mask, gate,
    weight, vectors, bias, inputs, grad_out, grad_two, normed, qkv, attended,
):
    core = pos[0]
    for part, chip, owner, block, n in join_parts(
        pos, (core, 1 - core), near_a, far_a, near_b, far_b
    ):
        row = pl.multiple_of((2 * chip + owner) * 128, 128)
        weight[pl.ds(row, 128), :] = block[pl.ds(n * 128, 128), pl.ds(0, 1536)]
        small = wide(block[pl.ds(n * 128, 16), pl.ds(1536, 128)])
        vectors[:, pl.ds(row, 128)] = small
        if part == 0:
            for j in range(4):
                column = pl.multiple_of(chip * 512 + j * 128, 128)
                bias[:, pl.ds(column, 128)] = small[10 + j : 11 + j]
    half = mine.shape[0] // 2
    piece = half // 2
    for there, block in ((core, mine), (1 - core, theirs)):
        for turn in range(2):
            first = there * half + lax.rem(pos[3] + turn, 2) * piece
            rows = pl.ds(pl.multiple_of(first, piece), piece)
            inputs[rows, :] = block[pl.ds(turn * half, piece), :]
            grad_out[rows, :] = block[pl.ds(turn * half + piece, piece), :]
    for rows in row_blocks(2 * half):
        unit, _ = unit_of(wide(inputs[rows, :]))
        normed[rows, :] = low(unit * vectors[0:1, :] + vectors[4:5, :])
        grad_two[rows, :] = low(wide(grad_out[rows, :]) * vectors[3:4, :] * gate[rows, :])
    for kind, shift in enumerate((5, None, 6)):
        made = dot_of(normed[...], weight[:, pl.ds(kind * 512, 512)], 1, 0)
        for chip in range(4):
            piece = made[:, chip * 128 : chip * 128 + 128]
            if shift is not None:
                column = pl.multiple_of((2 * chip + core) * 128, 128)
                piece = piece + vectors[shift : shift + 1, pl.ds(column, 128)]
            qkv[:, pl.ds(kind * 512 + chip * 128, 128)] = low(piece)
    lane = lax.broadcasted_iota(jnp.int32, (2 * half, 128), 1)
    live = mask[...] > 0
    for pair in range(4):
        query = qkv[:, pl.ds(pair * 128, 128)] * jnp.bfloat16(HD ** (-0.5))
        key = qkv[:, pl.ds(512 + pair * 128, 128)]
        value = qkv[:, pl.ds(1024 + pair * 128, 128)]
        got = []
        for head in range(2):
            chosen = (lane // HD) == head
            scores = dot_of(jnp.where(chosen, query, jnp.zeros_like(query)), key, 1, 1)
            scores = jnp.where(live, scores, NEGATIVE)
            expo = jnp.exp(scores - jnp.max(scores, axis=1, keepdims=True))
            probs = expo * (1.0 / jnp.sum(expo, axis=1, keepdims=True))
            got.append(dot_of(low(probs), value, 1, 0))
        attended[:, pl.ds(pair * 128, 128)] = low(jnp.where(lane < HD, got[0], got[1]))


def put_halves(values, tile, upper, lower):
    half = values.shape[0] // 2
    upper[:, tile] = low(values[:half])
    lower[:, tile] = low(values[half:])


def of_halves(upper, lower, n, size=128):
    count = upper.shape[0] // size
    return wide((upper, lower)[n // count][pl.ds((n % count) * size, size), :])


def proj_kernel(
    pos, attended, near_a, far_a, near_b, far_b, proj, upper, lower, semaphores
):
    pairs = []
    for part, chip, _, block, n in join_parts(pos, (0, 0), near_a, far_a, near_b, far_b):
        row = pl.multiple_of(chip * 128, 128)
        target = proj.at[pl.ds(row, 128), pl.ds(part * 512, 512)]
        pairs.append((block.at[pl.ds(n * 128, 128), pl.ds(2048, 512)], target))
    for copy in start_copies(pairs, semaphores):
        copy.wait()
    for tile in row_blocks(1024, 256):
        put_halves(dot_of(attended[...], proj[:, tile], 1, 0), tile, upper, lower)


def far_chips(pos):
    return (1 - pos[1], 3 - pos[1]), (2 * (1 - pos[2]), 2 * (1 - pos[2]) + 1)


def second_chips(pos):
    own = 2 * pos[2] + pos[1]
    over_y = 2 * (1 - pos[2]) + pos[1]
    over_x = 2 * pos[2] + 1 - pos[1]
    return ((own, pos[2]), (over_y, 1 - pos[2])), ((own, pos[1]), (over_x, 1 - pos[1]))


def chip_columns(ref, chip, count):
    return ref[:, pl.ds(pl.multiple_of(chip * count, count), count)]


def far_products(pos, left, right, outs):
    rows = left.shape[1] // 4
    cut = right.shape[1] // 2
    for part, chips in enumerate(far_chips(pos)):
        for n in range(2):
            made = dot_of(
                chip_columns(left, chips[n], rows), right[:, pl.ds(part * cut, cut)], 0, 0
            )
            outs[part][pl.ds(n * rows, rows), :] = low(made)


def fc1_copies(pos, near_a, far_a, near_b, far_b, fc1):
    pairs = []
    for _, chip, owner, block, n in join_parts(
        pos, (pos[0], 1 - pos[0]), near_a, far_a, near_b, far_b
    ):
        row = pl.multiple_of((2 * chip + owner) * 128, 128)
        source = block.at[pl.ds(n * 128, 128), pl.ds(0, 2048)]
        pairs.append((source, fc1.at[pl.ds(row, 128), :]))
    return pairs


def middle_kernel(
    pos, inputs, own_upper, own_lower, upper, lower, vectors, bias, gate, near_a, far_a, near_b,
    far_b, grad_two, hidden, normed, slope, activated, out_a, out_b, fc1, semaphores,
):
    pairs = fc1_copies(pos, near_a, far_a, near_b, far_b, fc1)
    started = start_copies(pairs, semaphores)
    for n, rows in enumerate(row_blocks(inputs.shape[0])):
        made = of_halves(own_upper, own_lower, n) + of_halves(upper, lower, n) + vectors[7:8, :]
        state = wide(inputs[rows, :]) + made * vectors[1:2, :] * gate[rows, :]
        hidden[rows, :] = state
        unit, _ = unit_of(state)
        normed[rows, :] = low(unit * vectors[2:3, :] + vectors[8:9, :])
    for copy in started:
        copy.wait()

    def units(n, _):
        tile = pl.ds(pl.multiple_of(n * 256, 256), 256)
        pre = dot_of(normed[...], fc1[:, tile], 1, 0) + bias[:, tile]
        bell = 0.5 * (1.0 + lax.erf(pre * ROOT_HALF))
        activated[:, tile] = low(pre * bell)
        slope[:, tile] = low(bell + pre * jnp.exp(-0.5 * pre * pre) * INV_ROOT_TWO_PI)
        return 0

    lax.fori_loop(0, 8, units, 0)
    far_products(pos, activated, grad_two, (out_a, out_b))


def units_back_kernel(
    pos, near_a, far_a, near_b, far_b, grad_two, slope, activated, normed,
    fc1_near_a, fc1_far_a, fc1_near_b, fc1_far_b,
    grad_pre, sums, partial, upper, lower, out_a, out_b, branch, branch_low, fc2, fc1, semaphores,
):
    started = start_copies(
        fc1_copies(pos, fc1_near_a, fc1_far_a, fc1_near_b, fc1_far_b, fc1), semaphores
    )
    for part, chip, _, block, n in join_parts(pos, (0, 0), near_a, far_a, near_b, far_b):
        row = pl.multiple_of(chip * 512 + part * 256, 256)
        fc2[pl.ds(row, 256), :] = block[pl.ds(n * 256, 256), :]

    def units(n, _):
        tile = pl.ds(pl.multiple_of(n * 256, 256), 256)
        made = low(dot_of(grad_two[...], fc2[tile, :], 1, 1) * wide(slope[:, tile]))
        grad_pre[:, tile] = made
        sums[:, tile] = down(wide(made))
        return 0

    lax.fori_loop(0, 8, units, 0)
    for copy in started:
        copy.wait()
    for tile in row_blocks(1024, 256):
        made = dot_of(grad_pre[...], fc1[tile, :], 1, 1)
        partial[:, tile] = made
        put_halves(made, tile, upper, lower)
    far_products(pos, normed, grad_pre, (out_a, out_b))
    half = branch.shape[0]
    mine = pl.ds(pl.multiple_of(pos[0] * half, half), half)
    theirs = pl.ds(pl.multiple_of((1 - pos[0]) * half, half), half)
    for tile in row_blocks(1024, 256):
        branch[:, tile] = dot_of(activated[mine, :], fc2[:, tile], 1, 0)
        branch_low[:, tile] = low(dot_of(activated[theirs, :], fc2[:, tile], 1, 0))


def proj_product(attended, grad_one, chip, part):
    return dot_of(chip_columns(attended, chip, 128), grad_one[:, pl.ds(part * 512, 512)], 0, 0)


def norm_back_kernel(
    pos, grad_out, partial, upper, lower, hidden, own_upper, own_lower, their_upper, their_lower,
    vectors, gate, proj, attended,
    fc1_a, fc1_b, grad_hidden, grad_one, grad_attended, sums, far_a, far_b,
):
    total = [0.0] * 4
    for n, rows in enumerate(row_blocks(hidden.shape[0])):
        grad = partial[rows, :] + of_halves(upper, lower, n)
        unit, inverse = unit_of(hidden[rows, :])
        state = wide(grad_out[rows, :]) + norm_back(grad, unit, inverse, vectors[2:3, :])
        grad_hidden[rows, :] = state
        gated = state * gate[rows, :]
        made = low(gated * vectors[1:2, :])
        grad_one[rows, :] = made
        branch = of_halves(own_upper, own_lower, n) + of_halves(their_upper, their_lower, n)
        terms = (gated * (branch + vectors[7:8, :]), grad * unit, wide(made), grad)
        total = [one + down(term) for one, term in zip(total, terms)]
    for n in range(4):
        sums[n : n + 1, :] = total[n]
    grad_attended[...] = low(dot_of(grad_one[...], proj[...], 1, 1))
    for part, chips in enumerate(far_chips(pos)):
        out = (far_a, far_b)[part]
        out[pl.ds(0, 512), :] = (fc1_a, fc1_b)[part][...]
        for n in range(2):
            made = low(proj_product(attended, grad_one, chips[n], part))
            here = pl.ds(512 + n * 64, 64)
            out[here, pl.ds(0, 512)] = made[:64]
            out[here, pl.ds(512, 512)] = made[64:]


def fold_kernel(pos, left, right, got_a, got_b, keep_a, give_a, keep_b, give_b):
    rows = left.shape[1] // 4
    cut = right.shape[1] // 2
    outs = ((keep_a, give_a), (keep_b, give_b))
    for part, chips in enumerate(second_chips(pos)):
        for n in range(2):
            chip, arrived = chips[n]
            made = dot_of(chip_columns(left, chip, rows), right[:, pl.ds(part * cut, cut)], 0, 0)
            there = pl.ds(pl.multiple_of(arrived * rows, rows), rows)
            outs[part][n][...] = low(made + wide((got_a, got_b)[part][there, :]))


def fc1_fold_kernel(
    pos, left, right, attended, grad_one, small, got_a, got_b, keep_a, give_a, keep_b, give_b
):
    outs = ((keep_a, give_a), (keep_b, give_b))
    for part, chips in enumerate(second_chips(pos)):
        got = (got_a, got_b)[part]
        for n in range(2):
            chip, arrived = chips[n]
            out = outs[part][n]
            made = dot_of(chip_columns(left, chip, 256), right[:, pl.ds(part * 1024, 1024)], 0, 0)
            there = pl.ds(pl.multiple_of(arrived * 256, 256), 256)
            out[pl.ds(0, 256), :] = low(made + wide(got[there, :]))
            made = proj_product(attended, grad_one, chip, part)
            there = pl.ds(pl.multiple_of(512 + arrived * 64, 64), 64)
            arrived_rows = wide(got[there, :])
            here = pl.ds(256, 64)
            out[here, pl.ds(0, 512)] = low(made[:64] + arrived_rows[:, :512])
            out[here, pl.ds(512, 512)] = low(made[64:] + arrived_rows[:, 512:])
    give_b[pl.ds(320, 16), :] = small[...]


def attend_back_kernel(
    pos, qkv, mask, grad, normed, out, sums, far_a, far_b
):
    length = qkv.shape[0]
    lane = lax.broadcasted_iota(jnp.int32, (length, 128), 1)
    live = mask[...] > 0
    factor = HD ** (-0.5)
    for pair in range(4):
        spans = [pl.ds(offset + pair * 128, 128) for offset in (0, 512, 1024)]
        query, key, value = (qkv[:, span] for span in spans)
        grad_pair = grad[:, pl.ds(pair * 128, 128)]
        grad_query, grad_key, grad_value = [], 0.0, 0.0
        for head in range(2):
            chosen = (lane // HD) == head
            query_one = jnp.where(chosen, query, jnp.zeros_like(query))
            grad_head = jnp.where(chosen, grad_pair, jnp.zeros_like(grad_pair))
            scores = dot_of(key, query_one, 1, 1) * factor
            scores = jnp.where(live, scores, NEGATIVE)
            expo = jnp.exp(scores - jnp.max(scores, axis=0, keepdims=True))
            probs = expo * (1.0 / jnp.sum(expo, axis=0, keepdims=True))
            grad_probs = dot_of(value, grad_head, 1, 1)
            along = jnp.sum(grad_probs * probs, axis=0, keepdims=True)
            grad_scores = low(probs * (grad_probs - along))
            grad_value += dot_of(low(probs), grad_head, 1, 0)
            grad_key += dot_of(grad_scores, query_one, 1, 0)
            grad_query.append(dot_of(grad_scores, key, 0, 0))
        made = jnp.where(lane < HD, grad_query[0], grad_query[1]) * factor
        for span, item in zip(spans, (made, grad_key * factor, grad_value)):
            item = low(item)
            out[:, span] = item
            sums[:, span] = down(wide(item))
    far_products(pos, normed, out, (far_a, far_b))


def last_fold_kernel(
    pos, normed, grad_qkv, got_a, got_b, small, small_got, keep_a, give_a, keep_b, give_b
):
    outs = ((keep_a, give_a), (keep_b, give_b))
    for part, chips in enumerate(second_chips(pos)):
        for n in range(2):
            chip, arrived = chips[n]
            made = dot_of(
                chip_columns(normed, chip, 256), grad_qkv[:, pl.ds(part * 768, 768)], 0, 0
            )
            there = pl.ds(pl.multiple_of(arrived * 256, 256), 256)
            outs[part][n][pl.ds(0, 256), :] = low(made + wide((got_a, got_b)[part][there, :]))
    for out, at_y in ((keep_a, pos[2]), (give_a, 1 - pos[2])):
        column = pl.multiple_of(at_y * 128, 128)
        sums = small[at_y] + wide(small_got[:, pl.ds(column, 128)])
        out[pl.ds(256, 32), :] = jnp.zeros((32, 768), jnp.bfloat16)
        out[pl.ds(256, 16), pl.ds(0, 128)] = low(sums)


def first_back_kernel(pos, grad_qkv, weight, last, partial, upper, lower):
    half = lower.shape[0]
    for tile in row_blocks(1024, 256):
        made = dot_of(grad_qkv[...], weight[tile, :], 1, 1)
        partial[:, tile] = made
        upper[pl.ds(0, half), tile] = low(made[:half])
        lower[:, tile] = low(made[half:])
    upper[pl.ds(half, 16), :] = low(jnp.broadcast_to(last[0:1, :], (16, 1024)))


def inputs_back_kernel(
    pos, inputs, partial, upper, lower, grad_hidden, vectors, out, sums, grads
):
    total = [0.0] * 2
    half = out.shape[0]
    for n, rows in enumerate(row_blocks(2 * half)):
        there = (upper, lower)[n * 128 // half]
        grad = partial[rows, :] + wide(there[pl.ds((n * 128) % half, 128), :])
        grads[rows, :] = grad
        unit, _ = unit_of(wide(inputs[rows, :]))
        total = [one + down(term) for one, term in zip(total, (grad * unit, grad))]
    for n in range(2):
        sums[n : n + 1, :] = total[n]
    sums[2:3, :] = wide(upper[pl.ds(half, 16), :])[0:1]
    for n in range(half // 128):
        rows = pl.ds(pl.multiple_of(pos[0] * half + n * 128, 128), 128)
        unit, inverse = unit_of(wide(inputs[rows, :]))
        state = grad_hidden[rows, :] + norm_back(grads[rows, :], unit, inverse, vectors[0:1, :])
        out[pl.ds(n * 128, 128), :] = low(state)


def output_kernel(
    pos, hidden, branch, other, vectors, gate, grad_out, grad_two, out, sums
):
    half = out.shape[0]
    gain_sum, shift_sum = 0.0, 0.0
    for n in range(half // 128):
        here = pl.ds(n * 128, 128)
        rows = pl.ds(pl.multiple_of(pos[0] * half + n * 128, 128), 128)
        made = branch[here, :] + wide(other[here, :]) + vectors[9:10, :]
        out[here, :] = low(hidden[rows, :] + made * vectors[3:4, :] * gate[rows, :])
        gain_sum += down(wide(grad_out[rows, :]) * gate[rows, :] * made)
    for rows in row_blocks(2 * half):
        shift_sum += down(wide(grad_two[rows, :]))
    sums[0:1, :] = gain_sum
    sums[1:2, :] = shift_sum


def small_kernel(pos, first, second, last, attention, units, keep, give):
    core = pos[0]
    order = [(first, 0), (second, 0), (second, 1), (last, 0), (first, 1)]
    order += [None, None, (second, 2), (second, 3), (last, 1)]
    give[...] = jnp.zeros_like(give)
    for at_y in range(2):
        for over in range(2):
            chip = 2 * at_y + (pos[1] if over == 0 else 1 - pos[1])
            own = pl.ds(pl.multiple_of((2 * chip + core) * 128, 128), 128)
            here = pl.multiple_of(chip * 128, 128)
            lines = [None if item is None else item[0][item[1] : item[1] + 1, own] for item in order]
            lines[3] = lines[3] + first[2:3, own]
            lines[5] = attention[:, pl.ds(here, 128)]
            lines[6] = attention[:, pl.ds(pl.multiple_of(1024 + chip * 128, 128), 128)]
            for j in range(4):
                column = pl.multiple_of(chip * 512 + j * 128, 128)
                lines.append(units[:, pl.ds(column, 128)])
            block = jnp.concatenate(lines + [jnp.zeros((2, 128), jnp.float32)], axis=0)
            if over == 0:
                keep[at_y, :, :] = block
            else:
                give[:, pl.ds(at_y * 128, 128)] = low(block)


def finish_qkv_kernel(pos, mine, theirs, out):
    core = pos[0]
    rows = pl.ds(pl.multiple_of(core * 128, 128), 128)
    for j in range(12):
        here = pl.ds(j * 128, 128)
        out[:, pl.ds(pl.multiple_of((2 * j + core) * 128, 128), 128)] = wide(mine[rows, here])
        out[:, pl.ds(pl.multiple_of((2 * j + 1 - core) * 128, 128), 128)] = wide(theirs[:, here])


def finish_fc1_kernel(pos, mine, theirs, out):
    core = pos[0]
    rows = pl.ds(pl.multiple_of(core * 128, 128), 128)
    for j in range(4):
        here = pl.ds(j * 512, 512)
        out[:, pl.ds(pl.multiple_of((2 * j + core) * 512, 512), 512)] = wide(mine[rows, here])
        out[:, pl.ds(pl.multiple_of((2 * j + 1 - core) * 512, 512), 512)] = wide(theirs[:, here])


def add_low(one, two):
    return (one.astype(jnp.float32) + two.astype(jnp.float32)).astype(jnp.bfloat16)


def line_in(values):
    return lax.ppermute(values, "seq", [(0, 1), (3, 2)])


def line_mid(values):
    return lax.ppermute(values, "seq", [(1, 2), (2, 1)])


def line_out(values):
    return lax.ppermute(values, "seq", [(1, 0), (2, 3)])


def inner():
    at_z = lax.axis_index("seq")
    return ((at_z == 1) | (at_z == 2)).astype(jnp.int32)


def image_moves(back):
    seq = lax.axis_size("seq")
    rounds = []
    for turn in range(2):
        moves = []
        for chip in range(lax.axis_size("dp") // 2):
            for core in range(2):
                for quarter in range(seq):
                    slot = (quarter + turn) % 2
                    source = (2 * chip + core) * seq + quarter
                    target = (2 * chip + quarter // 2) * seq + 2 * core + slot
                    moves.append((target, source) if back else (source, target))
        rounds.append(moves)
    return rounds


def to_images(first, second, *earlier):
    at_z = lax.axis_index("seq")
    first, second = after((first, second), *earlier)
    got = []
    for turn, moves in enumerate(image_moves(False)):
        slot = (at_z + turn) % 2
        sent = [lax.dynamic_index_in_dim(item, slot, 0, False) for item in (first, second)]
        got.append(lax.ppermute(jnp.concatenate(sent, axis=0), ("dp", "seq"), moves))
    return jnp.concatenate(got, axis=0)


def from_images(values):
    at_z = lax.axis_index("seq")
    pieces = values.reshape(2, values.shape[0] // 2, values.shape[1])
    got = []
    for turn, moves in enumerate(image_moves(True)):
        sent = lax.dynamic_index_in_dim(pieces, (at_z + turn) % 2, 0, False)
        got.append(lax.ppermute(sent, ("dp", "seq"), moves))
    return got


def slots_of(got):
    even = lax.axis_index("seq") % 2 == 0
    return jnp.stack([jnp.where(even, got[0], got[1]), jnp.where(even, got[1], got[0])])


def image_plan(
    tokens, group_count, pad_mask, w_qkv, w_proj, w_fc1, w_fc2, fc1_bias, scales, shifts, cotangent
):
    slot_count, _, width = tokens.shape
    length = pad_mask.shape[1]
    half = length // 2
    f32, bf16 = jnp.float32, jnp.bfloat16
    core, at_x, at_y = place()
    at_z = lax.axis_index("seq")
    pos = jnp.stack([core, at_x, at_y, at_z]).astype(jnp.int32)

    alive = jnp.arange(slot_count, dtype=jnp.int32) < group_count[0]
    mask_own = jnp.where(alive[:, None], pad_mask, 0).astype(f32)
    mine, give = local_call(
        cut_kernel, [((128, 4224), bf16), ((128, 3840), bf16)],
        group_count, w_qkv, w_fc1, w_proj, scales, shifts, fc1_bias.reshape(4, 128), pad_mask, room=56,
        outside=(0, 1, 2), copies=33,
    )
    got = swap(give, CORE)
    blocks = (mine, jnp.concatenate([got[:, :3712], w_proj[:, 512:]], axis=1))
    mask_both = joined(
        mask_own,
        got[:8, 3712:].reshape(4, slot_count, 128).transpose(1, 0, 2).reshape(
            slot_count, length
        ).astype(f32),
        core, 0,
    )
    mask_row = lax.dynamic_index_in_dim(mask_both, at_z, 0, False)
    token_gate = mask_row[:, None]

    def links(sent, order=(ALONG_X, ALONG_Y)):
        return swap(sent[0], order[0]), swap(sent[1], order[1])

    def second_link(blocks, got):
        near_a, near_b = (jnp.concatenate(pair, axis=0) for pair in zip(blocks, got))
        far_a, far_b = links((near_a, near_b), (ALONG_Y, ALONG_X))
        return near_a, far_a, near_b, far_b

    def lanes(pair, start, stop):
        return [item[:, start:stop] for item in pair]

    first = links(blocks)
    fc2_rows = after(w_fc2, blocks[1])
    fc2_blocks = (fc2_rows[:256], fc2_rows[256:])
    fc2_first = links(fc2_blocks)
    both = to_images(tokens, cotangent, blocks[1])
    qkv_parts = second_link(lanes(blocks, 0, 1664), lanes(first, 0, 1664))
    first = after(first, qkv_parts[0], qkv_parts[2])
    fc1_parts = second_link(lanes(blocks, 1664, 4224), lanes(first, 1664, 4224))
    fc2_parts = second_link(fc2_blocks, after(fc2_first, fc1_parts[0], fc1_parts[2]))

    full = (length, width)
    qkv_w, vectors, bias, inputs, grad_out, grad_two, normed_one, qkv, attended = local_call(
        front_kernel,
        [
            ((width, 1536), bf16), ((16, width), f32), ((1, 2048), f32), (full, bf16),
            (full, bf16), (full, bf16), (full, bf16), ((length, 1536), bf16),
            ((length, 512), bf16),
        ],
        pos, both, swap(both, CORE), *after(qkv_parts, fc2_parts[0], fc2_parts[2]),
        mask_row[None, :], token_gate, room=24,
    )
    halves = [((half, width), bf16)] * 2
    proj_w, *one_own = local_call(
        proj_kernel, [((512, width), bf16)] + halves,
        pos, attended, *fc1_parts, room=14, outside=(1, 2, 3, 4), copies=8,
    )
    one_other = [swap(item, CORE) for item in one_own]
    hidden, normed_two, slope, activated, far_a, far_b = local_call(
        middle_kernel,
        [
            (full, f32), (full, bf16), ((length, 2048), bf16), ((length, 2048), bf16),
            ((1024, 512), bf16), ((1024, 512), bf16),
        ],
        pos, inputs, *one_own, *one_other, vectors, bias, token_gate, *fc1_parts, grad_two,
        scratch=[((width, 2048), bf16)], room=30, outside=(8, 9, 10, 11), copies=8,
    )

    def fold(left, right, got, *earlier):
        block = (left.shape[1] // 4, right.shape[1] // 2)
        got_a, got_b = after(got, *earlier)
        keep_a, give_a, keep_b, give_b = local_call(
            fold_kernel, [(block, bf16)] * 4, pos, left, right, got_a, got_b, room=14,
    )
        return (keep_a, keep_b), (give_a, give_b)

    def half_of(keep, got):
        return [add_low(one, two) for one, two in zip(keep, got)]

    fc2_got = links((far_a, far_b))
    grad_pre, unit_sums, partial, upper, lower, far_a, far_b, branch_two, branch_low = local_call(
        units_back_kernel,
        [((length, 2048), bf16), ((1, 2048), f32), (full, f32)]
        + halves
        + [((512, 1024), bf16), ((512, 1024), bf16), ((half, width), f32), ((half, width), bf16)],
        pos, *fc2_parts, grad_two, slope, activated, normed_two, *fc1_parts,
        scratch=[((2048, width), bf16), ((width, 2048), bf16)], outside=(8, 9, 10, 11), copies=8,
    )
    others = [swap(item, CORE) for item in (upper, lower)]
    branch_other = swap(branch_low, CORE)
    output, last_sums = local_call(
        output_kernel, [((half, width), bf16), ((2, width), f32)],
        pos, hidden, branch_two, branch_other, vectors, token_gate, grad_out,
        grad_two, room=14,
    )
    out_got = from_images(output)
    fc1_far = ((640, 1024), bf16)
    grad_hidden, grad_one, grad_attended, second_sums, far_a, far_b = local_call(
        norm_back_kernel,
        [
            (full, f32), (full, bf16), ((length, 512), bf16), ((4, width), f32), fc1_far, fc1_far,
        ],
        pos, grad_out, partial, *after(others, output), hidden, *one_own, *one_other, vectors,
        token_gate, proj_w, attended, far_a, far_b, room=24,
    )
    fc2_keep, fc2_give = fold(activated, grad_two, fc2_got, grad_attended, out_got[0])
    fc2_again = links(fc2_give, (ALONG_Y, ALONG_X))
    fc1_got = links(after((far_a, far_b), *fc2_give))
    grad_qkv_rows, attention_sums, far_a, far_b = local_call(
        attend_back_kernel,
        [
            ((length, 1536), bf16), ((1, 1536), f32), ((512, 768), bf16), ((512, 768), bf16),
        ],
        pos, after(qkv, *fc2_give), token_gate, grad_attended, normed_one, room=24,
    )
    fc2_half = jnp.concatenate(half_of(fc2_keep, after(fc2_again, grad_qkv_rows, out_got[1])), axis=1)
    fc2_in = [line_in(fc2_half[:256]), line_in(fc2_half[256:])]
    partial, upper, lower = local_call(
        first_back_kernel, [(full, f32), ((half + 16, width), bf16), ((half, width), bf16)],
        pos, after(grad_qkv_rows, fc2_half), qkv_w, last_sums, room=16,
    )
    grad_input, first_sums = local_call(
        inputs_back_kernel, [((half, width), bf16), ((3, width), f32)],
        pos, inputs, partial, swap(upper, CORE), swap(lower, CORE), grad_hidden, vectors,
        scratch=[(full, f32)], room=16,
    )
    in_got = from_images(grad_input)
    small_keep, small_give = local_call(
        small_kernel, [((2, 16, 128), f32), ((16, 1024), bf16)],
        pos, first_sums, second_sums, last_sums, attention_sums, unit_sums, room=6,
    )
    fc1_block = ((320, 1024), bf16)
    keep_a, give_a, keep_b, give_b = local_call(
        fc1_fold_kernel, [fc1_block, fc1_block, fc1_block, ((336, 1024), bf16)],
        pos, normed_two, grad_pre, attended, grad_one, small_give, *fc1_got, room=20,
    )
    fc1_keep, fc1_give = (keep_a, keep_b), (give_a, give_b)
    fc1_again = links(fc1_give, (ALONG_Y, ALONG_X))
    last_got = links(after((far_a, far_b), *fc1_give))
    fc2_top = add_low(fc2_half[:256], after(fc2_in[0], *fc1_give))
    fc2_mid = [line_mid(fc2_top)]
    fc2_low = add_low(fc2_half[256:], after(fc2_in[1], fc2_top, *in_got))
    fc2_mid.append(line_mid(fc2_low))
    fc2_sum = jnp.concatenate([fc2_top, fc2_low], axis=0)

    small_got = fc1_again[1][320:]
    fc1_again = (fc1_again[0], fc1_again[1][:320])
    fc1_half = half_of(fc1_keep, after(fc1_again, fc2_sum))
    fc1_in = [line_in(item) for item in fc1_half]
    fc2_mid = jnp.concatenate(after(fc2_mid, *fc1_half), axis=0)
    fc2_total = add_low(fc2_sum, fc2_mid)
    fc2_out = line_out(fc2_total)
    fc1_sum, fc1_mid, fc1_total, fc1_out = [None] * 2, [None] * 2, [None] * 2, [None] * 2
    fc1_sum[0] = add_low(fc1_half[0], after(fc1_in[0], fc2_total))
    fc1_mid[0] = line_mid(fc1_sum[0])
    last_got = after(last_got, fc1_sum[0])
    wide_block, block = ((288, 768), bf16), ((256, 768), bf16)
    keep_a, give_a, keep_b, give_b = local_call(
        last_fold_kernel, [wide_block, wide_block, block, block],
        pos, normed_one, grad_qkv_rows, *last_got, small_keep, small_got, room=16,
    )
    last_again = links((give_a, give_b), (ALONG_Y, ALONG_X))
    fc1_sum[1] = add_low(fc1_half[1], after(fc1_in[1], give_a, give_b))
    fc1_mid[1] = line_mid(fc1_sum[1])
    last_again, fc2_out = after((last_again, fc2_out), fc1_sum[1])
    last_half = half_of((keep_a, keep_b), last_again)
    last_in = [None, line_in(last_half[1])]
    fc1_total[0] = add_low(fc1_sum[0], after(fc1_mid[0], *last_half))
    fc1_out[0] = line_out(fc1_total[0])

    def line_end(total, out):
        return jnp.where(inner() == 1, total, out)

    def core_give(values):
        return lax.dynamic_slice_in_dim(values, (1 - core) * 128, 128, 0)

    fc1_total[1] = add_low(fc1_sum[1], after(fc1_mid[1], fc1_total[0]))
    fc1_out[1] = line_out(fc1_total[1])
    grad_fc2 = line_end(fc2_total, after(fc2_out, fc1_total[1])).astype(f32)
    last_sum, last_mid, last_total, last_out = [None] * 2, [None] * 2, [None] * 2, [None] * 2
    arrived, fc1_out[0] = after((last_in[1], fc1_out[0]), grad_fc2)
    last_sum[1] = add_low(last_half[1], arrived)
    last_mid[1] = line_mid(last_sum[1])
    last_in[0] = line_in(after(last_half[0], last_sum[1]))
    arrived, fc1_out[1] = after((last_in[0], fc1_out[1]), last_sum[1])
    last_sum[0] = add_low(last_half[0], arrived)
    last_mid[0] = line_mid(last_sum[0])
    last_total[1] = add_low(last_sum[1], after(last_mid[1], last_sum[0]))
    last_out[1] = line_out(last_total[1])
    fc1_rows = [line_end(*pair) for pair in zip(fc1_total, after(fc1_out, last_total[1]))]
    grad_proj = jnp.concatenate(
        [
            jnp.concatenate([item[256:, :512], item[256:, 512:]], axis=0) for item in fc1_rows
        ],
        axis=1,
    ).astype(f32)
    fc1_rows = jnp.concatenate([item[:256] for item in fc1_rows], axis=1)
    last_total[0] = add_low(last_sum[0], after(last_mid[0], fc1_rows))
    last_out[0] = line_out(last_total[0])
    (grad_fc1,) = local_call(
        finish_fc1_kernel, [((128, 4096), f32)],
        pos, fc1_rows, after(swap(core_give(fc1_rows), CORE), last_total[0]), room=10,
    )
    last_out = after(last_out, grad_fc1)
    last_rows = [line_end(*pair) for pair in zip(last_total, last_out)]
    small = last_rows[0][256:272, :128].astype(f32)
    qkv_rows = jnp.concatenate([last_rows[0][:256], last_rows[1]], axis=1)
    qkv_core = swap(core_give(qkv_rows), CORE)
    (grad_qkv,) = local_call(
        finish_qkv_kernel, [((128, 3072), f32)], pos, qkv_rows, qkv_core, room=10
    )
    grad_scales = small[:4]
    grad_shifts = small[4:10]
    grad_bias = small[10:14].reshape(512)
    return (
        slots_of(out_got),
        slots_of(in_got),
        grad_qkv,
        grad_proj,
        grad_fc1,
        grad_fc2,
        grad_bias,
        grad_scales,
        grad_shifts,
    )


def on_device(*arrays):
    tokens = arrays[0]
    whole_images = 2 * tokens.shape[0] == lax.axis_size("seq")
    if lax.axis_size("dp") == 8 and lax.axis_size("seq") == 4 and whole_images:
        return image_plan(*arrays)
    return general_plan(*arrays)


def solution(mesh):
    return jax.shard_map(
        on_device,
        mesh=mesh,
        in_specs=(
            P("dp", "seq", None),
            P("dp"),
            P("dp", None),
            P("dp", None),
            P("dp", None),
            P("dp", None),
            P("dp", None),
            P("dp"),
            P(None, "dp"),
            P(None, "dp"),
            P("dp", "seq", None),
        ),
        out_specs=(
            P("dp", "seq", None),
            P("dp", "seq", None),
            P("dp", None),
            P("dp", None),
            P("dp", None),
            P("dp", None),
            P("dp"),
            P(None, "dp"),
            P(None, "dp"),
        ),
        check_vma=False,
    )
```
